32 devices in a mesh: dp: 8 (over y, x, core), tensor: 4 (over z).
Axes of the slice: x: 2, y: 2, z: 4, core: 2. Of those that a mesh axis runs over, the one named last changes fastest.
Arguments:
- inputs: bfloat16 [32768, 768], P(('dp', 'tensor')), may hold values from -6 to 6
- encoded: bfloat16 [32768, 768], P(('dp', 'tensor')), may hold values from -6 to 6
- cotangent: bfloat16 [32768, 768], P(('dp', 'tensor')), may hold values from -6 to 6
- tgt_seg: int32 [32, 1024], P('dp'), may hold values from 0 to 4, as said below
- src_seg: int32 [32, 1024], P('dp'), may hold values from 0 to 4, as said below
- self_qkv: bfloat16 [3, 768, 768], P(None, None, 'tensor'), may hold values from -0.21875 to 0.21875
- self_out: bfloat16 [768, 768], P('tensor'), may hold values from -1.75 to 1.75
- cross_q: bfloat16 [768, 768], P(None, 'tensor'), may hold values from -0.21875 to 0.21875
- cross_kv: bfloat16 [2, 768, 768], P(None, None, 'tensor'), may hold values from -0.21875 to 0.21875
- cross_out: bfloat16 [768, 768], P('tensor'), may hold values from -1.75 to 1.75
- ffn_up: bfloat16 [768, 3072], P(None, 'tensor'), may hold values from -0.21875 to 0.21875
- ffn_down: bfloat16 [3072, 768], P('tensor'), may hold values from -0.109375 to 0.109375
- gains: float32 [3, 768], replicated, may hold values from 0.5 to 1.5
- shifts: float32 [3, 768], replicated, may hold values from -3 to 3
Outputs:
- layer_out: bfloat16 [32768, 768], P(('dp', 'tensor'))
- grad_inputs: bfloat16 [32768, 768], P(('dp', 'tensor'))
- grad_encoded: bfloat16 [32768, 768], P(('dp', 'tensor'))
- grad_self_qkv: float32 [3, 768, 768], P(None, None, 'tensor')
- grad_self_out: float32 [768, 768], P('tensor')
- grad_cross_q: float32 [768, 768], P(None, 'tensor')
- grad_cross_kv: float32 [2, 768, 768], P(None, None, 'tensor')
- grad_cross_out: float32 [768, 768], P('tensor')
- grad_ffn_up: float32 [768, 3072], P(None, 'tensor')
- grad_ffn_down: float32 [3072, 768], P('tensor')
- grad_gains: float32 [3, 768], replicated
- grad_shifts: float32 [3, 768], replicated
The draws below stay inside these ranges and needn't reach their ends.
Inputs may be any that keep to these rules, and one draw needn't show every extreme that they name: `tgt_seg`: along each row the ids never fall; every id from 0 to 4 occurs in every row, and 4 marks the 1 to 128 padding positions at the row's end. `src_seg`: along each row the ids never fall; every id from 0 to 4 occurs in every row, and 4 marks the 1 to 128 padding positions at the row's end.
All inputs are finite; a program needn't handle non-finite values.
Results may differ from the reference program's by a relative error of at most 0.028.
Values may be sent and summed in bfloat16 or wider, within the bound.
A program may use at most 256 MiB of HBM per device.

```python
import jax
import jax.numpy as jnp
from jax import lax

D = 768
HEADS = 12
HDIM = 64
FF = 3072
LEN = 1024
SRC_LEN = 1024
DOCS = 4
ROWS = 32
TOKENS = 32768
SOURCES = 32768


def segment_ids(key, row_count, length):
    span = length // (DOCS + 1)
    offsets = jax.random.randint(key, (row_count, DOCS - 1), 0, span)
    starts = (jnp.arange(1, DOCS, dtype=jnp.int32) * span)[None, :] + offsets
    padding = length - jax.random.randint(jax.random.fold_in(key, 1), (row_count, 1), 1, length // 8 + 1)
    bounds = jnp.concatenate([starts, padding], axis=1).astype(jnp.int32)
    position = jnp.arange(length, dtype=jnp.int32)
    return jnp.sum((position[None, :, None] >= bounds[:, None, :]).astype(jnp.int32), axis=2).astype(jnp.int32)


def draw_tgt_seg(key, part):
    key = jax.random.fold_in(key, 11)
    return segment_ids(key, ROWS, LEN)


def draw_src_seg(key, part):
    key = jax.random.fold_in(key, 12)
    return segment_ids(key, ROWS, SRC_LEN)


def block_scale(own_key, extent, shards, least, high):
    def one(dim, shards_of):
        draws = jax.random.uniform(jax.random.fold_in(jax.random.fold_in(own_key, 6), dim), (shards_of,), jnp.float32, least / len(shards), high / len(shards))
        return jnp.repeat(jnp.exp(draws), extent[dim] // shards_of).reshape((-1,) + (1,) * (len(extent) - dim - 1))

    factor_of = one(*shards[0])
    for cut in shards[1:]:
        factor_of = factor_of * one(*cut)
    return factor_of


def gaussian(key, shape, scale, reach, pieces=(), held_as=jnp.bfloat16):
    array = jax.random.normal(key, shape, jnp.float32) * scale
    if len(pieces) > 0:
        array = block_scale(key, shape, pieces, -0.22, 0.18) * array
    return jnp.clip(array, min=-reach, max=reach).astype(held_as)


def setup_inputs(seed: int = 0) -> dict:
    seeds = jax.random.split(jax.random.key(seed), 15)
    inputs = gaussian(seeds[0], (TOKENS, D), 1.0, 6.0, ((0, 32),))
    encoded = gaussian(seeds[1], (SOURCES, D), 1.0, 6.0, ((0, 32),))
    cotangent = gaussian(seeds[2], (TOKENS, D), 1.0, 6.0, ((0, 32),))
    tgt_seg = draw_tgt_seg(jax.random.fold_in(seeds[14], 71), 0)
    src_seg = draw_src_seg(jax.random.fold_in(seeds[14], 71), 0)
    self_qkv = gaussian(seeds[5], (3, D, D), D ** -0.5, 0.21875, ((2, 4),))
    self_out = gaussian(seeds[6], (D, D), (D // 64) ** -0.5, 1.75, ((0, 4),))
    cross_q = gaussian(seeds[7], (D, D), D ** -0.5, 0.21875, ((1, 4),))
    cross_kv = gaussian(seeds[8], (2, D, D), D ** -0.5, 0.21875, ((2, 4),))
    cross_out = gaussian(seeds[9], (D, D), (D // 64) ** -0.5, 1.75, ((0, 4),))
    ffn_up = gaussian(seeds[10], (D, FF), D ** -0.5, 0.21875, ((1, 4),))
    ffn_down = gaussian(seeds[11], (FF, D), FF ** -0.5, 0.109375, ((0, 4),))
    gains = jnp.clip(jax.random.uniform(seeds[12], (3, D), jnp.float32, 0.5, 1.5), 0.5, 1.5)
    shifts = gaussian(seeds[13], (3, D), 0.5, 3.0, (), jnp.float32)
    return dict(inputs=inputs, encoded=encoded, cotangent=cotangent, tgt_seg=tgt_seg, src_seg=src_seg, self_qkv=self_qkv, self_out=self_out, cross_q=cross_q, cross_kv=cross_kv, cross_out=cross_out, ffn_up=ffn_up, ffn_down=ffn_down, gains=gains, shifts=shifts)


PRECISE = lax.Precision.HIGHEST
MASKED = -1e+30
EPSILON = 1e-05

@jax.custom_vjp
def low(v):
    return lax.optimization_barrier(v.astype(jnp.bfloat16)).astype(jnp.float32)

@jax.custom_vjp
def low_back(v):
    return v

def low_keep(v):
    return (low(v), None)

def low_pass(kept, grad):
    return (grad,)

def back_keep(v):
    return (v, None)

def back_low(kept, grad):
    return (low(grad),)
low.defvjp(low_keep, low_pass)
low_back.defvjp(back_keep, back_low)

def both_round(values):
    return low(low_back(values))

def layer_norm(summed, gain, shift):
    centred = summed - lax.optimization_barrier(jnp.mean(summed, axis=-1, keepdims=True))
    inverse = lax.rsqrt(lax.optimization_barrier(jnp.mean(centred * centred, axis=-1, keepdims=True)) + EPSILON)
    return centred * inverse * gain + shift

def attend_row(query, key, value, query_ids, key_ids, causal):
    query_count = query.shape[0]
    key_count = key.shape[0]
    scores = jnp.einsum('qhe,khe->hqk', query.reshape(query_count, HEADS, HDIM), key.reshape(key_count, HEADS, HDIM), precision=PRECISE) * HDIM ** (-0.5)
    scores = low_back(scores)
    allowed = query_ids[:, None] == key_ids[None, :]
    if causal:
        allowed = allowed & (jnp.arange(key_count)[None, :] <= jnp.arange(query_count)[:, None])
    scores = jnp.where(allowed[None], scores, MASKED)
    shifted = jnp.exp(scores - lax.optimization_barrier(jnp.max(scores, axis=-1, keepdims=True)))
    probs = low(shifted / lax.optimization_barrier(jnp.sum(shifted, axis=-1, keepdims=True)))
    mixed = jnp.einsum('hqk,khe->qhe', probs, value.reshape(key_count, HEADS, HDIM), precision=PRECISE)
    return mixed.reshape(query_count, D)

def self_attend(item):
    return attend_row(item[0], item[1], item[2], item[3], item[3], True)

def cross_attend(item):
    return attend_row(item[0], item[1], item[2], item[3], item[4], False)

def group_forward(params, target, source, target_ids, source_ids):
    self_qkv, self_out, cross_q, cross_kv, cross_out, ffn_up, ffn_down, gains, shifts = params
    group = target_ids.shape[0]
    projected = both_round(jnp.einsum('td,cde->cte', target, self_qkv, precision=PRECISE))
    projected = projected.reshape(3, group, LEN, D)
    self_mixed = lax.map(jax.checkpoint(self_attend), (projected[0], projected[1], projected[2], target_ids))
    self_mixed = both_round(self_mixed.reshape(group * LEN, D))
    first = layer_norm(target + low_back(jnp.dot(self_mixed, self_out, precision=PRECISE)), gains[0], shifts[0])
    first_low = low(first)
    cross_query = both_round(jnp.dot(first_low, cross_q, precision=PRECISE)).reshape(group, LEN, D)
    pairs = both_round(jnp.einsum('sd,cde->cse', source, cross_kv, precision=PRECISE))
    pairs = pairs.reshape(2, group, SRC_LEN, D)
    cross_mixed = lax.map(jax.checkpoint(cross_attend), (cross_query, pairs[0], pairs[1], target_ids, source_ids))
    cross_mixed = both_round(cross_mixed.reshape(group * LEN, D))
    second = layer_norm(first + low_back(jnp.dot(cross_mixed, cross_out, precision=PRECISE)), gains[1], shifts[1])
    second_low = low(second)
    hidden_pre = low_back(jnp.dot(second_low, ffn_up, precision=PRECISE))
    hidden = low(jax.nn.gelu(hidden_pre, approximate=False))
    branch = low_back(jnp.dot(hidden, ffn_down, precision=PRECISE))
    return layer_norm(second + branch, gains[2], shifts[2])

def reference(inputs, encoded, cotangent, tgt_seg, src_seg, self_qkv, self_out, cross_q, cross_kv, cross_out, ffn_up, ffn_down, gains, shifts):
    params = (self_qkv.astype(jnp.float32), self_out.astype(jnp.float32), cross_q.astype(jnp.float32), cross_kv.astype(jnp.float32), cross_out.astype(jnp.float32), ffn_up.astype(jnp.float32), ffn_down.astype(jnp.float32), gains.astype(jnp.float32), shifts.astype(jnp.float32))
    step_count = ROWS // 4
    items = (inputs.astype(jnp.float32).reshape(step_count, 4 * LEN, D), encoded.astype(jnp.float32).reshape(step_count, 4 * SRC_LEN, D), cotangent.astype(jnp.float32).reshape(step_count, 4 * LEN, D), tgt_seg.reshape(step_count, 4, LEN), src_seg.reshape(step_count, 4, SRC_LEN))

    def one_step(running, item):
        target, source, upstream, target_ids, source_ids = item

        def forward(weights, target_in, source_in):
            return group_forward(weights, target_in, source_in, target_ids, source_ids)
        result, pull = jax.vjp(forward, params, target, source)
        weight_grads, target_grad, source_grad = pull(upstream)
        running = jax.tree.map(jnp.add, running, weight_grads)
        return (running, (result.astype(jnp.bfloat16), target_grad.astype(jnp.bfloat16), source_grad.astype(jnp.bfloat16)))
    start = jax.tree.map(jnp.zeros_like, params)
    totals, (results, target_grads, source_grads) = lax.scan(one_step, start, items)
    return (results.reshape(TOKENS, D), target_grads.reshape(TOKENS, D), source_grads.reshape(SOURCES, D), totals[0], totals[1], totals[2], totals[3], totals[4], totals[5], totals[6], totals[7], totals[8])
```

```python
import functools
import jax, jax.numpy as jnp
from jax import lax
from jax.sharding import PartitionSpec as P
from jax.experimental import pallas as pl
from jax.experimental.pallas import tpu as pltpu

HDIM = 64
LANES = 128
MASKED = -1e30
EPSILON = 1e-5
F32 = jnp.float32
BF16 = jnp.bfloat16
NT = (((1,), (1,)), ((), ()))
TN = (((0,), (0,)), ((), ()))
NN = (((1,), (0,)), ((), ()))


def dot(a, b, dims):
    return lax.dot_general(a, b, dims, preferred_element_type=F32)


def attend_kernel(causal, bq, bk, lo_ref, hi_ref, q_ref, k_ref, v_ref, fq_ref, fk_ref, o_ref, lse_ref):
    n = q_ref.shape[0]
    lane = lax.broadcasted_iota(jnp.int32, (bq, LANES), 1)
    first = lane < HDIM
    ones = jnp.ones((bk, LANES), BF16)
    for i in range(n // bq):
        rows = pl.ds(i * bq, bq)
        q = q_ref[rows, :] * jnp.asarray(HDIM ** -0.5, BF16)
        fq = fq_ref[rows, :]
        zero = jnp.zeros_like(q)
        qs = jnp.concatenate(
            [
                jnp.concatenate([jnp.where(first, q, zero), fq], axis=1),
                jnp.concatenate([jnp.where(first, zero, q), fq], axis=1),
            ],
            axis=0,
        )

        def step(j, carry, diagonal=False):
            top, acc = carry
            keys = pl.ds(pl.multiple_of(j * bk, bk), bk)
            ks = jnp.concatenate([k_ref[keys, :], fk_ref[keys, :]], axis=1)
            s = dot(qs, ks, NT)
            if diagonal:
                row = lax.broadcasted_iota(jnp.int32, (2 * bq, bk), 0)
                row = jnp.where(row >= bq, row - bq, row) + i * bq
                col = lax.broadcasted_iota(jnp.int32, (2 * bq, bk), 1) + j * bk
                s = jnp.where(col <= row, s, MASKED)
            new_top = jnp.maximum(top, jnp.max(s, axis=1, keepdims=True))
            p = jnp.exp(s - new_top).astype(BF16)
            vs = jnp.concatenate([v_ref[keys, :], ones], axis=1)
            acc = acc * jnp.exp(top - new_top) + dot(p, vs, NN)
            return new_top, acc

        carry = (jnp.full((2 * bq, 1), MASKED, F32), jnp.zeros((2 * bq, 2 * LANES), F32))
        if causal:
            diag = [i * bq // bk + d for d in range(max(1, bq // bk))]
            for j in diag:
                carry = step(j, carry, True)
            carry = lax.fori_loop(lo_ref[i], diag[0], step, carry)
        else:
            carry = lax.fori_loop(lo_ref[i], hi_ref[i], step, carry)
        top, acc = carry
        total = acc[:, LANES : LANES + 1]
        out = acc[:, :LANES] / total
        o_ref[rows, :] = jnp.where(first, out[:bq], out[bq:]).astype(BF16)
        lse = top + jnp.log(total)
        lse_ref[rows, :] = jnp.where(lane == 0, lse[:bq], lse[bq:])


def attend_back_kernel(
    causal, bq, bk, lo_ref, hi_ref, q_ref, k_ref, v_ref, fq_ref, fk_ref, g_ref, lse_ref, d_ref, dq_ref, dk_ref, dv_ref, dq_acc
):
    n = q_ref.shape[0]
    m = k_ref.shape[0]
    lane = lax.broadcasted_iota(jnp.int32, (bk, LANES), 1)
    first = lane < HDIM
    dq_acc[...] = jnp.zeros_like(dq_acc)
    scale = jnp.asarray(HDIM ** -0.5, BF16)
    for j in range(m // bk):
        keys = pl.ds(j * bk, bk)
        k = k_ref[keys, :]
        v = v_ref[keys, :]
        fk = fk_ref[keys, :]
        zero = jnp.zeros_like(k)
        kh = jnp.concatenate([jnp.where(first, k, zero), jnp.where(first, zero, k)], axis=0)
        ks = jnp.concatenate([kh, jnp.concatenate([fk, fk], axis=0)], axis=1)
        vs = jnp.concatenate([jnp.where(first, v, zero), jnp.where(first, zero, v)], axis=0)

        def step(i, carry, diagonal=False):
            dk, dv = carry
            rows = pl.ds(pl.multiple_of(i * bq, bq), bq)
            q = q_ref[rows, :] * scale
            qs = jnp.concatenate([q, fq_ref[rows, :]], axis=1)
            g = g_ref[rows, :]
            s = dot(ks, qs, NT)
            if diagonal:
                row = lax.broadcasted_iota(jnp.int32, (2 * bk, bq), 1) + i * bq
                col = lax.broadcasted_iota(jnp.int32, (2 * bk, bq), 0)
                col = jnp.where(col >= bk, col - bk, col) + j * bk
                s = jnp.where(col <= row, s, MASKED)
            lse = lse_ref[0, :, rows]
            delta = d_ref[0, :, rows]
            dp = dot(vs, g, NT)
            p0 = jnp.exp(s[:bk] - lse[0:1, :])
            p1 = jnp.exp(s[bk:] - lse[1:2, :])
            ds0 = (p0 * (dp[:bk] - delta[0:1, :])).astype(BF16)
            ds1 = (p1 * (dp[bk:] - delta[1:2, :])).astype(BF16)
            p = jnp.concatenate([p0.astype(BF16), p1.astype(BF16)], axis=0)
            ds = jnp.concatenate([ds0, ds1], axis=0)
            dv = dv + dot(p, g, NN)
            dk = dk + dot(ds, q, NN)
            dq_acc[rows, :] += dot(ds, kh, TN)
            return dk, dv

        carry = (jnp.zeros((2 * bk, LANES), F32), jnp.zeros((2 * bk, LANES), F32))
        if causal:
            diag = [j * bk // bq + d for d in range(max(1, bk // bq))]
            for i in diag:
                carry = step(i, carry, True)
            carry = lax.fori_loop(diag[-1] + 1, hi_ref[j], step, carry)
        else:
            carry = lax.fori_loop(lo_ref[j], hi_ref[j], step, carry)
        dk, dv = carry
        dk_ref[keys, :] = jnp.where(first, dk[:bk], dk[bk:]).astype(BF16)
        dv_ref[keys, :] = jnp.where(first, dv[:bk], dv[bk:]).astype(BF16)
    dq_ref[...] = (dq_acc[...] * HDIM ** -0.5).astype(BF16)


def block_range(own, other, block, other_block):
    own = own.reshape(-1, block)
    lo = jnp.sum((other[None, :] < own[:, :1]).astype(jnp.int32), axis=1) // other_block
    hi = jnp.sum((other[None, :] <= own[:, -1:]).astype(jnp.int32), axis=1)
    return lo, (hi + other_block - 1) // other_block


def seg_features(q_ids, k_ids):
    lanes = jnp.arange(LANES, dtype=jnp.int32)[None, :]
    fq = jnp.where((lanes < 5) & (q_ids[:, None] != lanes), MASKED, 0.0).astype(BF16)
    fk = (k_ids[:, None] == lanes).astype(BF16)
    return fq, fk


VMEM_LIMIT = 56 * 2**20


def attend(q, k, v, q_ids, k_ids, fq, fk, causal, bq=256, bk=256):
    n, width = q.shape
    m = k.shape[0]
    lo, hi = block_range(q_ids, k_ids, bq, bk)
    pairs = width // LANES
    col = lambda rows: pl.BlockSpec((rows, LANES), lambda i, *_: (0, i))
    whole = lambda rows: pl.BlockSpec((rows, LANES), lambda i, *_: (0, 0))
    out, lse = pl.pallas_call(
        functools.partial(attend_kernel, causal, bq, bk),
        out_shape=(jax.ShapeDtypeStruct((n, width), BF16), jax.ShapeDtypeStruct((n, width), F32)),
        grid_spec=pltpu.PrefetchScalarGridSpec(
            num_scalar_prefetch=2,
            grid=(pairs,),
            in_specs=[col(n), col(m), col(m), whole(n), whole(m)],
            out_specs=[col(n), col(n)],
        ),
        compiler_params=pltpu.CompilerParams(vmem_limit_bytes=VMEM_LIMIT),
        cost_estimate=pl.CostEstimate(flops=int(4e9), bytes_accessed=int(12e6), transcendentals=int(4e6)),
        name="attend",
    )(lo, hi, q, k, v, fq, fk)
    lse = lse.reshape(n, pairs, LANES)[:, :, :2].transpose(1, 2, 0)
    return out, lse


def attend_back(q, k, v, g, lse, delta, q_ids, k_ids, fq, fk, causal, bq=256, bk=256):
    n, width = q.shape
    m = k.shape[0]
    lo, hi = block_range(k_ids, q_ids, bk, bq)
    pairs = width // LANES
    col = lambda rows: pl.BlockSpec((rows, LANES), lambda i, *_: (0, i))
    whole = lambda rows: pl.BlockSpec((rows, LANES), lambda i, *_: (0, 0))
    vec = pl.BlockSpec((1, 2, n), lambda i, *_: (i, 0, 0))
    return pl.pallas_call(
        functools.partial(attend_back_kernel, causal, bq, bk),
        out_shape=(
            jax.ShapeDtypeStruct((n, width), BF16),
            jax.ShapeDtypeStruct((m, width), BF16),
            jax.ShapeDtypeStruct((m, width), BF16),
        ),
        grid_spec=pltpu.PrefetchScalarGridSpec(
            num_scalar_prefetch=2,
            grid=(pairs,),
            in_specs=[col(n), col(m), col(m), whole(n), whole(m), col(n), vec, vec],
            out_specs=[col(n), col(m), col(m)],
            scratch_shapes=[pltpu.VMEM((n, LANES), F32)],
        ),
        compiler_params=pltpu.CompilerParams(vmem_limit_bytes=VMEM_LIMIT),
        cost_estimate=pl.CostEstimate(flops=int(10e9), bytes_accessed=int(12e6), transcendentals=int(4e6)),
        name="attend_back",
    )(lo, hi, q, k, v, fq, fk, g, lse, delta)


def norm_forward(summed, gain, shift):
    centred = summed - jnp.mean(summed, axis=-1, keepdims=True)
    inverse = lax.rsqrt(jnp.mean(centred * centred, axis=-1, keepdims=True) + EPSILON)
    normed = centred * inverse
    return normed * gain + shift, normed, inverse


def norm_backward(upstream, normed, inverse, gain):
    scaled = upstream * gain
    first_mean = jnp.mean(scaled, axis=-1, keepdims=True)
    second_mean = jnp.mean(scaled * normed, axis=-1, keepdims=True)
    result = inverse * (scaled - first_mean - normed * second_mean)
    return result, jnp.sum(upstream * normed, axis=0), jnp.sum(upstream, axis=0)


def head_sums(a, b):
    n, width = a.shape
    prod = (a.astype(F32) * b.astype(F32)).reshape(n, width // HDIM, HDIM)
    return jnp.sum(prod, axis=2).T.reshape(width // LANES, 2, n)


def local_step(x, e, ct, t_ids, s_ids, w, gains, shifts):
    x32 = x.astype(F32)
    q, k, v = [dot(x, w["qkv"][c], NT).astype(BF16) for c in range(3)]
    k2, v2 = [dot(e, w["ckv"][c], NT).astype(BF16) for c in range(2)]
    fq, fk = seg_features(t_ids, t_ids)
    _, fs = seg_features(t_ids, s_ids)
    ctx1, lse1 = attend(q, k, v, t_ids, t_ids, fq, fk, True)
    h1, n1, i1 = norm_forward(x32 + dot(ctx1, w["out"], NN), gains[0], shifts[0])
    h1b = h1.astype(BF16)
    q2 = dot(h1b, w["cq"], NT).astype(BF16)
    ctx2, lse2 = attend(q2, k2, v2, t_ids, s_ids, fq, fs, False)
    h2, n2, i2 = norm_forward(h1 + dot(ctx2, w["cout"], NN), gains[1], shifts[1])
    h2b = h2.astype(BF16)
    blocks = w["up"].shape[0]
    acts, slopes = [], []
    a3 = 0.0
    for b in range(blocks):
        u = dot(h2b, w["up"][b], NT)
        phi = 0.5 * (1.0 + lax.erf(u * (2 ** -0.5)))
        acts.append((u * phi).astype(BF16))
        slopes.append((phi + u * jnp.exp(-0.5 * u * u) * ((2 * jnp.pi) ** -0.5)).astype(BF16))
        a3 = a3 + dot(acts[b], w["down"][b], NN)
    h3, n3, i3 = norm_forward(h2 + a3, gains[2], shifts[2])
    layer_out = h3.astype(BF16)
    dr3, gg3, gs3 = norm_backward(ct.astype(F32), n3, i3, gains[2])
    da3 = dr3.astype(BF16)
    g_up, g_down = [], []
    dh2 = dr3
    for b in range(blocks):
        g_down.append(dot(acts[b], da3, TN).astype(BF16))
        du = (slopes[b].astype(F32) * dot(da3, w["down"][b], NT)).astype(BF16)
        g_up.append(dot(du, h2b, TN).astype(BF16))
        dh2 = dh2 + dot(du, w["up"][b], NN)
    dr2, gg2, gs2 = norm_backward(dh2, n2, i2, gains[1])
    da2 = dr2.astype(BF16)
    g_cout = dot(ctx2, da2, TN).astype(BF16)
    dctx2 = dot(da2, w["cout"], NT).astype(BF16)
    dq2, dk2, dv2 = attend_back(q2, k2, v2, dctx2, lse2, head_sums(dctx2, ctx2), t_ids, s_ids, fq, fs, False)
    g_cq = dot(dq2, h1b, TN).astype(BF16)
    g_ckv = jnp.stack([dot(dk2, e, TN), dot(dv2, e, TN)]).astype(BF16)
    grad_e = (dot(dk2, w["ckv"][0], NN) + dot(dv2, w["ckv"][1], NN)).astype(BF16)
    dh1 = dr2 + dot(dq2, w["cq"], NN)
    dr1, gg1, gs1 = norm_backward(dh1, n1, i1, gains[0])
    da1 = dr1.astype(BF16)
    g_out = dot(ctx1, da1, TN).astype(BF16)
    dctx1 = dot(da1, w["out"], NT).astype(BF16)
    dq, dk, dv = attend_back(q, k, v, dctx1, lse1, head_sums(dctx1, ctx1), t_ids, t_ids, fq, fk, True)
    g_qkv = jnp.stack([dot(dq, x, TN), dot(dk, x, TN), dot(dv, x, TN)]).astype(BF16)
    grad_x = (dr1 + dot(dq, w["qkv"][0], NN) + dot(dk, w["qkv"][1], NN) + dot(dv, w["qkv"][2], NN)).astype(BF16)
    grads = dict(qkv=g_qkv, out=g_out, cq=g_cq, ckv=g_ckv, cout=g_cout, up=jnp.stack(g_up), down=jnp.stack(g_down))
    return layer_out, grad_x, grad_e, grads, jnp.stack([gg1, gg2, gg3]), jnp.stack([gs1, gs2, gs3])


def gather_rows(shard):
    mats, rows, width = shard.shape
    dp, tensor = lax.axis_size("dp"), lax.axis_size("tensor")
    piece = mats * rows // dp
    mine = lax.dynamic_slice_in_dim(
        shard.reshape(mats * rows, width), lax.axis_index("dp") * piece, piece, 0
    )
    full = lax.all_gather(mine, ("dp", "tensor"), axis=0, tiled=True)
    full = full.reshape(mats, dp // mats, tensor, piece, width).transpose(0, 2, 1, 3, 4)
    return full.reshape(mats, tensor * rows, width)


def reduce_rows(grad):
    mats, all_rows, width = grad.shape
    dp, tensor = lax.axis_size("dp"), lax.axis_size("tensor")
    rows = all_rows // tensor
    piece = mats * rows // dp
    grad = grad.reshape(mats, tensor, dp // mats, piece, width).transpose(0, 2, 1, 3, 4)
    mine = lax.psum_scatter(
        grad.reshape(dp * tensor * piece, width), ("dp", "tensor"), scatter_dimension=0, tiled=True
    )
    return lax.all_gather(mine, "dp", axis=0, tiled=True).reshape(mats, rows, width)


def per_device(
    inputs, encoded, cotangent, tgt_seg, src_seg, self_qkv, self_out, cross_q, cross_kv, cross_out, ffn_up, ffn_down, gains, shifts
):
    me = lax.axis_index("tensor")
    t_ids = lax.dynamic_index_in_dim(tgt_seg, me, 0, keepdims=False)
    s_ids = lax.dynamic_index_in_dim(src_seg, me, 0, keepdims=False)
    pack = jnp.concatenate(
        [
            self_qkv.transpose(0, 2, 1),
            self_out[None],
            cross_q.T[None],
            cross_kv.transpose(0, 2, 1),
            cross_out[None],
        ],
        axis=0,
    )
    pack = gather_rows(pack)
    hidden = ffn_down.shape[0]
    dp, tensor = lax.axis_size("dp"), lax.axis_size("tensor")
    ffn = jnp.stack([ffn_up.T, ffn_down], axis=0)
    piece = hidden // dp
    mine = lax.dynamic_slice_in_dim(ffn, lax.axis_index("dp") * piece, piece, 1)
    ffn = lax.all_gather(mine, ("dp", "tensor"), axis=1, tiled=True)
    w = dict(
        qkv=pack[0:3], out=pack[3], cq=pack[4], ckv=pack[5:7], cout=pack[7],
        up=ffn[0].reshape(tensor, hidden, -1), down=ffn[1].reshape(tensor, hidden, -1),
    )
    layer_out, grad_x, grad_e, grads, grad_gains, grad_shifts = local_step(
        inputs, encoded, cotangent, t_ids, s_ids, w, gains, shifts
    )
    width = inputs.shape[1]
    g_ffn = jnp.stack([grads["up"].reshape(-1, width), grads["down"].reshape(-1, width)])
    g_ffn = lax.psum_scatter(g_ffn, ("dp", "tensor"), scatter_dimension=1, tiled=True)
    g_ffn = lax.all_gather(g_ffn, "dp", axis=1, tiled=True)
    g_pack = jnp.concatenate(
        [grads["qkv"], grads["out"][None], grads["cq"][None], grads["ckv"], grads["cout"][None]], axis=0
    )
    g_pack = reduce_rows(g_pack)
    g32 = g_pack.astype(F32)
    grad_gains, grad_shifts = lax.psum((grad_gains, grad_shifts), ("dp", "tensor"))
    return (
        layer_out,
        grad_x,
        grad_e,
        g32[0:3].transpose(0, 2, 1),
        g32[3],
        g32[4].T,
        g32[5:7].transpose(0, 2, 1),
        g32[7],
        g_ffn[0].astype(F32).T,
        g_ffn[1].astype(F32),
        grad_gains,
        grad_shifts,
    )


def solution(mesh):
    rows = P(("dp", "tensor"), None)
    in_specs = (
        rows, rows, rows, P("dp", None), P("dp", None),
        P(None, None, "tensor"), P("tensor", None), P(None, "tensor"), P(None, None, "tensor"), P("tensor", None),
        P(None, "tensor"), P("tensor", None), P(), P(),
    )
    out_specs = (
        rows, rows, rows,
        P(None, None, "tensor"), P("tensor", None), P(None, "tensor"), P(None, None, "tensor"), P("tensor", None),
        P(None, "tensor"), P("tensor", None), P(), P(),
    )
    return jax.shard_map(per_device, mesh=mesh, in_specs=in_specs, out_specs=out_specs, check_vma=False)
```

```python
import functools
import jax, jax.numpy as jnp
from jax import lax
from jax.sharding import PartitionSpec as P
from jax.experimental import pallas as pl
from jax.experimental.pallas import tpu as pltpu

HDIM = 64
LANES = 128
MASKED = -1e30
EPSILON = 1e-5
F32 = jnp.float32
BF16 = jnp.bfloat16
NT = (((1,), (1,)), ((), ()))
TN = (((0,), (0,)), ((), ()))
NN = (((1,), (0,)), ((), ()))


def dot(a, b, dims):
    return lax.dot_general(a, b, dims, preferred_element_type=F32)


def attend_kernel(causal, bq, bk, per, lo_ref, hi_ref, q_ref, k_ref, v_ref, fq_ref, fk_ref, o_ref, lse_ref):
    n = q_ref.shape[0]
    first = lax.broadcasted_iota(jnp.int32, (bk, LANES), 1) < HDIM
    for i in range(n // bq):
        rows = pl.ds(i * bq, bq)
        fq = fq_ref[rows, :]
        qs = [
            jnp.concatenate([q_ref[rows, h * LANES : (h + 1) * LANES] * jnp.asarray(HDIM ** -0.5, BF16), fq], axis=1)
            for h in range(per)
        ]

        def step(j, carry, diagonal=False):
            keys = pl.ds(pl.multiple_of(j * bk, bk), bk)
            fk = fk_ref[keys, :]
            if diagonal:
                row = lax.broadcasted_iota(jnp.int32, (bk, bq), 1) + i * bq
                col = lax.broadcasted_iota(jnp.int32, (bk, bq), 0) + j * bk
                allowed = col <= row
            out = []
            for h in range(per):
                k = k_ref[keys, h * LANES : (h + 1) * LANES]
                v = v_ref[keys, h * LANES : (h + 1) * LANES]
                zero = jnp.zeros_like(k)
                halves = (jnp.where(first, k, zero), jnp.where(first, zero, k))
                for side in range(2):
                    top, total, acc = carry[2 * h + side]
                    s = dot(jnp.concatenate([halves[side], fk], axis=1), qs[h], NT)
                    if diagonal:
                        s = jnp.where(allowed, s, MASKED)
                    new_top = jnp.maximum(top, jnp.max(s, axis=0, keepdims=True))
                    p = jnp.exp(s - new_top)
                    alpha = jnp.exp(top - new_top)
                    total = total * alpha + jnp.sum(p, axis=0, keepdims=True)
                    acc = acc * alpha + dot(v[:, side * HDIM : (side + 1) * HDIM], p.astype(BF16), TN)
                    out.append((new_top, total, acc))
            return tuple(out)

        carry = tuple(
            (jnp.full((1, bq), MASKED, F32), jnp.zeros((1, bq), F32), jnp.zeros((HDIM, bq), F32))
            for _ in range(2 * per)
        )
        if causal:
            carry = step(i * bq // bk, carry, True)
            carry = lax.fori_loop(lo_ref[i], i * bq // bk, step, carry)
        else:
            carry = lax.fori_loop(lo_ref[i], hi_ref[i], step, carry)
        for h in range(per):
            both = jnp.concatenate([acc / total for _, total, acc in carry[2 * h : 2 * h + 2]], axis=0)
            o_ref[rows, h * LANES : (h + 1) * LANES] = both.T.astype(BF16)
            for side in range(2):
                top, total, _ = carry[2 * h + side]
                lse_ref[0, 2 * h + side : 2 * h + side + 1, rows] = top + jnp.log(total)


def attend_back_kernel(
    causal, bq, bk, per, lo_ref, hi_ref, q_ref, k_ref, v_ref, fq_ref, fk_ref, g_ref, o_ref, lse_ref, dq_ref, dk_ref, dv_ref, dq_acc, delta
):
    n = q_ref.shape[0]
    m = k_ref.shape[0]
    first = lax.broadcasted_iota(jnp.int32, (bk, LANES), 1) < HDIM
    pick = lax.broadcasted_iota(jnp.int32, (8, LANES), 1) // HDIM == lax.broadcasted_iota(jnp.int32, (8, LANES), 0)
    pick = pick.astype(BF16)
    dq_acc[...] = jnp.zeros_like(dq_acc)
    scale = jnp.asarray(HDIM ** -0.5, BF16)
    for h in range(per):
        lanes = slice(h * LANES, (h + 1) * LANES)
        prod = g_ref[:, lanes].astype(F32) * o_ref[:, lanes].astype(F32)
        high = prod.astype(BF16)
        rest = (prod - high.astype(F32)).astype(BF16)
        delta[h] = dot(pick, high, NT) + dot(pick, rest, NT)
    for j in range(m // bk):
        keys = pl.ds(j * bk, bk)
        fk = fk_ref[keys, :]
        fk = jnp.concatenate([fk, fk], axis=0)
        kh, ks, vs = [], [], []
        for h in range(per):
            k = k_ref[keys, h * LANES : (h + 1) * LANES]
            v = v_ref[keys, h * LANES : (h + 1) * LANES]
            zero = jnp.zeros_like(k)
            kh.append(jnp.concatenate([jnp.where(first, k, zero), jnp.where(first, zero, k)], axis=0))
            ks.append(jnp.concatenate([kh[h], fk], axis=1))
            vs.append(jnp.concatenate([jnp.where(first, v, zero), jnp.where(first, zero, v)], axis=0))

        def step(i, carry, diagonal=False):
            rows = pl.ds(pl.multiple_of(i * bq, bq), bq)
            fq = fq_ref[rows, :]
            if diagonal:
                row = lax.broadcasted_iota(jnp.int32, (bk, bq), 1) + i * bq
                col = lax.broadcasted_iota(jnp.int32, (bk, bq), 0) + j * bk
                allowed = col <= row
            out = []
            for h in range(per):
                lanes = slice(h * LANES, (h + 1) * LANES)
                dk, dv = carry[h]
                q = q_ref[rows, lanes] * scale
                g = g_ref[rows, lanes]
                s = dot(ks[h], jnp.concatenate([q, fq], axis=1), NT)
                dp = dot(vs[h], g, NT)
                ps, dss = [], []
                for side in range(2):
                    part = s[side * bk : (side + 1) * bk]
                    if diagonal:
                        part = jnp.where(allowed, part, MASKED)
                    p = jnp.exp(part - lse_ref[0, 2 * h + side : 2 * h + side + 1, rows])
                    ds = p * (dp[side * bk : (side + 1) * bk] - delta[h, side : side + 1, rows])
                    ps.append(p.astype(BF16))
                    dss.append(ds.astype(BF16))
                ds = jnp.concatenate(dss, axis=0)
                dv = dv + dot(jnp.concatenate(ps, axis=0), g, NN)
                dk = dk + dot(ds, q, NN)
                dq_acc[rows, lanes] += dot(ds, kh[h], TN)
                out.append((dk, dv))
            return tuple(out)

        carry = tuple((jnp.zeros((2 * bk, LANES), F32), jnp.zeros((2 * bk, LANES), F32)) for _ in range(per))
        if causal:
            carry = step(j * bk // bq, carry, True)
            carry = lax.fori_loop(j * bk // bq + 1, hi_ref[j], step, carry)
        else:
            carry = lax.fori_loop(lo_ref[j], hi_ref[j], step, carry)
        for h in range(per):
            dk, dv = carry[h]
            dk_ref[keys, h * LANES : (h + 1) * LANES] = jnp.where(first, dk[:bk], dk[bk:]).astype(BF16)
            dv_ref[keys, h * LANES : (h + 1) * LANES] = jnp.where(first, dv[:bk], dv[bk:]).astype(BF16)
    dq_ref[...] = (dq_acc[...] * HDIM ** -0.5).astype(BF16)


def block_range(own, other, block, other_block):
    own = own.reshape(-1, block)
    lo = jnp.sum((other[None, :] < own[:, :1]).astype(jnp.int32), axis=1) // other_block
    hi = jnp.sum((other[None, :] <= own[:, -1:]).astype(jnp.int32), axis=1)
    return lo, (hi + other_block - 1) // other_block


def seg_features(q_ids, k_ids):
    lanes = jnp.arange(LANES, dtype=jnp.int32)[None, :]
    fq = jnp.where((lanes < 5) & (q_ids[:, None] != lanes), MASKED, 0.0).astype(BF16)
    fk = (k_ids[:, None] == lanes).astype(BF16)
    return fq, fk


VMEM_LIMIT = 56 * 2**20
FWD_PER = 2
BWD_PER = 1


def attend(q, k, v, q_ids, k_ids, fq, fk, causal, bq=256, bk=256, per=FWD_PER):
    n, width = q.shape
    m = k.shape[0]
    lo, hi = block_range(q_ids, k_ids, bq, bk)
    wide = per * LANES
    col = lambda rows: pl.BlockSpec((rows, wide), lambda i, *_: (0, i))
    whole = lambda rows: pl.BlockSpec((rows, LANES), lambda i, *_: (0, 0))
    vec = pl.BlockSpec((1, 2 * per, n), lambda i, *_: (i, 0, 0))
    return pl.pallas_call(
        functools.partial(attend_kernel, causal, bq, bk, per),
        out_shape=(
            jax.ShapeDtypeStruct((n, width), BF16),
            jax.ShapeDtypeStruct((width // wide, 2 * per, n), F32),
        ),
        grid_spec=pltpu.PrefetchScalarGridSpec(
            num_scalar_prefetch=2,
            grid=(width // wide,),
            in_specs=[col(n), col(m), col(m), whole(n), whole(m)],
            out_specs=[col(n), vec],
        ),
        compiler_params=pltpu.CompilerParams(vmem_limit_bytes=VMEM_LIMIT),
        cost_estimate=pl.CostEstimate(flops=int(8e9), bytes_accessed=int(8e6), transcendentals=int(4e6)),
        name="attend",
    )(lo, hi, q, k, v, fq, fk)


def attend_back(q, k, v, g, out, lse, q_ids, k_ids, fq, fk, causal, bq=256, bk=256, per=BWD_PER):
    n, width = q.shape
    m = k.shape[0]
    lo, hi = block_range(k_ids, q_ids, bk, bq)
    wide = per * LANES
    lse = lse.reshape(width // wide, 2 * per, n)
    col = lambda rows: pl.BlockSpec((rows, wide), lambda i, *_: (0, i))
    whole = lambda rows: pl.BlockSpec((rows, LANES), lambda i, *_: (0, 0))
    vec = pl.BlockSpec((1, 2 * per, n), lambda i, *_: (i, 0, 0))
    return pl.pallas_call(
        functools.partial(attend_back_kernel, causal, bq, bk, per),
        out_shape=(
            jax.ShapeDtypeStruct((n, width), BF16),
            jax.ShapeDtypeStruct((m, width), BF16),
            jax.ShapeDtypeStruct((m, width), BF16),
        ),
        grid_spec=pltpu.PrefetchScalarGridSpec(
            num_scalar_prefetch=2,
            grid=(width // wide,),
            in_specs=[col(n), col(m), col(m), whole(n), whole(m), col(n), col(n), vec],
            out_specs=[col(n), col(m), col(m)],
            scratch_shapes=[pltpu.VMEM((n, wide), F32), pltpu.VMEM((per, 8, n), F32)],
        ),
        compiler_params=pltpu.CompilerParams(vmem_limit_bytes=VMEM_LIMIT),
        cost_estimate=pl.CostEstimate(flops=int(20e9), bytes_accessed=int(12e6), transcendentals=int(4e6)),
        name="attend_back",
    )(lo, hi, q, k, v, fq, fk, g, out, lse)


def norm_forward(summed, gain, shift):
    centred = summed - jnp.mean(summed, axis=-1, keepdims=True)
    inverse = lax.rsqrt(jnp.mean(centred * centred, axis=-1, keepdims=True) + EPSILON)
    normed = centred * inverse
    return normed * gain + shift, normed, inverse


def norm_backward(upstream, normed, inverse, gain):
    scaled = upstream * gain
    first_mean = jnp.mean(scaled, axis=-1, keepdims=True)
    second_mean = jnp.mean(scaled * normed, axis=-1, keepdims=True)
    result = inverse * (scaled - first_mean - normed * second_mean)
    return result, jnp.sum(upstream * normed, axis=0), jnp.sum(upstream, axis=0)


def local_step(x, e, ct, t_ids, s_ids, w, gains, shifts):
    x32 = x.astype(F32)
    q, k, v = [dot(x, w["qkv"][c], NT).astype(BF16) for c in range(3)]
    k2, v2 = [dot(e, w["ckv"][c], NT).astype(BF16) for c in range(2)]
    fq, fk = seg_features(t_ids, t_ids)
    _, fs = seg_features(t_ids, s_ids)
    ctx1, lse1 = attend(q, k, v, t_ids, t_ids, fq, fk, True)
    h1, n1, i1 = norm_forward(x32 + dot(ctx1, w["out"], NN), gains[0], shifts[0])
    h1b = h1.astype(BF16)
    q2 = dot(h1b, w["cq"], NT).astype(BF16)
    ctx2, lse2 = attend(q2, k2, v2, t_ids, s_ids, fq, fs, False)
    h2, n2, i2 = norm_forward(h1 + dot(ctx2, w["cout"], NN), gains[1], shifts[1])
    h2b = h2.astype(BF16)
    blocks = w["up"].shape[0]
    acts, slopes = [], []
    a3 = 0.0
    for b in range(blocks):
        u = dot(h2b, w["up"][b], NT)
        phi = 0.5 * (1.0 + lax.erf(u * (2 ** -0.5)))
        acts.append((u * phi).astype(BF16))
        slopes.append((phi + u * jnp.exp(-0.5 * u * u) * ((2 * jnp.pi) ** -0.5)).astype(BF16))
        a3 = a3 + dot(acts[b], w["down"][b], NN)
    h3, n3, i3 = norm_forward(h2 + a3, gains[2], shifts[2])
    layer_out = h3.astype(BF16)
    dr3, gg3, gs3 = norm_backward(ct.astype(F32), n3, i3, gains[2])
    da3 = dr3.astype(BF16)
    g_up, g_down = [], []
    dh2 = dr3
    for b in range(blocks):
        g_down.append(dot(acts[b], da3, TN).astype(BF16))
        du = (slopes[b].astype(F32) * dot(da3, w["down"][b], NT)).astype(BF16)
        g_up.append(dot(du, h2b, TN).astype(BF16))
        dh2 = dh2 + dot(du, w["up"][b], NN)
    dr2, gg2, gs2 = norm_backward(dh2, n2, i2, gains[1])
    da2 = dr2.astype(BF16)
    g_cout = dot(ctx2, da2, TN).astype(BF16)
    dctx2 = dot(da2, w["cout"], NT).astype(BF16)
    dq2, dk2, dv2 = attend_back(q2, k2, v2, dctx2, ctx2, lse2, t_ids, s_ids, fq, fs, False)
    g_cq = dot(dq2, h1b, TN).astype(BF16)
    g_ckv = [dot(dk2, e, TN).astype(BF16), dot(dv2, e, TN).astype(BF16)]
    grad_e = (dot(dk2, w["ckv"][0], NN) + dot(dv2, w["ckv"][1], NN)).astype(BF16)
    dh1 = dr2 + dot(dq2, w["cq"], NN)
    dr1, gg1, gs1 = norm_backward(dh1, n1, i1, gains[0])
    da1 = dr1.astype(BF16)
    g_out = dot(ctx1, da1, TN).astype(BF16)
    dctx1 = dot(da1, w["out"], NT).astype(BF16)
    dq, dk, dv = attend_back(q, k, v, dctx1, ctx1, lse1, t_ids, t_ids, fq, fk, True)
    g_qkv = [dot(d, x, TN).astype(BF16) for d in (dq, dk, dv)]
    grad_x = (dr1 + dot(dq, w["qkv"][0], NN) + dot(dk, w["qkv"][1], NN) + dot(dv, w["qkv"][2], NN)).astype(BF16)
    grads = dict(qkv=g_qkv, out=g_out, cq=g_cq, ckv=g_ckv, cout=g_cout, up=jnp.stack(g_up), down=jnp.stack(g_down))
    return layer_out, grad_x, grad_e, grads, jnp.stack([gg1, gg2, gg3]), jnp.stack([gs1, gs2, gs3])

MESH = pl.DeviceIdType.MESH

def greet(devices):
    barrier = pltpu.get_barrier_semaphore()
    for device in devices:
        pl.semaphore_signal(barrier, inc=1, device_id=device, device_id_type=MESH)
    pl.semaphore_wait(barrier, len(devices))


def gather_kernel(groups, chunks, window, pack_ref, out_ref, local_sem, send_sem, recv_sem):
    p, t = lax.axis_index("dp"), lax.axis_index("tensor")
    rows = pack_ref.shape[1]
    n = rows // chunks
    zs = [jnp.bitwise_xor(t, j) for j in (1, 2, 3)]
    to_c, to_x, to_y = [(jnp.bitwise_xor(p, b), t) for b in (1, 2, 4)]
    far = jnp.bitwise_xor(p, 6)
    greet([to_c, to_x, to_y] + [(p, z) for z in zs])
    keep = pltpu.make_async_copy(pack_ref, out_ref.at[:, t], local_sem)
    keep.start()
    count = [0]
    copies = []

    def send(src, dst, device):
        i = count[0]
        count[0] += 1
        copy = pltpu.make_async_remote_copy(
            src, dst, send_sem.at[i], recv_sem.at[i], device_id=device, device_id_type=MESH
        )
        copy.start()
        copies.append(copy)
        return copy

    cut = lambda c: pl.ds(c * n, n)
    steps = [(g, c) for g in range(groups) for c in range(chunks)]
    z_in, x_in, y_in, xd_in, yd_in = {}, {}, {}, {}, {}
    last = []

    def start_z(i):
        g, c = steps[i]
        a = g * 8 + p
        for j in range(3):
            z_in[i, j] = send(pack_ref.at[a, cut(c)], out_ref.at[a, t, cut(c)], (p, zs[j]))

    def stage_z(i):
        g, c = steps[i]
        for j in range(3):
            z_in[i, j].wait_recv()
            ref = out_ref.at[g * 8 + p, zs[j], cut(c)]
            x_in[i, j] = send(ref, ref, to_x)
            y_in[i, j] = send(ref, ref, to_y)
            last.append(send(ref, ref, to_c))
        if i + window < len(steps):
            start_z(i + window)

    def stage_xy(i):
        g, c = steps[i]
        for j in range(3):
            x_in[i, j].wait_recv()
            ref = out_ref.at[g * 8 + to_x[0], zs[j]]
            part = ref.at[pl.ds(c * n, n // 2)]
            yd_in[i, j] = send(part, part, to_y)
            part = ref.at[cut(c)]
            last.append(send(part, part, to_c))
            y_in[i, j].wait_recv()
            ref = out_ref.at[g * 8 + to_y[0], zs[j]]
            part = ref.at[pl.ds(c * n + n // 2, n // 2)]
            xd_in[i, j] = send(part, part, to_x)
            part = ref.at[cut(c)]
            last.append(send(part, part, to_c))

    def stage_far(i):
        g, c = steps[i]
        for j in range(3):
            xd_in[i, j].wait_recv()
            yd_in[i, j].wait_recv()
            ref = out_ref.at[g * 8 + far, zs[j], cut(c)]
            last.append(send(ref, ref, to_c))

    for i in range(window):
        start_z(i)
    stages = (stage_z, stage_xy, stage_far)
    for step in range(len(steps) + 2):
        for k in (2, 1, 0):
            if 0 <= step - k < len(steps):
                stages[k](step - k)
    for copy in last:
        copy.wait_recv()
    for copy in copies:
        copy.wait_send()
    keep.wait()


def gather_pack(pack, collective_id, chunks=3, window=1):
    mats, rows, width = pack.shape
    groups = mats // 8
    count = groups * chunks * (3 + 9 + 3 * 2 + 3 * 2 + 3)
    return pl.pallas_call(
        functools.partial(gather_kernel, groups, chunks, window),
        out_shape=jax.ShapeDtypeStruct((mats, 4, rows, width), pack.dtype),
        in_specs=[pl.BlockSpec(memory_space=pltpu.VMEM)],
        out_specs=pl.BlockSpec(memory_space=pl.ANY),
        scratch_shapes=[
            pltpu.SemaphoreType.DMA,
            pltpu.SemaphoreType.DMA((count,)),
            pltpu.SemaphoreType.DMA((count,)),
        ],
        compiler_params=pltpu.CompilerParams(collective_id=collective_id, has_side_effects=True, vmem_limit_bytes=32 * 2**20),
        name="gather_pack",
    )(pack)


def reduce_kernel(chunks, mats, *refs):
    grads, small_ref = refs[:mats], refs[mats]
    (out_ref, small_out_ref, mine, from_c, from_x1, from_y1, from_x2, from_y2, from_z, piece,
     s_send, s_c, s_x, s_y, s_z, local_sem, send_sem, recv_sem, small_send, small_recv) = refs[mats + 1 :]
    p, t = lax.axis_index("dp"), lax.axis_index("tensor")
    half = grads[0].shape[1] // 2
    n = half // chunks
    per = mats // 4
    core, cx, cy = lax.rem(p, 2), lax.rem(p // 2, 2), p // 4
    chip = p // 2
    zs = [jnp.bitwise_xor(t, j) for j in (1, 2, 3)]
    to_c, to_x, to_y = [(jnp.bitwise_xor(p, b), t) for b in (1, 2, 4)]
    greet([to_c, to_x, to_y] + [(p, z) for z in zs])
    count = [0]
    copies = []

    def send(src, dst, device):
        i = count[0]
        count[0] += 1
        copy = pltpu.make_async_remote_copy(
            src, dst, send_sem.at[i], recv_sem.at[i], device_id=device, device_id_type=MESH
        )
        copy.start()
        copies.append(copy)
        return copy

    small_count = [0]

    def send_small(src, dst, device):
        i = small_count[0]
        small_count[0] += 1
        copy = pltpu.make_async_remote_copy(
            src, dst, small_send.at[i], small_recv.at[i], device_id=device, device_id_type=MESH
        )
        copy.start()
        return copy

    nx, ny = 1 - cx, 1 - cy
    c_in, x1, y1, x2, y2, z_in, gx, gy, gxd, gyd, last = {}, {}, {}, {}, {}, {}, {}, {}, {}, {}, []
    local = {}
    cut = lambda c: pl.ds(c * n, n)
    own_cut = lambda c: pl.ds(pl.multiple_of(core * half + c * n, 16), n)
    other_cut = lambda c: pl.ds(pl.multiple_of((1 - core) * half + c * n, 16), n)
    owned = lambda q: pl.ds(q * per, per)
    for c in range(chunks):
        c_in[c], local[c] = [], []
        for a in range(mats):
            c_in[c].append(send(grads[a].at[:, other_cut(c)], from_c.at[a, :, cut(c)], to_c))
            copy = pltpu.make_async_copy(
                grads[a].at[:, own_cut(c)], mine.at[a, :, cut(c)], local_sem.at[c * mats + a]
            )
            copy.start()
            local[c].append(copy)
    small = send_small(small_ref, s_c, to_c)

    def add(dst, src):
        dst[...] = (dst[...].astype(F32) + src[...].astype(F32)).astype(dst.dtype)

    def stage_c(c):
        for a in range(mats):
            c_in[c][a].wait_recv()
            local[c][a].wait()
            for b in range(4):
                add(mine.at[a, b, cut(c)], from_c.at[a, b, cut(c)])
        x1[c] = [send(mine.at[owned(q * 2 + nx), 0:2, cut(c)], from_x1.at[q, :, :, cut(c)], to_x) for q in range(2)]
        y1[c] = [send(mine.at[owned(ny * 2 + q), 2:4, cut(c)], from_y1.at[q, :, :, cut(c)], to_y) for q in range(2)]

    def stage_xy(c):
        for q in range(2):
            x1[c][q].wait_recv()
            for i in range(per):
                for b in range(2):
                    add(mine.at[(q * 2 + cx) * per + i, b, cut(c)], from_x1.at[q, i, b, cut(c)])
        x2[c] = send(mine.at[owned(ny * 2 + cx), 0:2, cut(c)], from_x2.at[:, :, cut(c)], to_y)
        for q in range(2):
            y1[c][q].wait_recv()
            for i in range(per):
                for b in range(2):
                    add(mine.at[(cy * 2 + q) * per + i, 2 + b, cut(c)], from_y1.at[q, i, b, cut(c)])
        y2[c] = send(mine.at[owned(cy * 2 + nx), 2:4, cut(c)], from_y2.at[:, :, cut(c)], to_x)

    def stage_z(c):
        x2[c].wait_recv()
        for i in range(per):
            for b in range(2):
                add(mine.at[chip * per + i, b, cut(c)], from_x2.at[i, b, cut(c)])
        y2[c].wait_recv()
        for i in range(per):
            for b in range(2):
                add(mine.at[chip * per + i, 2 + b, cut(c)], from_y2.at[i, b, cut(c)])
        z_in[c] = [
            send(mine.at[owned(chip), zs[j], cut(c)], from_z.at[j, :, cut(c)], (p, zs[j])) for j in range(3)
        ]

    def stage_out(c):
        for j in range(3):
            z_in[c][j].wait_recv()
        for i in range(per):
            total = mine[chip * per + i, t, cut(c), :].astype(F32)
            for j in range(3):
                total = total + from_z[j, i, cut(c), :].astype(F32)
            piece[chip * per + i, own_cut(c), :] = total.astype(piece.dtype)
        ref = piece.at[owned(chip), own_cut(c)]
        gx[c] = send(ref, ref, to_x)
        gy[c] = send(ref, ref, to_y)
        last.append(send(ref, ref, to_c))

    def stage_far(c):
        gx[c].wait_recv()
        ref = piece.at[owned(cy * 2 + nx), own_cut(c)]
        gyd[c] = send(ref.at[: per // 2], ref.at[: per // 2], to_y)
        last.append(send(ref, ref, to_c))
        gy[c].wait_recv()
        ref = piece.at[owned(ny * 2 + cx), own_cut(c)]
        gxd[c] = send(ref.at[per // 2 :], ref.at[per // 2 :], to_x)
        last.append(send(ref, ref, to_c))

    def stage_end(c):
        gxd[c].wait_recv()
        gyd[c].wait_recv()
        ref = piece.at[owned(ny * 2 + nx), own_cut(c)]
        last.append(send(ref, ref, to_c))

    stages = (stage_c, stage_xy, stage_z, stage_out, stage_far, stage_end)
    for step in range(chunks + len(stages) - 1):
        for k in reversed(range(len(stages))):
            if 0 <= step - k < chunks:
                stages[k](step - k)
        if step == 0:
            small.wait()
            s_send[0] = small_ref[...] + s_c[...]
            small = send_small(s_send.at[0], s_x, to_x)
        elif step == 1:
            small.wait()
            s_send[1] = s_send[0] + s_x[...]
            small = send_small(s_send.at[1], s_y, to_y)
        elif step == 2:
            small.wait()
            s_send[2] = s_send[1] + s_y[...]
            s_z[t] = s_send[2]
            small = [send_small(s_send.at[2], s_z.at[t], (p, z)) for z in zs]
    for copy in small:
        copy.wait()
    small_out_ref[...] = (s_z[0] + s_z[1]) + (s_z[2] + s_z[3])
    for copy in last:
        copy.wait_recv()
    for copy in copies:
        copy.wait_send()
    for a in range(mats):
        out_ref[a] = piece[a].astype(out_ref.dtype)


def reduce_pack(grads, small, collective_id, chunks=3):
    mats = len(grads)
    tensor, rows, width = grads[0].shape
    half, per = rows // 2, mats // 4
    count = chunks * (mats + 4 + 2 + 3 + 3 + 4 + 1)
    vmem = pl.BlockSpec(memory_space=pltpu.VMEM)
    buf = lambda *s: pltpu.VMEM(s + (half, width), BF16)
    sb = lambda *s: pltpu.VMEM(s + small.shape, F32)
    return pl.pallas_call(
        functools.partial(reduce_kernel, chunks, mats),
        out_shape=(jax.ShapeDtypeStruct((mats, rows, width), F32), jax.ShapeDtypeStruct(small.shape, F32)),
        in_specs=[pl.BlockSpec(memory_space=pl.ANY)] * mats + [vmem],
        out_specs=(vmem, vmem),
        scratch_shapes=[
            buf(mats, 4), buf(mats, 4), buf(2, per, 2), buf(2, per, 2), buf(per, 2), buf(per, 2), buf(3, per),
            pltpu.VMEM((mats, rows, width), BF16),
            sb(3), sb(), sb(), sb(), sb(4),
            pltpu.SemaphoreType.DMA((chunks * mats,)),
            pltpu.SemaphoreType.DMA((count,)),
            pltpu.SemaphoreType.DMA((count,)),
            pltpu.SemaphoreType.DMA((6,)),
            pltpu.SemaphoreType.DMA((6,)),
        ],
        compiler_params=pltpu.CompilerParams(
            collective_id=collective_id, has_side_effects=True, vmem_limit_bytes=48 * 2**20
        ),
        cost_estimate=pl.CostEstimate(flops=int(1e9), bytes_accessed=int(60e6), transcendentals=0),
        name="reduce_pack",
    )(*grads, small)


def gather_rows(shard):
    mats, rows, width = shard.shape
    dp, tensor = lax.axis_size("dp"), lax.axis_size("tensor")
    if (dp, tensor, mats) == (8, 4, 8):
        return gather_pack(shard, 0).reshape(mats, tensor * rows, width)
    piece = mats * rows // dp
    mine = lax.dynamic_slice_in_dim(
        shard.reshape(mats * rows, width), lax.axis_index("dp") * piece, piece, 0
    )
    full = lax.all_gather(mine, ("dp", "tensor"), axis=0, tiled=True)
    full = full.reshape(mats, dp // mats, tensor, piece, width).transpose(0, 2, 1, 3, 4)
    return full.reshape(mats, tensor * rows, width)


def reduce_rows(grads, small):
    mats = len(grads)
    all_rows, width = grads[0].shape
    dp, tensor = lax.axis_size("dp"), lax.axis_size("tensor")
    rows = all_rows // tensor
    if (dp, tensor, mats) == (8, 4, 8):
        return reduce_pack([g.reshape(tensor, rows, width) for g in grads], small, 1)
    piece = mats * rows // dp
    grad = jnp.stack(grads).reshape(mats, tensor, dp // mats, piece, width).transpose(0, 2, 1, 3, 4)
    mine = lax.psum_scatter(
        grad.reshape(dp * tensor * piece, width), ("dp", "tensor"), scatter_dimension=0, tiled=True
    )
    total = lax.all_gather(mine, "dp", axis=0, tiled=True).reshape(mats, rows, width).astype(F32)
    return total, lax.psum(small, ("dp", "tensor"))


def per_device(
    inputs, encoded, cotangent, tgt_seg, src_seg, self_qkv, self_out, cross_q, cross_kv, cross_out, ffn_up, ffn_down, gains, shifts
):
    me = lax.axis_index("tensor")
    t_ids = lax.dynamic_index_in_dim(tgt_seg, me, 0, keepdims=False)
    s_ids = lax.dynamic_index_in_dim(src_seg, me, 0, keepdims=False)
    pack = jnp.concatenate(
        [
            self_qkv.transpose(0, 2, 1),
            self_out[None],
            cross_q.T[None],
            cross_kv.transpose(0, 2, 1),
            cross_out[None],
        ],
        axis=0,
    )
    pack = gather_rows(pack)
    hidden = ffn_down.shape[0]
    width = inputs.shape[1]
    dp, tensor = lax.axis_size("dp"), lax.axis_size("tensor")
    ffn = jnp.stack([ffn_up.T, ffn_down], axis=0)
    piece = hidden // dp
    mine = lax.dynamic_slice_in_dim(ffn, lax.axis_index("dp") * piece, piece, 1)
    ffn = lax.all_gather(mine, ("dp", "tensor"), axis=1, tiled=True)
    w = dict(
        qkv=pack[0:3], out=pack[3], cq=pack[4], ckv=pack[5:7], cout=pack[7],
        up=ffn[0].reshape(tensor, hidden, -1), down=ffn[1].reshape(tensor, hidden, -1),
    )
    layer_out, grad_x, grad_e, grads, grad_gains, grad_shifts = local_step(
        inputs, encoded, cotangent, t_ids, s_ids, w, gains, shifts
    )
    g_ffn = jnp.stack([grads["up"].reshape(-1, width), grads["down"].reshape(-1, width)])
    g_ffn = lax.psum_scatter(g_ffn, ("dp", "tensor"), scatter_dimension=1, tiled=True)
    g_ffn = lax.all_gather(g_ffn, "dp", axis=1, tiled=True)
    small = jnp.concatenate([grad_gains, grad_shifts, jnp.zeros((2, width), F32)], axis=0)
    total, small = reduce_rows(
        [*grads["qkv"], grads["out"], grads["cq"], *grads["ckv"], grads["cout"]], small
    )
    return (
        layer_out,
        grad_x,
        grad_e,
        total[0:3].transpose(0, 2, 1),
        total[3],
        total[4].T,
        total[5:7].transpose(0, 2, 1),
        total[7],
        g_ffn[0].astype(F32).T,
        g_ffn[1].astype(F32),
        small[0:3],
        small[3:6],
    )


def solution(mesh):
    rows = P(("dp", "tensor"), None)
    in_specs = (
        rows, rows, rows, P("dp", None), P("dp", None),
        P(None, None, "tensor"), P("tensor", None), P(None, "tensor"), P(None, None, "tensor"), P("tensor", None),
        P(None, "tensor"), P("tensor", None), P(), P(),
    )
    out_specs = (
        rows, rows, rows,
        P(None, None, "tensor"), P("tensor", None), P(None, "tensor"), P(None, None, "tensor"), P("tensor", None),
        P(None, "tensor"), P("tensor", None), P(), P(),
    )
    return jax.shard_map(per_device, mesh=mesh, in_specs=in_specs, out_specs=out_specs, check_vma=False)
```

```python
import functools
import jax, jax.numpy as jnp
from jax import lax
from jax.sharding import PartitionSpec as P
from jax.experimental import pallas as pl
from jax.experimental.pallas import tpu as pltpu

HDIM = 64
LANES = 128
MASKED = -1e30
EPSILON = 1e-5
F32 = jnp.float32
BF16 = jnp.bfloat16
NT = (((1,), (1,)), ((), ()))
TN = (((0,), (0,)), ((), ()))
NN = (((1,), (0,)), ((), ()))


def dot(a, b, dims):
    return lax.dot_general(a, b, dims, preferred_element_type=F32)


def by_head(x):
    first = lax.broadcasted_iota(jnp.int32, x.shape, 1) < HDIM
    zero = jnp.zeros_like(x)
    return jnp.concatenate([jnp.where(first, x, zero), jnp.where(first, zero, x)], axis=0)


def later_keys(bk, bq, offset):
    row = lax.broadcasted_iota(jnp.int32, (bk, bq), 1)
    col = lax.broadcasted_iota(jnp.int32, (bk, bq), 0)
    late = col > row + offset
    return jnp.concatenate([late, late], axis=1)


def stacked(x):
    n = x.shape[1] // 2
    return jnp.concatenate([x[:, :n], x[:, n:]], axis=0)


def attend_kernel(causal, block, per, lo_ref, hi_ref, q_ref, k_ref, v_ref, fq_ref, fk_ref, o_ref, lse_ref, scores, acc):
    n = q_ref.shape[0]
    for i in range(n // block):
        rows = pl.ds(i * block, block)
        fq = fq_ref[rows, :]
        fq = jnp.concatenate([fq, fq], axis=0)
        qs = [
            jnp.concatenate(
                [by_head(q_ref[rows, h * LANES : (h + 1) * LANES] * jnp.asarray(HDIM ** -0.5, BF16)), fq], axis=1
            )
            for h in range(per)
        ]

        def score(j, tops, diagonal=False):
            keys = pl.ds(pl.multiple_of(j * block, block), block)
            fk = fk_ref[keys, :]
            out = []
            for h in range(per):
                k = k_ref[keys, h * LANES : (h + 1) * LANES]
                s = dot(jnp.concatenate([k, fk], axis=1), qs[h], NT)
                if diagonal:
                    s = jnp.where(later_keys(block, block, 0), MASKED, s)
                scores[h, keys, :] = s
                out.append(jnp.maximum(tops[h], jnp.max(s, axis=0, keepdims=True)))
            return tuple(out)

        def mix(j, totals, tops):
            keys = pl.ds(pl.multiple_of(j * block, block), block)
            out = []
            for h in range(per):
                p = jnp.exp(scores[h, keys, :] - tops[h])
                out.append(totals[h] + jnp.sum(p, axis=0, keepdims=True))
                v = by_head(v_ref[keys, h * LANES : (h + 1) * LANES])
                acc[h] += dot(stacked(p.astype(BF16)), v, TN)
            return tuple(out)

        tops = tuple(jnp.full((1, 2 * block), MASKED, F32) for _ in range(per))
        totals = tuple(jnp.zeros((1, 2 * block), F32) for _ in range(per))
        acc[...] = jnp.zeros_like(acc)
        if causal:
            tops = score(i, tops, True)
            tops = lax.fori_loop(lo_ref[i], i, score, tops)
            totals = lax.fori_loop(lo_ref[i], i + 1, functools.partial(mix, tops=tops), totals)
        else:
            tops = lax.fori_loop(lo_ref[i], hi_ref[i], score, tops)
            totals = lax.fori_loop(lo_ref[i], hi_ref[i], functools.partial(mix, tops=tops), totals)
        for h in range(per):
            inverse = 1.0 / totals[h]
            inverse = jnp.concatenate(
                [jnp.broadcast_to(inverse[:, side * block : (side + 1) * block], (HDIM, block)) for side in range(2)], axis=0
            )
            o_ref[rows, h * LANES : (h + 1) * LANES] = (acc[h] * inverse.T).astype(BF16)
            lse_ref[h, i] = tops[h] + jnp.log(totals[h])


def attend_back_kernel(
    causal, block, per, lo_ref, hi_ref, q_ref, k_ref, v_ref, fq_ref, fk_ref, g_ref, o_ref, lse_ref,
    dq_ref, dk_ref, dv_ref, dq_acc, dk_acc, dv_acc, qs, gs, delta,
):
    n = q_ref.shape[0]
    m = k_ref.shape[0]
    pick = lax.broadcasted_iota(jnp.int32, (8, LANES), 1) // HDIM == lax.broadcasted_iota(jnp.int32, (8, LANES), 0)
    pick = pick.astype(BF16)
    dq_acc[...] = jnp.zeros_like(dq_acc)
    for h in range(per):
        lanes = slice(h * LANES, (h + 1) * LANES)
        for i in range(n // block):
            rows = pl.ds(i * block, block)
            fq = fq_ref[rows, :]
            qs[h, i, :, :LANES] = by_head(q_ref[rows, lanes] * jnp.asarray(HDIM ** -0.5, BF16))
            qs[h, i, :, LANES:] = jnp.concatenate([fq, fq], axis=0)
            gs[h, i] = by_head(g_ref[rows, lanes])
            prod = g_ref[rows, lanes].astype(F32) * o_ref[rows, lanes].astype(F32)
            high = prod.astype(BF16)
            rest = (prod - high.astype(F32)).astype(BF16)
            sums = dot(pick, high, NT) + dot(pick, rest, NT)
            delta[h, i] = jnp.concatenate([sums[0:1], sums[1:2]], axis=1)
    for j in range(m // block):
        keys = pl.ds(j * block, block)
        fk = fk_ref[keys, :]
        dk_acc[...] = jnp.zeros_like(dk_acc)
        dv_acc[...] = jnp.zeros_like(dv_acc)

        def step(i, _, diagonal=False):
            rows = pl.ds(pl.multiple_of(i * block, block), block)
            ss, dps, ps, dss = [], [], [], []
            for h in range(per):
                lanes = slice(h * LANES, (h + 1) * LANES)
                ss.append(dot(jnp.concatenate([k_ref[keys, lanes], fk], axis=1), qs[h, i], NT))
                dps.append(dot(v_ref[keys, lanes], gs[h, i], NT))
            for h in range(per):
                s = ss[h]
                if diagonal:
                    s = jnp.where(later_keys(block, block, 0), MASKED, s)
                p = jnp.exp(s - lse_ref[h, i])
                ps.append(p.astype(BF16))
                dss.append((p * (dps[h] - delta[h, i])).astype(BF16))
            adds = []
            for h in range(per):
                lanes = slice(h * LANES, (h + 1) * LANES)
                adds.append((dot(ps[h], gs[h, i], NN), dot(dss[h], qs[h, i, :, :LANES], NN), dot(stacked(dss[h]), by_head(k_ref[keys, lanes]), TN)))
            for h in range(per):
                lanes = slice(h * LANES, (h + 1) * LANES)
                dv_acc[h] += adds[h][0]
                dk_acc[h] += adds[h][1]
                dq_acc[rows, lanes] += adds[h][2]
            return 0

        if causal:
            step(j, 0, True)
            lax.fori_loop(j + 1, hi_ref[j], step, 0)
        else:
            lax.fori_loop(lo_ref[j], hi_ref[j], step, 0)
        for h in range(per):
            dk_ref[keys, h * LANES : (h + 1) * LANES] = dk_acc[h].astype(BF16)
            dv_ref[keys, h * LANES : (h + 1) * LANES] = dv_acc[h].astype(BF16)
    dq_ref[...] = (dq_acc[...] * HDIM ** -0.5).astype(BF16)


def block_range(own, other, block, other_block):
    own = own.reshape(-1, block)
    lo = jnp.sum((other[None, :] < own[:, :1]).astype(jnp.int32), axis=1) // other_block
    hi = jnp.sum((other[None, :] <= own[:, -1:]).astype(jnp.int32), axis=1)
    return lo, (hi + other_block - 1) // other_block


def seg_features(q_ids, k_ids):
    lanes = jnp.arange(LANES, dtype=jnp.int32)[None, :]
    fq = jnp.where((lanes < 5) & (q_ids[:, None] != lanes), MASKED, 0.0).astype(BF16)
    fk = (k_ids[:, None] == lanes).astype(BF16)
    return fq, fk


VMEM_LIMIT = 56 * 2**20
FWD_PER = 6
BWD_PER = 3


def attend(q, k, v, q_ids, k_ids, fq, fk, causal, block=256, per=FWD_PER):
    n, width = q.shape
    m = k.shape[0]
    lo, hi = block_range(q_ids, k_ids, block, block)
    wide = per * LANES
    pairs = width // LANES
    col = lambda rows: pl.BlockSpec((rows, wide), lambda i, *_: (0, i))
    whole = lambda rows: pl.BlockSpec((rows, LANES), lambda i, *_: (0, 0))
    vec = pl.BlockSpec((per, n // block, 1, 2 * block), lambda i, *_: (i, 0, 0, 0))
    return pl.pallas_call(
        functools.partial(attend_kernel, causal, block, per),
        out_shape=(
            jax.ShapeDtypeStruct((n, width), BF16),
            jax.ShapeDtypeStruct((pairs, n // block, 1, 2 * block), F32),
        ),
        grid_spec=pltpu.PrefetchScalarGridSpec(
            num_scalar_prefetch=2,
            grid=(pairs // per,),
            in_specs=[col(n), col(m), col(m), whole(n), whole(m)],
            out_specs=[col(n), vec],
            scratch_shapes=[pltpu.VMEM((per, m, 2 * block), F32), pltpu.VMEM((per, block, LANES), F32)],
        ),
        compiler_params=pltpu.CompilerParams(vmem_limit_bytes=VMEM_LIMIT),
        cost_estimate=pl.CostEstimate(flops=int(8e9), bytes_accessed=int(8e6), transcendentals=int(4e6)),
        name="attend",
    )(lo, hi, q, k, v, fq, fk)


def attend_back(q, k, v, g, out, lse, q_ids, k_ids, fq, fk, causal, block=256, per=BWD_PER):
    n, width = q.shape
    m = k.shape[0]
    lo, hi = block_range(k_ids, q_ids, block, block)
    wide = per * LANES
    pairs = width // LANES
    count = n // block
    col = lambda rows: pl.BlockSpec((rows, wide), lambda i, *_: (0, i))
    whole = lambda rows: pl.BlockSpec((rows, LANES), lambda i, *_: (0, 0))
    vec = pl.BlockSpec((per, count, 1, 2 * block), lambda i, *_: (i, 0, 0, 0))
    return pl.pallas_call(
        functools.partial(attend_back_kernel, causal, block, per),
        out_shape=(
            jax.ShapeDtypeStruct((n, width), BF16),
            jax.ShapeDtypeStruct((m, width), BF16),
            jax.ShapeDtypeStruct((m, width), BF16),
        ),
        grid_spec=pltpu.PrefetchScalarGridSpec(
            num_scalar_prefetch=2,
            grid=(pairs // per,),
            in_specs=[col(n), col(m), col(m), whole(n), whole(m), col(n), col(n), vec],
            out_specs=[col(n), col(m), col(m)],
            scratch_shapes=[
                pltpu.VMEM((n, wide), F32),
                pltpu.VMEM((per, block, LANES), F32),
                pltpu.VMEM((per, block, LANES), F32),
                pltpu.VMEM((per, count, 2 * block, 2 * LANES), BF16),
                pltpu.VMEM((per, count, 2 * block, LANES), BF16),
                pltpu.VMEM((per, count, 1, 2 * block), F32),
            ],
        ),
        compiler_params=pltpu.CompilerParams(vmem_limit_bytes=VMEM_LIMIT),
        cost_estimate=pl.CostEstimate(flops=int(20e9), bytes_accessed=int(12e6), transcendentals=int(4e6)),
        name="attend_back",
    )(lo, hi, q, k, v, fq, fk, g, out, lse)


def norm_forward(summed, gain, shift):
    centred = summed - jnp.mean(summed, axis=-1, keepdims=True)
    inverse = lax.rsqrt(jnp.mean(centred * centred, axis=-1, keepdims=True) + EPSILON)
    normed = centred * inverse
    return normed * gain + shift, normed, inverse


def norm_backward(upstream, normed, inverse, gain):
    scaled = upstream * gain
    first_mean = jnp.mean(scaled, axis=-1, keepdims=True)
    second_mean = jnp.mean(scaled * normed, axis=-1, keepdims=True)
    result = inverse * (scaled - first_mean - normed * second_mean)
    return result, jnp.sum(upstream * normed, axis=0, keepdims=True), jnp.sum(upstream, axis=0, keepdims=True)


CHUNK = 256


def ffn_kernel(
    r2_ref, ct_ref, gains_ref, shifts_ref, up_ref, down_ref,
    acts_ref, slopes_ref, out_ref, dr3_ref, da3_ref, h2b_ref, gs_ref, h2, a3,
):
    step = pl.program_id(0)
    chunks = r2_ref.shape[0] // CHUNK
    rows_of = lambda c: pl.ds(pl.multiple_of(c * CHUNK, CHUNK), CHUNK)

    @pl.when(step == 0)
    def _():
        def first(c, _):
            rows = rows_of(c)
            h, _, _ = norm_forward(r2_ref[rows, :], gains_ref[1:2, :], shifts_ref[1:2, :])
            h2[rows, :] = h
            h2b_ref[rows, :] = h.astype(BF16)
            a3[rows, :] = jnp.zeros_like(h)
            return 0

        lax.fori_loop(0, chunks, first, 0)

    def main(c, _):
        rows = rows_of(c)
        u = dot(h2b_ref[rows, :], up_ref[...], NT)
        phi = 0.5 * (1.0 + lax.erf(u * (2 ** -0.5)))
        act = (u * phi).astype(BF16)
        acts_ref[rows, :] = act
        slopes_ref[rows, :] = (phi + u * jnp.exp(-0.5 * u * u) * ((2 * jnp.pi) ** -0.5)).astype(BF16)
        a3[rows, :] += dot(act, down_ref[...], NN)
        return 0

    lax.fori_loop(0, chunks, main, 0, unroll=True)

    @pl.when(step == pl.num_programs(0) - 1)
    def _():
        def final(c, carry):
            rows = rows_of(c)
            h, normed, inverse = norm_forward(h2[rows, :] + a3[rows, :], gains_ref[2:3, :], shifts_ref[2:3, :])
            out_ref[rows, :] = h.astype(BF16)
            dr, gg, gs = norm_backward(ct_ref[rows, :].astype(F32), normed, inverse, gains_ref[2:3, :])
            dr3_ref[rows, :] = dr
            da3_ref[rows, :] = dr.astype(BF16)
            return carry[0] + gg, carry[1] + gs

        zero = jnp.zeros((1, r2_ref.shape[1]), F32)
        gg, gs = lax.fori_loop(0, chunks, final, (zero, zero))
        gs_ref[...] = jnp.concatenate([gg, gs], axis=0)


def ffn_back_kernel(
    dr3_ref, da3_ref, h2b_ref, r2_ref, gains_ref, acts_ref, slopes_ref, up_ref, down_ref,
    gup_ref, gdown_ref, dr2_ref, da2_ref, gs_ref, du, dh2,
):
    step = pl.program_id(0)
    chunks = dr3_ref.shape[0] // CHUNK
    rows_of = lambda c: pl.ds(pl.multiple_of(c * CHUNK, CHUNK), CHUNK)

    @pl.when(step == 0)
    def _():
        dh2[...] = dr3_ref[...]

    def main(c, _):
        rows = rows_of(c)
        dg = dot(da3_ref[rows, :], down_ref[...], NT)
        d = (slopes_ref[rows, :].astype(F32) * dg).astype(BF16)
        du[rows, :] = d
        dh2[rows, :] += dot(d, up_ref[...], NN)
        return 0

    lax.fori_loop(0, chunks, main, 0, unroll=True)
    gdown_ref[...] = dot(acts_ref[...], da3_ref[...], TN).astype(BF16)
    gup_ref[...] = dot(du[...], h2b_ref[...], TN).astype(BF16)

    @pl.when(step == pl.num_programs(0) - 1)
    def _():
        def final(c, carry):
            rows = rows_of(c)
            r = r2_ref[rows, :]
            _, normed, inverse = norm_forward(r, gains_ref[1:2, :], 0.0)
            dr, gg, gs = norm_backward(dh2[rows, :], normed, inverse, gains_ref[1:2, :])
            dr2_ref[rows, :] = dr
            da2_ref[rows, :] = dr.astype(BF16)
            return carry[0] + gg, carry[1] + gs

        zero = jnp.zeros((1, r2_ref.shape[1]), F32)
        gg, gs = lax.fori_loop(0, chunks, final, (zero, zero))
        gs_ref[...] = jnp.concatenate([gg, gs], axis=0)


FFN_BLOCK = 512


def ffn(r2, ct, gains, shifts, up, down):
    n, width = r2.shape
    hidden = up.shape[0]
    whole = lambda *s: pl.BlockSpec(s, lambda i: (0,) * len(s))
    wblk = pl.BlockSpec((FFN_BLOCK, width), lambda i: (i, 0))
    ablk = pl.BlockSpec((n, FFN_BLOCK), lambda i: (0, i))
    return pl.pallas_call(
        ffn_kernel,
        grid=(hidden // FFN_BLOCK,),
        in_specs=[whole(n, width), whole(n, width), whole(3, width), whole(3, width), wblk, wblk],
        out_specs=[ablk, ablk, whole(n, width), whole(n, width), whole(n, width), whole(n, width), whole(2, width)],
        out_shape=[
            jax.ShapeDtypeStruct((n, hidden), BF16),
            jax.ShapeDtypeStruct((n, hidden), BF16),
            jax.ShapeDtypeStruct((n, width), BF16),
            jax.ShapeDtypeStruct((n, width), F32),
            jax.ShapeDtypeStruct((n, width), BF16),
            jax.ShapeDtypeStruct((n, width), BF16),
            jax.ShapeDtypeStruct((2, width), F32),
        ],
        scratch_shapes=[pltpu.VMEM((n, width), F32), pltpu.VMEM((n, width), F32)],
        compiler_params=pltpu.CompilerParams(vmem_limit_bytes=VMEM_LIMIT),
        cost_estimate=pl.CostEstimate(flops=4 * n * width * hidden, bytes_accessed=int(30e6), transcendentals=2 * n * hidden),
        name="ffn",
    )(r2, ct, gains, shifts, up, down)


def ffn_back(dr3, da3, h2b, r2, gains, acts, slopes, up, down):
    n, width = r2.shape
    hidden = up.shape[0]
    whole = lambda *s: pl.BlockSpec(s, lambda i: (0,) * len(s))
    wblk = pl.BlockSpec((FFN_BLOCK, width), lambda i: (i, 0))
    ablk = pl.BlockSpec((n, FFN_BLOCK), lambda i: (0, i))
    return pl.pallas_call(
        ffn_back_kernel,
        grid=(hidden // FFN_BLOCK,),
        in_specs=[whole(n, width), whole(n, width), whole(n, width), whole(n, width), whole(3, width), ablk, ablk, wblk, wblk],
        out_specs=[wblk, wblk, whole(n, width), whole(n, width), whole(2, width)],
        out_shape=[
            jax.ShapeDtypeStruct((hidden, width), BF16),
            jax.ShapeDtypeStruct((hidden, width), BF16),
            jax.ShapeDtypeStruct((n, width), F32),
            jax.ShapeDtypeStruct((n, width), BF16),
            jax.ShapeDtypeStruct((2, width), F32),
        ],
        scratch_shapes=[pltpu.VMEM((n, FFN_BLOCK), BF16), pltpu.VMEM((n, width), F32)],
        compiler_params=pltpu.CompilerParams(vmem_limit_bytes=VMEM_LIMIT),
        cost_estimate=pl.CostEstimate(flops=8 * n * width * hidden, bytes_accessed=int(40e6), transcendentals=0),
        name="ffn_back",
    )(dr3, da3, h2b, r2, gains, acts, slopes, up, down)


def local_step(x, e, ct, t_ids, s_ids, w, gains, shifts):
    x32 = x.astype(F32)
    q, k, v = [dot(x, w["qkv"][c], NT).astype(BF16) for c in range(3)]
    k2, v2 = [dot(e, w["ckv"][c], NT).astype(BF16) for c in range(2)]
    fq, fk = seg_features(t_ids, t_ids)
    _, fs = seg_features(t_ids, s_ids)
    ctx1, lse1 = attend(q, k, v, t_ids, t_ids, fq, fk, True)
    h1, n1, i1 = norm_forward(x32 + dot(ctx1, w["out"], NN), gains[0], shifts[0])
    h1b = h1.astype(BF16)
    q2 = dot(h1b, w["cq"], NT).astype(BF16)
    ctx2, lse2 = attend(q2, k2, v2, t_ids, s_ids, fq, fs, False)
    r2 = h1 + dot(ctx2, w["cout"], NN)
    acts, slopes, layer_out, dr3, da3, h2b, small3 = ffn(r2, ct, gains, shifts, w["up"], w["down"])
    g_up, g_down, dr2, da2, small2 = ffn_back(dr3, da3, h2b, r2, gains, acts, slopes, w["up"], w["down"])
    g_cout = dot(ctx2, da2, TN).astype(BF16)
    dctx2 = dot(da2, w["cout"], NT).astype(BF16)
    dq2, dk2, dv2 = attend_back(q2, k2, v2, dctx2, ctx2, lse2, t_ids, s_ids, fq, fs, False)
    g_cq = dot(dq2, h1b, TN).astype(BF16)
    g_ckv = [dot(dk2, e, TN).astype(BF16), dot(dv2, e, TN).astype(BF16)]
    grad_e = (dot(dk2, w["ckv"][0], NN) + dot(dv2, w["ckv"][1], NN)).astype(BF16)
    dh1 = dr2 + dot(dq2, w["cq"], NN)
    dr1, gg1, gs1 = norm_backward(dh1, n1, i1, gains[0])
    da1 = dr1.astype(BF16)
    g_out = dot(ctx1, da1, TN).astype(BF16)
    dctx1 = dot(da1, w["out"], NT).astype(BF16)
    dq, dk, dv = attend_back(q, k, v, dctx1, ctx1, lse1, t_ids, t_ids, fq, fk, True)
    g_qkv = [dot(d, x, TN).astype(BF16) for d in (dq, dk, dv)]
    grad_x = (dr1 + dot(dq, w["qkv"][0], NN) + dot(dk, w["qkv"][1], NN) + dot(dv, w["qkv"][2], NN)).astype(BF16)
    grads = dict(qkv=g_qkv, out=g_out, cq=g_cq, ckv=g_ckv, cout=g_cout, up=g_up, down=g_down)
    grad_gains = jnp.concatenate([gg1, small2[0:1], small3[0:1]], axis=0)
    grad_shifts = jnp.concatenate([gs1, small2[1:2], small3[1:2]], axis=0)
    return layer_out, grad_x, grad_e, grads, grad_gains, grad_shifts

MESH = pl.DeviceIdType.MESH

def greet(devices):
    barrier = pltpu.get_barrier_semaphore()
    for device in devices:
        pl.semaphore_signal(barrier, inc=1, device_id=device, device_id_type=MESH)
    pl.semaphore_wait(barrier, len(devices))


def gather_kernel(groups, chunks, window, pack_ref, out_ref, local_sem, send_sem, recv_sem):
    p, t = lax.axis_index("dp"), lax.axis_index("tensor")
    rows = pack_ref.shape[1]
    n = rows // chunks
    zs = [jnp.bitwise_xor(t, j) for j in (1, 2, 3)]
    to_c, to_x, to_y = [(jnp.bitwise_xor(p, b), t) for b in (1, 2, 4)]
    far = jnp.bitwise_xor(p, 6)
    greet([to_c, to_x, to_y] + [(p, z) for z in zs])
    keep = pltpu.make_async_copy(pack_ref, out_ref.at[:, t], local_sem)
    keep.start()
    count = [0]
    copies = []

    def send(src, dst, device):
        i = count[0]
        count[0] += 1
        copy = pltpu.make_async_remote_copy(
            src, dst, send_sem.at[i], recv_sem.at[i], device_id=device, device_id_type=MESH
        )
        copy.start()
        copies.append(copy)
        return copy

    cut = lambda c: pl.ds(c * n, n)
    steps = [(g, c) for g in range(groups) for c in range(chunks)]
    z_in, x_in, y_in, xd_in, yd_in = {}, {}, {}, {}, {}
    last = []

    def start_z(i):
        g, c = steps[i]
        a = g * 8 + p
        for j in range(3):
            z_in[i, j] = send(pack_ref.at[a, cut(c)], out_ref.at[a, t, cut(c)], (p, zs[j]))

    def stage_z(i):
        g, c = steps[i]
        for j in range(3):
            z_in[i, j].wait_recv()
            ref = out_ref.at[g * 8 + p, zs[j], cut(c)]
            x_in[i, j] = send(ref, ref, to_x)
            y_in[i, j] = send(ref, ref, to_y)
            last.append(send(ref, ref, to_c))
        if i + window < len(steps):
            start_z(i + window)

    def stage_xy(i):
        g, c = steps[i]
        for j in range(3):
            x_in[i, j].wait_recv()
            ref = out_ref.at[g * 8 + to_x[0], zs[j]]
            part = ref.at[pl.ds(c * n, n // 2)]
            yd_in[i, j] = send(part, part, to_y)
            part = ref.at[cut(c)]
            last.append(send(part, part, to_c))
            y_in[i, j].wait_recv()
            ref = out_ref.at[g * 8 + to_y[0], zs[j]]
            part = ref.at[pl.ds(c * n + n // 2, n // 2)]
            xd_in[i, j] = send(part, part, to_x)
            part = ref.at[cut(c)]
            last.append(send(part, part, to_c))

    def stage_far(i):
        g, c = steps[i]
        for j in range(3):
            xd_in[i, j].wait_recv()
            yd_in[i, j].wait_recv()
            ref = out_ref.at[g * 8 + far, zs[j], cut(c)]
            last.append(send(ref, ref, to_c))

    for i in range(window):
        start_z(i)
    stages = (stage_z, stage_xy, stage_far)
    for step in range(len(steps) + 2):
        for k in (2, 1, 0):
            if 0 <= step - k < len(steps):
                stages[k](step - k)
    for copy in last:
        copy.wait_recv()
    for copy in copies:
        copy.wait_send()
    keep.wait()


def gather_pack(pack, collective_id, chunks=3, window=1):
    mats, rows, width = pack.shape
    groups = mats // 8
    count = groups * chunks * (3 + 9 + 3 * 2 + 3 * 2 + 3)
    return pl.pallas_call(
        functools.partial(gather_kernel, groups, chunks, window),
        out_shape=jax.ShapeDtypeStruct((mats, 4, rows, width), pack.dtype),
        in_specs=[pl.BlockSpec(memory_space=pltpu.VMEM)],
        out_specs=pl.BlockSpec(memory_space=pl.ANY),
        scratch_shapes=[
            pltpu.SemaphoreType.DMA,
            pltpu.SemaphoreType.DMA((count,)),
            pltpu.SemaphoreType.DMA((count,)),
        ],
        compiler_params=pltpu.CompilerParams(collective_id=collective_id, has_side_effects=True, vmem_limit_bytes=32 * 2**20),
        name="gather_pack",
    )(pack)


def reduce_kernel(chunks, mats, *refs):
    grads, small_ref = refs[:mats], refs[mats]
    (out_ref, small_out_ref, mine, from_c, from_x1, from_y1, from_x2, from_y2, from_z, piece,
     s_send, s_c, s_x, s_y, s_z, local_sem, send_sem, recv_sem, small_send, small_recv) = refs[mats + 1 :]
    p, t = lax.axis_index("dp"), lax.axis_index("tensor")
    half = grads[0].shape[1] // 2
    n = half // chunks
    per = mats // 4
    core, cx, cy = lax.rem(p, 2), lax.rem(p // 2, 2), p // 4
    chip = p // 2
    zs = [jnp.bitwise_xor(t, j) for j in (1, 2, 3)]
    to_c, to_x, to_y = [(jnp.bitwise_xor(p, b), t) for b in (1, 2, 4)]
    greet([to_c, to_x, to_y] + [(p, z) for z in zs])
    count = [0]
    copies = []

    def send(src, dst, device):
        i = count[0]
        count[0] += 1
        copy = pltpu.make_async_remote_copy(
            src, dst, send_sem.at[i], recv_sem.at[i], device_id=device, device_id_type=MESH
        )
        copy.start()
        copies.append(copy)
        return copy

    small_count = [0]

    def send_small(src, dst, device):
        i = small_count[0]
        small_count[0] += 1
        copy = pltpu.make_async_remote_copy(
            src, dst, small_send.at[i], small_recv.at[i], device_id=device, device_id_type=MESH
        )
        copy.start()
        return copy

    nx, ny = 1 - cx, 1 - cy
    c_in, x1, y1, x2, y2, z_in, gx, gy, gxd, gyd, last = {}, {}, {}, {}, {}, {}, {}, {}, {}, {}, []
    local = {}
    cut = lambda c: pl.ds(c * n, n)
    own_cut = lambda c: pl.ds(pl.multiple_of(core * half + c * n, 16), n)
    other_cut = lambda c: pl.ds(pl.multiple_of((1 - core) * half + c * n, 16), n)
    owned = lambda q: pl.ds(q * per, per)
    for c in range(chunks):
        c_in[c], local[c] = [], []
        for a in range(mats):
            c_in[c].append(send(grads[a].at[:, other_cut(c)], from_c.at[a, :, cut(c)], to_c))
            copy = pltpu.make_async_copy(
                grads[a].at[:, own_cut(c)], mine.at[a, :, cut(c)], local_sem.at[c * mats + a]
            )
            copy.start()
            local[c].append(copy)
    small = send_small(small_ref, s_c, to_c)

    def add(dst, src):
        dst[...] = (dst[...].astype(F32) + src[...].astype(F32)).astype(dst.dtype)

    def stage_c(c):
        for a in range(mats):
            c_in[c][a].wait_recv()
            local[c][a].wait()
            for b in range(4):
                add(mine.at[a, b, cut(c)], from_c.at[a, b, cut(c)])
        x1[c] = [send(mine.at[owned(q * 2 + nx), 0:2, cut(c)], from_x1.at[q, :, :, cut(c)], to_x) for q in range(2)]
        y1[c] = [send(mine.at[owned(ny * 2 + q), 2:4, cut(c)], from_y1.at[q, :, :, cut(c)], to_y) for q in range(2)]

    def stage_xy(c):
        for q in range(2):
            x1[c][q].wait_recv()
            for i in range(per):
                for b in range(2):
                    add(mine.at[(q * 2 + cx) * per + i, b, cut(c)], from_x1.at[q, i, b, cut(c)])
        x2[c] = send(mine.at[owned(ny * 2 + cx), 0:2, cut(c)], from_x2.at[:, :, cut(c)], to_y)
        for q in range(2):
            y1[c][q].wait_recv()
            for i in range(per):
                for b in range(2):
                    add(mine.at[(cy * 2 + q) * per + i, 2 + b, cut(c)], from_y1.at[q, i, b, cut(c)])
        y2[c] = send(mine.at[owned(cy * 2 + nx), 2:4, cut(c)], from_y2.at[:, :, cut(c)], to_x)

    def stage_z(c):
        x2[c].wait_recv()
        for i in range(per):
            for b in range(2):
                add(mine.at[chip * per + i, b, cut(c)], from_x2.at[i, b, cut(c)])
        y2[c].wait_recv()
        for i in range(per):
            for b in range(2):
                add(mine.at[chip * per + i, 2 + b, cut(c)], from_y2.at[i, b, cut(c)])
        z_in[c] = [
            send(mine.at[owned(chip), zs[j], cut(c)], from_z.at[j, :, cut(c)], (p, zs[j])) for j in range(3)
        ]

    def stage_out(c):
        for j in range(3):
            z_in[c][j].wait_recv()
        for i in range(per):
            total = mine[chip * per + i, t, cut(c), :].astype(F32)
            for j in range(3):
                total = total + from_z[j, i, cut(c), :].astype(F32)
            piece[chip * per + i, own_cut(c), :] = total.astype(piece.dtype)
        ref = piece.at[owned(chip), own_cut(c)]
        gx[c] = send(ref, ref, to_x)
        gy[c] = send(ref, ref, to_y)
        last.append(send(ref, ref, to_c))

    def stage_far(c):
        gx[c].wait_recv()
        ref = piece.at[owned(cy * 2 + nx), own_cut(c)]
        gyd[c] = send(ref.at[: per // 2], ref.at[: per // 2], to_y)
        last.append(send(ref, ref, to_c))
        gy[c].wait_recv()
        ref = piece.at[owned(ny * 2 + cx), own_cut(c)]
        gxd[c] = send(ref.at[per // 2 :], ref.at[per // 2 :], to_x)
        last.append(send(ref, ref, to_c))

    def stage_end(c):
        gxd[c].wait_recv()
        gyd[c].wait_recv()
        ref = piece.at[owned(ny * 2 + nx), own_cut(c)]
        last.append(send(ref, ref, to_c))

    stages = (stage_c, stage_xy, stage_z, stage_out, stage_far, stage_end)
    for step in range(chunks + len(stages) - 1):
        for k in reversed(range(len(stages))):
            if 0 <= step - k < chunks:
                stages[k](step - k)
        if step == 0:
            small.wait()
            s_send[0] = small_ref[...] + s_c[...]
            small = send_small(s_send.at[0], s_x, to_x)
        elif step == 1:
            small.wait()
            s_send[1] = s_send[0] + s_x[...]
            small = send_small(s_send.at[1], s_y, to_y)
        elif step == 2:
            small.wait()
            s_send[2] = s_send[1] + s_y[...]
            s_z[t] = s_send[2]
            small = [send_small(s_send.at[2], s_z.at[t], (p, z)) for z in zs]
    for copy in small:
        copy.wait()
    small_out_ref[...] = (s_z[0] + s_z[1]) + (s_z[2] + s_z[3])
    for copy in last:
        copy.wait_recv()
    for copy in copies:
        copy.wait_send()
    for a in range(mats):
        out_ref[a] = piece[a].astype(out_ref.dtype)


def reduce_pack(grads, small, collective_id, chunks=3):
    mats = len(grads)
    tensor, rows, width = grads[0].shape
    half, per = rows // 2, mats // 4
    count = chunks * (mats + 4 + 2 + 3 + 3 + 4 + 1)
    vmem = pl.BlockSpec(memory_space=pltpu.VMEM)
    buf = lambda *s: pltpu.VMEM(s + (half, width), BF16)
    sb = lambda *s: pltpu.VMEM(s + small.shape, F32)
    return pl.pallas_call(
        functools.partial(reduce_kernel, chunks, mats),
        out_shape=(jax.ShapeDtypeStruct((mats, rows, width), F32), jax.ShapeDtypeStruct(small.shape, F32)),
        in_specs=[pl.BlockSpec(memory_space=pl.ANY)] * mats + [vmem],
        out_specs=(vmem, vmem),
        scratch_shapes=[
            buf(mats, 4), buf(mats, 4), buf(2, per, 2), buf(2, per, 2), buf(per, 2), buf(per, 2), buf(3, per),
            pltpu.VMEM((mats, rows, width), BF16),
            sb(3), sb(), sb(), sb(), sb(4),
            pltpu.SemaphoreType.DMA((chunks * mats,)),
            pltpu.SemaphoreType.DMA((count,)),
            pltpu.SemaphoreType.DMA((count,)),
            pltpu.SemaphoreType.DMA((6,)),
            pltpu.SemaphoreType.DMA((6,)),
        ],
        compiler_params=pltpu.CompilerParams(
            collective_id=collective_id, has_side_effects=True, vmem_limit_bytes=48 * 2**20
        ),
        cost_estimate=pl.CostEstimate(flops=int(1e9), bytes_accessed=int(60e6), transcendentals=0),
        name="reduce_pack",
    )(*grads, small)


def gather_rows(shard):
    mats, rows, width = shard.shape
    dp, tensor = lax.axis_size("dp"), lax.axis_size("tensor")
    if (dp, tensor, mats) == (8, 4, 8):
        return gather_pack(shard, 0).reshape(mats, tensor * rows, width)
    piece = mats * rows // dp
    mine = lax.dynamic_slice_in_dim(
        shard.reshape(mats * rows, width), lax.axis_index("dp") * piece, piece, 0
    )
    full = lax.all_gather(mine, ("dp", "tensor"), axis=0, tiled=True)
    full = full.reshape(mats, dp // mats, tensor, piece, width).transpose(0, 2, 1, 3, 4)
    return full.reshape(mats, tensor * rows, width)


def reduce_rows(grads, small):
    mats = len(grads)
    all_rows, width = grads[0].shape
    dp, tensor = lax.axis_size("dp"), lax.axis_size("tensor")
    rows = all_rows // tensor
    if (dp, tensor, mats) == (8, 4, 8):
        return reduce_pack([g.reshape(tensor, rows, width) for g in grads], small, 1)
    piece = mats * rows // dp
    grad = jnp.stack(grads).reshape(mats, tensor, dp // mats, piece, width).transpose(0, 2, 1, 3, 4)
    mine = lax.psum_scatter(
        grad.reshape(dp * tensor * piece, width), ("dp", "tensor"), scatter_dimension=0, tiled=True
    )
    total = lax.all_gather(mine, "dp", axis=0, tiled=True).reshape(mats, rows, width).astype(F32)
    return total, lax.psum(small, ("dp", "tensor"))


def per_device(
    inputs, encoded, cotangent, tgt_seg, src_seg, self_qkv, self_out, cross_q, cross_kv, cross_out, ffn_up, ffn_down, gains, shifts
):
    me = lax.axis_index("tensor")
    t_ids = lax.dynamic_index_in_dim(tgt_seg, me, 0, keepdims=False)
    s_ids = lax.dynamic_index_in_dim(src_seg, me, 0, keepdims=False)
    pack = jnp.concatenate(
        [
            self_qkv.transpose(0, 2, 1),
            self_out[None],
            cross_q.T[None],
            cross_kv.transpose(0, 2, 1),
            cross_out[None],
        ],
        axis=0,
    )
    pack = gather_rows(pack)
    hidden = ffn_down.shape[0]
    width = inputs.shape[1]
    dp, tensor = lax.axis_size("dp"), lax.axis_size("tensor")
    piece = hidden // dp
    start = lax.axis_index("dp") * piece
    up, down = [
        lax.all_gather(lax.dynamic_slice_in_dim(m, start, piece, 0), ("dp", "tensor"), axis=0, tiled=True)
        for m in (ffn_up.T, ffn_down)
    ]
    w = dict(qkv=pack[0:3], out=pack[3], cq=pack[4], ckv=pack[5:7], cout=pack[7], up=up, down=down)
    layer_out, grad_x, grad_e, grads, grad_gains, grad_shifts = local_step(
        inputs, encoded, cotangent, t_ids, s_ids, w, gains, shifts
    )
    g_up, g_down = [
        lax.all_gather(
            lax.psum_scatter(grads[name], ("dp", "tensor"), scatter_dimension=0, tiled=True), "dp", axis=0, tiled=True
        )
        for name in ("up", "down")
    ]
    small = jnp.concatenate([grad_gains, grad_shifts, jnp.zeros((2, width), F32)], axis=0)
    total, small = reduce_rows(
        [*grads["qkv"], grads["out"], grads["cq"], *grads["ckv"], grads["cout"]], small
    )
    return (
        layer_out,
        grad_x,
        grad_e,
        total[0:3].transpose(0, 2, 1),
        total[3],
        total[4].T,
        total[5:7].transpose(0, 2, 1),
        total[7],
        g_up.astype(F32).T,
        g_down.astype(F32),
        small[0:3],
        small[3:6],
    )


def solution(mesh):
    rows = P(("dp", "tensor"), None)
    in_specs = (
        rows, rows, rows, P("dp", None), P("dp", None),
        P(None, None, "tensor"), P("tensor", None), P(None, "tensor"), P(None, None, "tensor"), P("tensor", None),
        P(None, "tensor"), P("tensor", None), P(), P(),
    )
    out_specs = (
        rows, rows, rows,
        P(None, None, "tensor"), P("tensor", None), P(None, "tensor"), P(None, None, "tensor"), P("tensor", None),
        P(None, "tensor"), P("tensor", None), P(), P(),
    )
    return jax.shard_map(per_device, mesh=mesh, in_specs=in_specs, out_specs=out_specs, check_vma=False)
```

```python
import functools
import jax, jax.numpy as jnp
from jax import lax
from jax.sharding import PartitionSpec as P
from jax.experimental import pallas as pl
from jax.experimental.pallas import tpu as pltpu

HDIM = 64
LANES = 128
MASKED = -1e30
EPSILON = 1e-5
F32 = jnp.float32
BF16 = jnp.bfloat16
NT = (((1,), (1,)), ((), ()))
TN = (((0,), (0,)), ((), ()))
NN = (((1,), (0,)), ((), ()))


def dot(a, b, dims):
    return lax.dot_general(a, b, dims, preferred_element_type=F32)


def by_head(x):
    first = lax.broadcasted_iota(jnp.int32, x.shape, 1) < HDIM
    zero = jnp.zeros_like(x)
    return jnp.concatenate([jnp.where(first, x, zero), jnp.where(first, zero, x)], axis=0)


def later_keys(bk, bq, offset):
    row = lax.broadcasted_iota(jnp.int32, (bk, bq), 1)
    col = lax.broadcasted_iota(jnp.int32, (bk, bq), 0)
    late = col > row + offset
    return jnp.concatenate([late, late], axis=1)


def stacked(x):
    n = x.shape[1] // 2
    return jnp.concatenate([x[:, :n], x[:, n:]], axis=0)


def attend_kernel(causal, block, per, lo_ref, hi_ref, q_ref, k_ref, v_ref, fq_ref, fk_ref, o_ref, lse_ref, scores, acc):
    n = q_ref.shape[0]
    for i in range(n // block):
        rows = pl.ds(i * block, block)
        fq = fq_ref[rows, :]
        fq = jnp.concatenate([fq, fq], axis=0)
        qs = [
            jnp.concatenate(
                [by_head(q_ref[rows, h * LANES : (h + 1) * LANES] * jnp.asarray(HDIM ** -0.5, BF16)), fq], axis=1
            )
            for h in range(per)
        ]

        def score(j, tops, diagonal=False):
            keys = pl.ds(pl.multiple_of(j * block, block), block)
            fk = fk_ref[keys, :]
            out = []
            for h in range(per):
                k = k_ref[keys, h * LANES : (h + 1) * LANES]
                s = dot(jnp.concatenate([k, fk], axis=1), qs[h], NT)
                if diagonal:
                    s = jnp.where(later_keys(block, block, 0), MASKED, s)
                scores[h, keys, :] = s
                out.append(jnp.maximum(tops[h], jnp.max(s, axis=0, keepdims=True)))
            return tuple(out)

        def mix(j, totals, tops):
            keys = pl.ds(pl.multiple_of(j * block, block), block)
            out = []
            for h in range(per):
                p = jnp.exp(scores[h, keys, :] - tops[h])
                out.append(totals[h] + jnp.sum(p, axis=0, keepdims=True))
                v = by_head(v_ref[keys, h * LANES : (h + 1) * LANES])
                acc[h] += dot(stacked(p.astype(BF16)), v, TN)
            return tuple(out)

        tops = tuple(jnp.full((1, 2 * block), MASKED, F32) for _ in range(per))
        totals = tuple(jnp.zeros((1, 2 * block), F32) for _ in range(per))
        acc[...] = jnp.zeros_like(acc)
        if causal:
            tops = score(i, tops, True)
            tops = lax.fori_loop(lo_ref[i], i, score, tops)
            totals = lax.fori_loop(lo_ref[i], i + 1, functools.partial(mix, tops=tops), totals)
        else:
            tops = lax.fori_loop(lo_ref[i], hi_ref[i], score, tops)
            totals = lax.fori_loop(lo_ref[i], hi_ref[i], functools.partial(mix, tops=tops), totals)
        for h in range(per):
            inverse = 1.0 / totals[h]
            inverse = jnp.concatenate(
                [jnp.broadcast_to(inverse[:, side * block : (side + 1) * block], (HDIM, block)) for side in range(2)], axis=0
            )
            o_ref[rows, h * LANES : (h + 1) * LANES] = (acc[h] * inverse.T).astype(BF16)
            lse_ref[h, i] = tops[h] + jnp.log(totals[h])


def attend_back_kernel(
    causal, block, per, lo_ref, hi_ref, q_ref, k_ref, v_ref, fq_ref, fk_ref, g_ref, o_ref, lse_ref,
    dq_ref, dk_ref, dv_ref, dq_acc, dk_acc, dv_acc, qs, gs, delta,
):
    n = q_ref.shape[0]
    m = k_ref.shape[0]
    pick = lax.broadcasted_iota(jnp.int32, (8, LANES), 1) // HDIM == lax.broadcasted_iota(jnp.int32, (8, LANES), 0)
    pick = pick.astype(BF16)
    dq_acc[...] = jnp.zeros_like(dq_acc)
    for h in range(per):
        lanes = slice(h * LANES, (h + 1) * LANES)
        for i in range(n // block):
            rows = pl.ds(i * block, block)
            fq = fq_ref[rows, :]
            qs[h, i, :, :LANES] = by_head(q_ref[rows, lanes] * jnp.asarray(HDIM ** -0.5, BF16))
            qs[h, i, :, LANES:] = jnp.concatenate([fq, fq], axis=0)
            gs[h, i] = by_head(g_ref[rows, lanes])
            prod = g_ref[rows, lanes].astype(F32) * o_ref[rows, lanes].astype(F32)
            high = prod.astype(BF16)
            rest = (prod - high.astype(F32)).astype(BF16)
            sums = dot(pick, high, NT) + dot(pick, rest, NT)
            delta[h, i] = jnp.concatenate([sums[0:1], sums[1:2]], axis=1)
    for j in range(m // block):
        keys = pl.ds(j * block, block)
        fk = fk_ref[keys, :]
        dk_acc[...] = jnp.zeros_like(dk_acc)
        dv_acc[...] = jnp.zeros_like(dv_acc)

        def step(i, _, diagonal=False):
            rows = pl.ds(pl.multiple_of(i * block, block), block)
            ss, dps, ps, dss = [], [], [], []
            for h in range(per):
                lanes = slice(h * LANES, (h + 1) * LANES)
                ss.append(dot(jnp.concatenate([k_ref[keys, lanes], fk], axis=1), qs[h, i], NT))
                dps.append(dot(v_ref[keys, lanes], gs[h, i], NT))
            for h in range(per):
                s = ss[h]
                if diagonal:
                    s = jnp.where(later_keys(block, block, 0), MASKED, s)
                p = jnp.exp(s - lse_ref[h, i])
                ps.append(p.astype(BF16))
                dss.append((p * (dps[h] - delta[h, i])).astype(BF16))
            adds = []
            for h in range(per):
                lanes = slice(h * LANES, (h + 1) * LANES)
                adds.append((dot(ps[h], gs[h, i], NN), dot(dss[h], qs[h, i, :, :LANES], NN), dot(stacked(dss[h]), by_head(k_ref[keys, lanes]), TN)))
            for h in range(per):
                lanes = slice(h * LANES, (h + 1) * LANES)
                dv_acc[h] += adds[h][0]
                dk_acc[h] += adds[h][1]
                dq_acc[rows, lanes] += adds[h][2]
            return 0

        if causal:
            step(j, 0, True)
            lax.fori_loop(j + 1, hi_ref[j], step, 0)
        else:
            lax.fori_loop(lo_ref[j], hi_ref[j], step, 0)
        for h in range(per):
            dk_ref[keys, h * LANES : (h + 1) * LANES] = dk_acc[h].astype(BF16)
            dv_ref[keys, h * LANES : (h + 1) * LANES] = dv_acc[h].astype(BF16)
    dq_ref[...] = (dq_acc[...] * HDIM ** -0.5).astype(BF16)


def block_range(own, other, block, other_block):
    own = own.reshape(-1, block)
    lo = jnp.sum((other[None, :] < own[:, :1]).astype(jnp.int32), axis=1) // other_block
    hi = jnp.sum((other[None, :] <= own[:, -1:]).astype(jnp.int32), axis=1)
    return lo, (hi + other_block - 1) // other_block


def seg_features(q_ids, k_ids):
    lanes = jnp.arange(LANES, dtype=jnp.int32)[None, :]
    fq = jnp.where((lanes < 5) & (q_ids[:, None] != lanes), MASKED, 0.0).astype(BF16)
    fk = (k_ids[:, None] == lanes).astype(BF16)
    return fq, fk


VMEM_LIMIT = 56 * 2**20
FWD_PER = 3
BWD_PER = 3


def attend(q, k, v, q_ids, k_ids, fq, fk, causal, block=256, per=FWD_PER):
    n, width = q.shape
    m = k.shape[0]
    lo, hi = block_range(q_ids, k_ids, block, block)
    wide = per * LANES
    pairs = width // LANES
    col = lambda rows: pl.BlockSpec((rows, wide), lambda i, *_: (0, i))
    whole = lambda rows: pl.BlockSpec((rows, LANES), lambda i, *_: (0, 0))
    vec = pl.BlockSpec((per, n // block, 1, 2 * block), lambda i, *_: (i, 0, 0, 0))
    return pl.pallas_call(
        functools.partial(attend_kernel, causal, block, per),
        out_shape=(
            jax.ShapeDtypeStruct((n, width), BF16),
            jax.ShapeDtypeStruct((pairs, n // block, 1, 2 * block), F32),
        ),
        grid_spec=pltpu.PrefetchScalarGridSpec(
            num_scalar_prefetch=2,
            grid=(pairs // per,),
            in_specs=[col(n), col(m), col(m), whole(n), whole(m)],
            out_specs=[col(n), vec],
            scratch_shapes=[pltpu.VMEM((per, m, 2 * block), F32), pltpu.VMEM((per, block, LANES), F32)],
        ),
        compiler_params=pltpu.CompilerParams(vmem_limit_bytes=VMEM_LIMIT),
        cost_estimate=pl.CostEstimate(flops=int(8e9), bytes_accessed=int(8e6), transcendentals=int(4e6)),
        name="attend",
    )(lo, hi, q, k, v, fq, fk)


def attend_back(q, k, v, g, out, lse, q_ids, k_ids, fq, fk, causal, block=256, per=BWD_PER):
    n, width = q.shape
    m = k.shape[0]
    lo, hi = block_range(k_ids, q_ids, block, block)
    wide = per * LANES
    pairs = width // LANES
    count = n // block
    col = lambda rows: pl.BlockSpec((rows, wide), lambda i, *_: (0, i))
    whole = lambda rows: pl.BlockSpec((rows, LANES), lambda i, *_: (0, 0))
    vec = pl.BlockSpec((per, count, 1, 2 * block), lambda i, *_: (i, 0, 0, 0))
    return pl.pallas_call(
        functools.partial(attend_back_kernel, causal, block, per),
        out_shape=(
            jax.ShapeDtypeStruct((n, width), BF16),
            jax.ShapeDtypeStruct((m, width), BF16),
            jax.ShapeDtypeStruct((m, width), BF16),
        ),
        grid_spec=pltpu.PrefetchScalarGridSpec(
            num_scalar_prefetch=2,
            grid=(pairs // per,),
            in_specs=[col(n), col(m), col(m), whole(n), whole(m), col(n), col(n), vec],
            out_specs=[col(n), col(m), col(m)],
            scratch_shapes=[
                pltpu.VMEM((n, wide), F32),
                pltpu.VMEM((per, block, LANES), F32),
                pltpu.VMEM((per, block, LANES), F32),
                pltpu.VMEM((per, count, 2 * block, 2 * LANES), BF16),
                pltpu.VMEM((per, count, 2 * block, LANES), BF16),
                pltpu.VMEM((per, count, 1, 2 * block), F32),
            ],
        ),
        compiler_params=pltpu.CompilerParams(vmem_limit_bytes=VMEM_LIMIT),
        cost_estimate=pl.CostEstimate(flops=int(20e9), bytes_accessed=int(12e6), transcendentals=int(4e6)),
        name="attend_back",
    )(lo, hi, q, k, v, fq, fk, g, out, lse)


def norm_forward(summed, gain, shift):
    centred = summed - jnp.mean(summed, axis=-1, keepdims=True)
    inverse = lax.rsqrt(jnp.mean(centred * centred, axis=-1, keepdims=True) + EPSILON)
    normed = centred * inverse
    return normed * gain + shift, normed, inverse


def norm_backward(upstream, normed, inverse, gain):
    scaled = upstream * gain
    first_mean = jnp.mean(scaled, axis=-1, keepdims=True)
    second_mean = jnp.mean(scaled * normed, axis=-1, keepdims=True)
    result = inverse * (scaled - first_mean - normed * second_mean)
    return result, jnp.sum(upstream * normed, axis=0, keepdims=True), jnp.sum(upstream, axis=0, keepdims=True)


CHUNK = 256


def ffn_kernel(
    r2_ref, ct_ref, gains_ref, shifts_ref, w_ref,
    acts_ref, slopes_ref, out_ref, dr3_ref, da3_ref, h2b_ref, gs_ref, h2, a3,
):
    step = pl.program_id(0)
    chunks = r2_ref.shape[0] // CHUNK
    rows_of = lambda c: pl.ds(pl.multiple_of(c * CHUNK, CHUNK), CHUNK)

    @pl.when(step == 0)
    def _():
        def first(c, _):
            rows = rows_of(c)
            h, _, _ = norm_forward(r2_ref[rows, :], gains_ref[1:2, :], shifts_ref[1:2, :])
            h2[rows, :] = h
            h2b_ref[rows, :] = h.astype(BF16)
            a3[rows, :] = jnp.zeros_like(h)
            return 0

        lax.fori_loop(0, chunks, first, 0)

    def main(c, _):
        rows = rows_of(c)
        u = dot(h2b_ref[rows, :], w_ref[0], NT)
        phi = 0.5 * (1.0 + lax.erf(u * (2 ** -0.5)))
        act = (u * phi).astype(BF16)
        acts_ref[rows, :] = act
        slopes_ref[rows, :] = (phi + u * jnp.exp(-0.5 * u * u) * ((2 * jnp.pi) ** -0.5)).astype(BF16)
        a3[rows, :] += dot(act, w_ref[1], NN)
        return 0

    lax.fori_loop(0, chunks, main, 0, unroll=True)

    @pl.when(step == pl.num_programs(0) - 1)
    def _():
        def final(c, carry):
            rows = rows_of(c)
            h, normed, inverse = norm_forward(h2[rows, :] + a3[rows, :], gains_ref[2:3, :], shifts_ref[2:3, :])
            out_ref[rows, :] = h.astype(BF16)
            dr, gg, gs = norm_backward(ct_ref[rows, :].astype(F32), normed, inverse, gains_ref[2:3, :])
            dr3_ref[rows, :] = dr
            da3_ref[rows, :] = dr.astype(BF16)
            return carry[0] + gg, carry[1] + gs

        zero = jnp.zeros((1, r2_ref.shape[1]), F32)
        gg, gs = lax.fori_loop(0, chunks, final, (zero, zero))
        gs_ref[...] = jnp.concatenate([gg, gs], axis=0)


def ffn_back_kernel(
    dr3_ref, da3_ref, h2b_ref, r2_ref, gains_ref, acts_ref, slopes_ref, w_ref,
    g_ref, dr2_ref, da2_ref, gs_ref, du, dh2,
):
    step = pl.program_id(0)
    chunks = dr3_ref.shape[0] // CHUNK
    rows_of = lambda c: pl.ds(pl.multiple_of(c * CHUNK, CHUNK), CHUNK)

    @pl.when(step == 0)
    def _():
        dh2[...] = dr3_ref[...]

    def main(c, _):
        rows = rows_of(c)
        dg = dot(da3_ref[rows, :], w_ref[1], NT)
        d = (slopes_ref[rows, :].astype(F32) * dg).astype(BF16)
        du[rows, :] = d
        dh2[rows, :] += dot(d, w_ref[0], NN)
        return 0

    lax.fori_loop(0, chunks, main, 0, unroll=True)
    g_ref[1] = dot(acts_ref[...], da3_ref[...], TN).astype(BF16)
    g_ref[0] = dot(du[...], h2b_ref[...], TN).astype(BF16)

    @pl.when(step == pl.num_programs(0) - 1)
    def _():
        def final(c, carry):
            rows = rows_of(c)
            r = r2_ref[rows, :]
            _, normed, inverse = norm_forward(r, gains_ref[1:2, :], 0.0)
            dr, gg, gs = norm_backward(dh2[rows, :], normed, inverse, gains_ref[1:2, :])
            dr2_ref[rows, :] = dr
            da2_ref[rows, :] = dr.astype(BF16)
            return carry[0] + gg, carry[1] + gs

        zero = jnp.zeros((1, r2_ref.shape[1]), F32)
        gg, gs = lax.fori_loop(0, chunks, final, (zero, zero))
        gs_ref[...] = jnp.concatenate([gg, gs], axis=0)


FFN_BLOCK = 512


def ffn(r2, ct, gains, shifts, w):
    n, width = r2.shape
    hidden = w.shape[1]
    whole = lambda *s: pl.BlockSpec(s, lambda i: (0,) * len(s))
    wblk = pl.BlockSpec((2, FFN_BLOCK, width), lambda i: (0, i, 0))
    ablk = pl.BlockSpec((n, FFN_BLOCK), lambda i: (0, i))
    return pl.pallas_call(
        ffn_kernel,
        grid=(hidden // FFN_BLOCK,),
        in_specs=[whole(n, width), whole(n, width), whole(3, width), whole(3, width), wblk],
        out_specs=[ablk, ablk, whole(n, width), whole(n, width), whole(n, width), whole(n, width), whole(2, width)],
        out_shape=[
            jax.ShapeDtypeStruct((n, hidden), BF16),
            jax.ShapeDtypeStruct((n, hidden), BF16),
            jax.ShapeDtypeStruct((n, width), BF16),
            jax.ShapeDtypeStruct((n, width), F32),
            jax.ShapeDtypeStruct((n, width), BF16),
            jax.ShapeDtypeStruct((n, width), BF16),
            jax.ShapeDtypeStruct((2, width), F32),
        ],
        scratch_shapes=[pltpu.VMEM((n, width), F32), pltpu.VMEM((n, width), F32)],
        compiler_params=pltpu.CompilerParams(vmem_limit_bytes=VMEM_LIMIT),
        cost_estimate=pl.CostEstimate(flops=4 * n * width * hidden, bytes_accessed=int(30e6), transcendentals=2 * n * hidden),
        name="ffn",
    )(r2, ct, gains, shifts, w)


def ffn_back(dr3, da3, h2b, r2, gains, acts, slopes, w):
    n, width = r2.shape
    hidden = w.shape[1]
    whole = lambda *s: pl.BlockSpec(s, lambda i: (0,) * len(s))
    wblk = pl.BlockSpec((2, FFN_BLOCK, width), lambda i: (0, i, 0))
    ablk = pl.BlockSpec((n, FFN_BLOCK), lambda i: (0, i))
    return pl.pallas_call(
        ffn_back_kernel,
        grid=(hidden // FFN_BLOCK,),
        in_specs=[whole(n, width), whole(n, width), whole(n, width), whole(n, width), whole(3, width), ablk, ablk, wblk],
        out_specs=[wblk, whole(n, width), whole(n, width), whole(2, width)],
        out_shape=[
            jax.ShapeDtypeStruct((2, hidden, width), BF16),
            jax.ShapeDtypeStruct((n, width), F32),
            jax.ShapeDtypeStruct((n, width), BF16),
            jax.ShapeDtypeStruct((2, width), F32),
        ],
        scratch_shapes=[pltpu.VMEM((n, FFN_BLOCK), BF16), pltpu.VMEM((n, width), F32)],
        compiler_params=pltpu.CompilerParams(vmem_limit_bytes=VMEM_LIMIT),
        cost_estimate=pl.CostEstimate(flops=8 * n * width * hidden, bytes_accessed=int(40e6), transcendentals=0),
        name="ffn_back",
    )(dr3, da3, h2b, r2, gains, acts, slopes, w)


def local_step(x, e, ct, t_ids, s_ids, w, gains, shifts, halvings):
    x32 = x.astype(F32)
    q, k, v = [dot(x, w["qkv"][c], NT).astype(BF16) for c in range(3)]
    k2, v2 = [dot(e, w["ckv"][c], NT).astype(BF16) for c in range(2)]
    fq, fk = seg_features(t_ids, t_ids)
    _, fs = seg_features(t_ids, s_ids)
    ctx1, lse1 = attend(q, k, v, t_ids, t_ids, fq, fk, True)
    h1, n1, i1 = norm_forward(x32 + dot(ctx1, w["out"], NN), gains[0], shifts[0])
    h1b = h1.astype(BF16)
    q2 = dot(h1b, w["cq"], NT).astype(BF16)
    ctx2, lse2 = attend(q2, k2, v2, t_ids, s_ids, fq, fs, False)
    r2 = h1 + dot(ctx2, w["cout"], NN)
    acts, slopes, layer_out, dr3, da3, h2b, small3 = ffn(r2, ct, gains, shifts, w["ffn"])
    g_ffn, dr2, da2, small2 = ffn_back(dr3, da3, h2b, r2, gains, acts, slopes, w["ffn"])
    g_ffn = halvings[0](g_ffn)
    g_cout = dot(ctx2, da2, TN).astype(BF16)
    dctx2 = dot(da2, w["cout"], NT).astype(BF16)
    dctx2, g_ffn = lax.optimization_barrier((dctx2, g_ffn))
    g_ffn = halvings[1](g_ffn)
    dq2, dk2, dv2 = attend_back(q2, k2, v2, dctx2, ctx2, lse2, t_ids, s_ids, fq, fs, False)
    dq2, dk2, dv2, g_ffn = lax.optimization_barrier((dq2, dk2, dv2, g_ffn))
    g_ffn = halvings[2](g_ffn)
    g_cq = dot(dq2, h1b, TN).astype(BF16)
    g_ckv = [dot(dk2, e, TN).astype(BF16), dot(dv2, e, TN).astype(BF16)]
    grad_e = (dot(dk2, w["ckv"][0], NN) + dot(dv2, w["ckv"][1], NN)).astype(BF16)
    dh1 = dr2 + dot(dq2, w["cq"], NN)
    dr1, gg1, gs1 = norm_backward(dh1, n1, i1, gains[0])
    da1 = dr1.astype(BF16)
    g_out = dot(ctx1, da1, TN).astype(BF16)
    dctx1 = dot(da1, w["out"], NT).astype(BF16)
    dq, dk, dv = attend_back(q, k, v, dctx1, ctx1, lse1, t_ids, t_ids, fq, fk, True)
    dq, dk, dv, g_ffn = lax.optimization_barrier((dq, dk, dv, g_ffn))
    g_qkv = [dot(d, x, TN).astype(BF16) for d in (dq, dk, dv)]
    grad_x = (dr1 + dot(dq, w["qkv"][0], NN) + dot(dk, w["qkv"][1], NN) + dot(dv, w["qkv"][2], NN)).astype(BF16)
    grads = dict(qkv=g_qkv, out=g_out, cq=g_cq, ckv=g_ckv, cout=g_cout, ffn=g_ffn)
    grad_gains = jnp.concatenate([gg1, small2[0:1], small3[0:1]], axis=0)
    grad_shifts = jnp.concatenate([gs1, small2[1:2], small3[1:2]], axis=0)
    return layer_out, grad_x, grad_e, grads, grad_gains, grad_shifts

MESH = pl.DeviceIdType.MESH

def greet(devices):
    barrier = pltpu.get_barrier_semaphore()
    for device in devices:
        pl.semaphore_signal(barrier, inc=1, device_id=device, device_id_type=MESH)
    pl.semaphore_wait(barrier, len(devices))


def gather_kernel(groups, chunks, window, pack_ref, out_ref, local_sem, send_sem, recv_sem):
    p, t = lax.axis_index("dp"), lax.axis_index("tensor")
    rows = pack_ref.shape[1]
    n = rows // chunks
    zs = [jnp.bitwise_xor(t, j) for j in (1, 2, 3)]
    to_c, to_x, to_y = [(jnp.bitwise_xor(p, b), t) for b in (1, 2, 4)]
    far = jnp.bitwise_xor(p, 6)
    greet([to_c, to_x, to_y] + [(p, z) for z in zs])
    keep = pltpu.make_async_copy(pack_ref, out_ref.at[:, t], local_sem)
    keep.start()
    count = [0]
    copies = []

    def send(src, dst, device):
        i = count[0]
        count[0] += 1
        copy = pltpu.make_async_remote_copy(
            src, dst, send_sem.at[i], recv_sem.at[i], device_id=device, device_id_type=MESH
        )
        copy.start()
        copies.append(copy)
        return copy

    cut = lambda c: pl.ds(c * n, n)
    steps = [(g, c) for g in range(groups) for c in range(chunks)]
    z_in, x_in, y_in, xd_in, yd_in = {}, {}, {}, {}, {}
    last = []

    def start_z(i):
        g, c = steps[i]
        a = g * 8 + p
        for j in range(3):
            z_in[i, j] = send(pack_ref.at[a, cut(c)], out_ref.at[a, t, cut(c)], (p, zs[j]))

    def stage_z(i):
        g, c = steps[i]
        for j in range(3):
            z_in[i, j].wait_recv()
            ref = out_ref.at[g * 8 + p, zs[j], cut(c)]
            x_in[i, j] = send(ref, ref, to_x)
            y_in[i, j] = send(ref, ref, to_y)
            last.append(send(ref, ref, to_c))
        if i + window < len(steps):
            start_z(i + window)

    def stage_xy(i):
        g, c = steps[i]
        for j in range(3):
            x_in[i, j].wait_recv()
            ref = out_ref.at[g * 8 + to_x[0], zs[j]]
            part = ref.at[pl.ds(c * n, n // 2)]
            yd_in[i, j] = send(part, part, to_y)
            part = ref.at[cut(c)]
            last.append(send(part, part, to_c))
            y_in[i, j].wait_recv()
            ref = out_ref.at[g * 8 + to_y[0], zs[j]]
            part = ref.at[pl.ds(c * n + n // 2, n // 2)]
            xd_in[i, j] = send(part, part, to_x)
            part = ref.at[cut(c)]
            last.append(send(part, part, to_c))

    def stage_far(i):
        g, c = steps[i]
        for j in range(3):
            xd_in[i, j].wait_recv()
            yd_in[i, j].wait_recv()
            ref = out_ref.at[g * 8 + far, zs[j], cut(c)]
            last.append(send(ref, ref, to_c))

    for i in range(window):
        start_z(i)
    stages = (stage_z, stage_xy, stage_far)
    for step in range(len(steps) + 2):
        for k in (2, 1, 0):
            if 0 <= step - k < len(steps):
                stages[k](step - k)
    for copy in last:
        copy.wait_recv()
    for copy in copies:
        copy.wait_send()
    keep.wait()


def gather_pack(pack, collective_id, chunks=3, window=1):
    mats, rows, width = pack.shape
    groups = mats // 8
    count = groups * chunks * (3 + 9 + 3 * 2 + 3 * 2 + 3)
    return pl.pallas_call(
        functools.partial(gather_kernel, groups, chunks, window),
        out_shape=jax.ShapeDtypeStruct((mats, 4, rows, width), pack.dtype),
        in_specs=[pl.BlockSpec(memory_space=pltpu.VMEM)],
        out_specs=pl.BlockSpec(memory_space=pl.ANY),
        scratch_shapes=[
            pltpu.SemaphoreType.DMA,
            pltpu.SemaphoreType.DMA((count,)),
            pltpu.SemaphoreType.DMA((count,)),
        ],
        compiler_params=pltpu.CompilerParams(collective_id=collective_id, has_side_effects=True, vmem_limit_bytes=32 * 2**20),
        name="gather_pack",
    )(pack)


def reduce_kernel(chunks, mats, *refs):
    grads, small_ref, ffn_ref = refs[:mats], refs[mats], refs[mats + 1]
    (out_ref, small_out_ref, ffn_out_ref, ffn_z, ffn_piece, mine, from_c, from_x1, from_y1, from_x2, from_y2, from_z, piece,
     s_send, s_c, s_x, s_y, s_z, local_sem, send_sem, recv_sem, small_send, small_recv) = refs[mats + 2 :]
    p, t = lax.axis_index("dp"), lax.axis_index("tensor")
    half = grads[0].shape[1] // 2
    n = half // chunks
    per = mats // 4
    core, cx, cy = lax.rem(p, 2), lax.rem(p // 2, 2), p // 4
    chip = p // 2
    zs = [jnp.bitwise_xor(t, j) for j in (1, 2, 3)]
    to_c, to_x, to_y = [(jnp.bitwise_xor(p, b), t) for b in (1, 2, 4)]
    greet([to_c, to_x, to_y] + [(p, z) for z in zs])
    count = [0]
    copies = []

    def send(src, dst, device):
        i = count[0]
        count[0] += 1
        copy = pltpu.make_async_remote_copy(
            src, dst, send_sem.at[i], recv_sem.at[i], device_id=device, device_id_type=MESH
        )
        copy.start()
        copies.append(copy)
        return copy

    small_count = [0]

    def send_small(src, dst, device):
        i = small_count[0]
        small_count[0] += 1
        copy = pltpu.make_async_remote_copy(
            src, dst, small_send.at[i], small_recv.at[i], device_id=device, device_id_type=MESH
        )
        copy.start()
        return copy

    nx, ny = 1 - cx, 1 - cy
    c_in, x1, y1, x2, y2, z_in, gx, gy, gxd, gyd, last = {}, {}, {}, {}, {}, {}, {}, {}, {}, {}, []
    local = {}
    cut = lambda c: pl.ds(c * n, n)
    own_cut = lambda c: pl.ds(pl.multiple_of(core * half + c * n, 16), n)
    other_cut = lambda c: pl.ds(pl.multiple_of((1 - core) * half + c * n, 16), n)
    owned = lambda q: pl.ds(q * per, per)
    for c in range(chunks):
        c_in[c], local[c] = [], []
        for a in range(mats):
            c_in[c].append(send(grads[a].at[:, other_cut(c)], from_c.at[a, :, cut(c)], to_c))
            copy = pltpu.make_async_copy(
                grads[a].at[:, own_cut(c)], mine.at[a, :, cut(c)], local_sem.at[c * mats + a]
            )
            copy.start()
            local[c].append(copy)
    small = send_small(small_ref, s_c, to_c)
    f_in = [send(ffn_ref.at[:, zs[j]], ffn_z.at[j], (p, zs[j])) for j in range(3)]
    f_way = {}

    def ffn_total():
        for j in range(3):
            f_in[j].wait_recv()
        for i in range(2):
            total = ffn_ref[i, t].astype(F32)
            for j in range(3):
                total = total + ffn_z[j, i].astype(F32)
            ffn_piece[p, i] = total.astype(ffn_piece.dtype)
        ref = ffn_piece.at[p]
        f_way["x"] = send(ref, ref, to_x)
        f_way["y"] = send(ref, ref, to_y)
        last.append(send(ref, ref, to_c))

    def ffn_far():
        f_way["x"].wait_recv()
        ref = ffn_piece.at[to_x[0]]
        f_way["yd"] = send(ref.at[0], ref.at[0], to_y)
        last.append(send(ref, ref, to_c))
        f_way["y"].wait_recv()
        ref = ffn_piece.at[to_y[0]]
        f_way["xd"] = send(ref.at[1], ref.at[1], to_x)
        last.append(send(ref, ref, to_c))

    def ffn_end():
        f_way["xd"].wait_recv()
        f_way["yd"].wait_recv()
        ref = ffn_piece.at[jnp.bitwise_xor(p, 6)]
        last.append(send(ref, ref, to_c))

    def add(dst, src):
        dst[...] = (dst[...].astype(F32) + src[...].astype(F32)).astype(dst.dtype)

    def stage_c(c):
        for a in range(mats):
            c_in[c][a].wait_recv()
            local[c][a].wait()
            for b in range(4):
                add(mine.at[a, b, cut(c)], from_c.at[a, b, cut(c)])
        x1[c] = [send(mine.at[owned(q * 2 + nx), 0:2, cut(c)], from_x1.at[q, :, :, cut(c)], to_x) for q in range(2)]
        y1[c] = [send(mine.at[owned(ny * 2 + q), 2:4, cut(c)], from_y1.at[q, :, :, cut(c)], to_y) for q in range(2)]

    def stage_xy(c):
        for q in range(2):
            x1[c][q].wait_recv()
            for i in range(per):
                for b in range(2):
                    add(mine.at[(q * 2 + cx) * per + i, b, cut(c)], from_x1.at[q, i, b, cut(c)])
        x2[c] = send(mine.at[owned(ny * 2 + cx), 0:2, cut(c)], from_x2.at[:, :, cut(c)], to_y)
        for q in range(2):
            y1[c][q].wait_recv()
            for i in range(per):
                for b in range(2):
                    add(mine.at[(cy * 2 + q) * per + i, 2 + b, cut(c)], from_y1.at[q, i, b, cut(c)])
        y2[c] = send(mine.at[owned(cy * 2 + nx), 2:4, cut(c)], from_y2.at[:, :, cut(c)], to_x)

    def stage_z(c):
        x2[c].wait_recv()
        for i in range(per):
            for b in range(2):
                add(mine.at[chip * per + i, b, cut(c)], from_x2.at[i, b, cut(c)])
        y2[c].wait_recv()
        for i in range(per):
            for b in range(2):
                add(mine.at[chip * per + i, 2 + b, cut(c)], from_y2.at[i, b, cut(c)])
        z_in[c] = [
            send(mine.at[owned(chip), zs[j], cut(c)], from_z.at[j, :, cut(c)], (p, zs[j])) for j in range(3)
        ]

    def stage_out(c):
        for j in range(3):
            z_in[c][j].wait_recv()
        for i in range(per):
            total = mine[chip * per + i, t, cut(c), :].astype(F32)
            for j in range(3):
                total = total + from_z[j, i, cut(c), :].astype(F32)
            piece[chip * per + i, own_cut(c), :] = total.astype(piece.dtype)
        ref = piece.at[owned(chip), own_cut(c)]
        gx[c] = send(ref, ref, to_x)
        gy[c] = send(ref, ref, to_y)
        last.append(send(ref, ref, to_c))

    def stage_far(c):
        gx[c].wait_recv()
        ref = piece.at[owned(cy * 2 + nx), own_cut(c)]
        gyd[c] = send(ref.at[: per // 2], ref.at[: per // 2], to_y)
        last.append(send(ref, ref, to_c))
        gy[c].wait_recv()
        ref = piece.at[owned(ny * 2 + cx), own_cut(c)]
        gxd[c] = send(ref.at[per // 2 :], ref.at[per // 2 :], to_x)
        last.append(send(ref, ref, to_c))

    def stage_end(c):
        gxd[c].wait_recv()
        gyd[c].wait_recv()
        ref = piece.at[owned(ny * 2 + nx), own_cut(c)]
        last.append(send(ref, ref, to_c))

    stages = (stage_c, stage_xy, stage_z, stage_out, stage_far, stage_end)
    for step in range(chunks + len(stages) - 1):
        for k in reversed(range(len(stages))):
            if 0 <= step - k < chunks:
                stages[k](step - k)
        if step == 0:
            small.wait()
            s_send[0] = small_ref[...] + s_c[...]
            small = send_small(s_send.at[0], s_x, to_x)
        elif step == 1:
            small.wait()
            s_send[1] = s_send[0] + s_x[...]
            small = send_small(s_send.at[1], s_y, to_y)
        elif step == 2:
            small.wait()
            s_send[2] = s_send[1] + s_y[...]
            s_z[t] = s_send[2]
            small = [send_small(s_send.at[2], s_z.at[t], (p, z)) for z in zs]
            ffn_total()
        elif step == 4:
            ffn_far()
        elif step == 5:
            ffn_end()
    for copy in small:
        copy.wait()
    small_out_ref[...] = (s_z[0] + s_z[1]) + (s_z[2] + s_z[3])
    for copy in last:
        copy.wait_recv()
    for copy in copies:
        copy.wait_send()
    for a in range(mats):
        out_ref[a] = piece[a].astype(out_ref.dtype)
    part = ffn_piece.shape[2]
    for a in range(8):
        for i in range(2):
            ffn_out_ref[i, pl.ds(a * part, part), :] = ffn_piece[a, i].astype(ffn_out_ref.dtype)


def reduce_pack(grads, small, ffn, collective_id, chunks=3):
    mats = len(grads)
    tensor, rows, width = grads[0].shape
    half, per = rows // 2, mats // 4
    part = ffn.shape[2]
    count = chunks * (mats + 4 + 2 + 3 + 3 + 4 + 1) + 11
    vmem = pl.BlockSpec(memory_space=pltpu.VMEM)
    buf = lambda *s: pltpu.VMEM(s + (half, width), BF16)
    sb = lambda *s: pltpu.VMEM(s + small.shape, F32)
    return pl.pallas_call(
        functools.partial(reduce_kernel, chunks, mats),
        out_shape=(
            jax.ShapeDtypeStruct((mats, rows, width), F32),
            jax.ShapeDtypeStruct(small.shape, F32),
            jax.ShapeDtypeStruct((2, 8 * part, width), F32),
        ),
        in_specs=[pl.BlockSpec(memory_space=pl.ANY)] * mats + [vmem, vmem],
        out_specs=(vmem, vmem, vmem),
        scratch_shapes=[
            pltpu.VMEM((3, 2, part, width), BF16),
            pltpu.VMEM((8, 2, part, width), BF16),
            buf(mats, 4), buf(mats, 4), buf(2, per, 2), buf(2, per, 2), buf(per, 2), buf(per, 2), buf(3, per),
            pltpu.VMEM((mats, rows, width), BF16),
            sb(3), sb(), sb(), sb(), sb(4),
            pltpu.SemaphoreType.DMA((chunks * mats,)),
            pltpu.SemaphoreType.DMA((count,)),
            pltpu.SemaphoreType.DMA((count,)),
            pltpu.SemaphoreType.DMA((6,)),
            pltpu.SemaphoreType.DMA((6,)),
        ],
        compiler_params=pltpu.CompilerParams(
            collective_id=collective_id, has_side_effects=True, vmem_limit_bytes=48 * 2**20
        ),
        cost_estimate=pl.CostEstimate(flops=int(1e9), bytes_accessed=int(60e6), transcendentals=0),
        name="reduce_pack",
    )(*grads, small, ffn)


def flip(x, bit):
    return lax.ppermute(x, "dp", [(i, i ^ bit) for i in range(lax.axis_size("dp"))])


def take(x, i, axis):
    return lax.dynamic_index_in_dim(x, i, axis, keepdims=False)


def halve_core(grad):
    tensor = lax.axis_size("tensor")
    core = lax.axis_index("dp") % 2
    grad = grad.reshape(2, 2, 2, 2, tensor, grad.shape[1] // (8 * tensor), grad.shape[2])
    return take(grad, core, 3) + flip(take(grad, 1 - core, 3), 1)


def halve_plane(grad):
    p = lax.axis_index("dp")
    cx, cy = p // 2 % 2, p // 4
    cut = grad.shape[3] // 2
    left, right = grad[:, :, :, :cut], grad[:, :, :, cut:]
    left_in, right_in = flip(take(left, 1 - cx, 2), 2), flip(take(right, 1 - cy, 1), 4)
    return take(left, cx, 2) + left_in, take(right, cy, 1) + right_in


def halve_rest(halves):
    left, right = halves
    p = lax.axis_index("dp")
    cx, cy = p // 2 % 2, p // 4
    left_in, right_in = flip(take(left, 1 - cy, 1), 4), flip(take(right, 1 - cx, 1), 2)
    return jnp.concatenate([take(left, cy, 1) + left_in, take(right, cx, 1) + right_in], axis=1)


def gather_rows(shard):
    mats, rows, width = shard.shape
    dp, tensor = lax.axis_size("dp"), lax.axis_size("tensor")
    if own_kernels():
        return gather_pack(shard, 0).reshape(mats, tensor * rows, width)
    piece = mats * rows // dp
    mine = lax.dynamic_slice_in_dim(
        shard.reshape(mats * rows, width), lax.axis_index("dp") * piece, piece, 0
    )
    full = lax.all_gather(mine, ("dp", "tensor"), axis=0, tiled=True)
    full = full.reshape(mats, dp // mats, tensor, piece, width).transpose(0, 2, 1, 3, 4)
    return full.reshape(mats, tensor * rows, width)


def own_kernels():
    return (lax.axis_size("dp"), lax.axis_size("tensor")) == (8, 4)


def reduce_rows(grads, small, ffn):
    mats = len(grads)
    all_rows, width = grads[0].shape
    dp, tensor = lax.axis_size("dp"), lax.axis_size("tensor")
    rows = all_rows // tensor
    if own_kernels():
        return reduce_pack([g.reshape(tensor, rows, width) for g in grads], small, ffn, 1)
    piece = mats * rows // dp
    grad = jnp.stack(grads).reshape(mats, tensor, dp // mats, piece, width).transpose(0, 2, 1, 3, 4)
    mine = lax.psum_scatter(
        grad.reshape(dp * tensor * piece, width), ("dp", "tensor"), scatter_dimension=0, tiled=True
    )
    total = lax.all_gather(mine, "dp", axis=0, tiled=True).reshape(mats, rows, width).astype(F32)
    ffn = lax.psum_scatter(ffn, ("dp", "tensor"), scatter_dimension=1, tiled=True)
    ffn = lax.all_gather(ffn, "dp", axis=1, tiled=True).astype(F32)
    return total, lax.psum(small, ("dp", "tensor")), ffn


def per_device(
    inputs, encoded, cotangent, tgt_seg, src_seg, self_qkv, self_out, cross_q, cross_kv, cross_out, ffn_up, ffn_down, gains, shifts
):
    me = lax.axis_index("tensor")
    t_ids = lax.dynamic_index_in_dim(tgt_seg, me, 0, keepdims=False)
    s_ids = lax.dynamic_index_in_dim(src_seg, me, 0, keepdims=False)
    pack = jnp.concatenate(
        [
            self_qkv.transpose(0, 2, 1),
            self_out[None],
            cross_q.T[None],
            cross_kv.transpose(0, 2, 1),
            cross_out[None],
        ],
        axis=0,
    )
    pack = gather_rows(pack)
    hidden = ffn_down.shape[0]
    width = inputs.shape[1]
    dp, tensor = lax.axis_size("dp"), lax.axis_size("tensor")
    piece = hidden // dp
    start = lax.axis_index("dp") * piece
    ffn_w = jnp.stack([ffn_up.T, ffn_down], axis=0)
    ffn_w = lax.dynamic_slice_in_dim(ffn_w, start, piece, 1)
    ffn_w = lax.all_gather(ffn_w, ("dp", "tensor"), axis=1, tiled=True)
    w = dict(qkv=pack[0:3], out=pack[3], cq=pack[4], ckv=pack[5:7], cout=pack[7], ffn=ffn_w)
    halvings = (halve_core, halve_plane, halve_rest) if own_kernels() else (lambda g: g,) * 3
    layer_out, grad_x, grad_e, grads, grad_gains, grad_shifts = local_step(
        inputs, encoded, cotangent, t_ids, s_ids, w, gains, shifts, halvings
    )
    small = jnp.concatenate([grad_gains, grad_shifts, jnp.zeros((2, width), F32)], axis=0)
    total, small, g_ffn = reduce_rows(
        [*grads["qkv"], grads["out"], grads["cq"], *grads["ckv"], grads["cout"]], small, grads["ffn"]
    )
    return (
        layer_out,
        grad_x,
        grad_e,
        total[0:3].transpose(0, 2, 1),
        total[3],
        total[4].T,
        total[5:7].transpose(0, 2, 1),
        total[7],
        g_ffn[0].T,
        g_ffn[1],
        small[0:3],
        small[3:6],
    )


def solution(mesh):
    rows = P(("dp", "tensor"), None)
    in_specs = (
        rows, rows, rows, P("dp", None), P("dp", None),
        P(None, None, "tensor"), P("tensor", None), P(None, "tensor"), P(None, None, "tensor"), P("tensor", None),
        P(None, "tensor"), P("tensor", None), P(), P(),
    )
    out_specs = (
        rows, rows, rows,
        P(None, None, "tensor"), P("tensor", None), P(None, "tensor"), P(None, None, "tensor"), P("tensor", None),
        P(None, "tensor"), P("tensor", None), P(), P(),
    )
    return jax.shard_map(per_device, mesh=mesh, in_specs=in_specs, out_specs=out_specs, check_vma=False)
```

```python
import functools
import jax, jax.numpy as jnp
from jax import lax
from jax.sharding import PartitionSpec as P
from jax.experimental import pallas as pl
from jax.experimental.pallas import tpu as pltpu

HDIM = 64
LANES = 128
MASKED = -1e30
EPSILON = 1e-5
F32 = jnp.float32
BF16 = jnp.bfloat16
NT = (((1,), (1,)), ((), ()))
TN = (((0,), (0,)), ((), ()))
NN = (((1,), (0,)), ((), ()))


def dot(a, b, dims):
    return lax.dot_general(a, b, dims, preferred_element_type=F32)


def by_head(x):
    first = lax.broadcasted_iota(jnp.int32, x.shape, 1) < HDIM
    zero = jnp.zeros_like(x)
    return jnp.concatenate([jnp.where(first, x, zero), jnp.where(first, zero, x)], axis=0)


def later_keys(bk, bq, offset):
    row = lax.broadcasted_iota(jnp.int32, (bk, bq), 1)
    col = lax.broadcasted_iota(jnp.int32, (bk, bq), 0)
    late = col > row + offset
    return jnp.concatenate([late, late], axis=1)


def stacked(x):
    n = x.shape[1] // 2
    return jnp.concatenate([x[:, :n], x[:, n:]], axis=0)


def attend_kernel(causal, block, per, lo_ref, hi_ref, q_ref, k_ref, v_ref, fq_ref, fk_ref, o_ref, lse_ref, scores, acc):
    n = q_ref.shape[0]
    for i in range(n // block):
        rows = pl.ds(i * block, block)
        fq = fq_ref[rows, :]
        fq = jnp.concatenate([fq, fq], axis=0)
        qs = [
            jnp.concatenate(
                [by_head(q_ref[rows, h * LANES : (h + 1) * LANES] * jnp.asarray(HDIM ** -0.5, BF16)), fq], axis=1
            )
            for h in range(per)
        ]

        def score(j, tops, diagonal=False):
            keys = pl.ds(pl.multiple_of(j * block, block), block)
            fk = fk_ref[keys, :]
            out = []
            for h in range(per):
                k = k_ref[keys, h * LANES : (h + 1) * LANES]
                s = dot(jnp.concatenate([k, fk], axis=1), qs[h], NT)
                if diagonal:
                    s = jnp.where(later_keys(block, block, 0), MASKED, s)
                scores[h, keys, :] = s
                out.append(jnp.maximum(tops[h], jnp.max(s, axis=0, keepdims=True)))
            return tuple(out)

        def mix(j, totals, tops):
            keys = pl.ds(pl.multiple_of(j * block, block), block)
            out = []
            for h in range(per):
                p = jnp.exp(scores[h, keys, :] - tops[h])
                out.append(totals[h] + jnp.sum(p, axis=0, keepdims=True))
                v = by_head(v_ref[keys, h * LANES : (h + 1) * LANES])
                acc[h] += dot(stacked(p.astype(BF16)), v, TN)
            return tuple(out)

        tops = tuple(jnp.full((1, 2 * block), MASKED, F32) for _ in range(per))
        totals = tuple(jnp.zeros((1, 2 * block), F32) for _ in range(per))
        acc[...] = jnp.zeros_like(acc)
        if causal:
            tops = score(i, tops, True)
            tops = lax.fori_loop(lo_ref[i], i, score, tops)
            totals = lax.fori_loop(lo_ref[i], i + 1, functools.partial(mix, tops=tops), totals)
        else:
            tops = lax.fori_loop(lo_ref[i], hi_ref[i], score, tops)
            totals = lax.fori_loop(lo_ref[i], hi_ref[i], functools.partial(mix, tops=tops), totals)
        for h in range(per):
            inverse = 1.0 / totals[h]
            inverse = jnp.concatenate(
                [jnp.broadcast_to(inverse[:, side * block : (side + 1) * block], (HDIM, block)) for side in range(2)], axis=0
            )
            o_ref[rows, h * LANES : (h + 1) * LANES] = (acc[h] * inverse.T).astype(BF16)
            lse_ref[h, i] = tops[h] + jnp.log(totals[h])


def attend_back_kernel(
    causal, block, per, lo_ref, hi_ref, q_ref, k_ref, v_ref, fq_ref, fk_ref, g_ref, o_ref, lse_ref,
    dq_ref, dk_ref, dv_ref, dq_acc, dk_acc, dv_acc, qs, gs, delta,
):
    n = q_ref.shape[0]
    m = k_ref.shape[0]
    pick = lax.broadcasted_iota(jnp.int32, (8, LANES), 1) // HDIM == lax.broadcasted_iota(jnp.int32, (8, LANES), 0)
    pick = pick.astype(BF16)
    dq_acc[...] = jnp.zeros_like(dq_acc)
    for h in range(per):
        lanes = slice(h * LANES, (h + 1) * LANES)
        for i in range(n // block):
            rows = pl.ds(i * block, block)
            fq = fq_ref[rows, :]
            qs[h, i, :, :LANES] = by_head(q_ref[rows, lanes] * jnp.asarray(HDIM ** -0.5, BF16))
            qs[h, i, :, LANES:] = jnp.concatenate([fq, fq], axis=0)
            gs[h, i] = by_head(g_ref[rows, lanes])
            prod = g_ref[rows, lanes].astype(F32) * o_ref[rows, lanes].astype(F32)
            high = prod.astype(BF16)
            rest = (prod - high.astype(F32)).astype(BF16)
            sums = dot(pick, high, NT) + dot(pick, rest, NT)
            delta[h, i] = jnp.concatenate([sums[0:1], sums[1:2]], axis=1)
    for j in range(m // block):
        keys = pl.ds(j * block, block)
        fk = fk_ref[keys, :]
        dk_acc[...] = jnp.zeros_like(dk_acc)
        dv_acc[...] = jnp.zeros_like(dv_acc)

        def step(i, _, diagonal=False):
            rows = pl.ds(pl.multiple_of(i * block, block), block)
            ss, dps, ps, dss = [], [], [], []
            for h in range(per):
                lanes = slice(h * LANES, (h + 1) * LANES)
                ss.append(dot(jnp.concatenate([k_ref[keys, lanes], fk], axis=1), qs[h, i], NT))
                dps.append(dot(v_ref[keys, lanes], gs[h, i], NT))
            for h in range(per):
                s = ss[h]
                if diagonal:
                    s = jnp.where(later_keys(block, block, 0), MASKED, s)
                p = jnp.exp(s - lse_ref[h, i])
                ps.append(p.astype(BF16))
                dss.append((p * (dps[h] - delta[h, i])).astype(BF16))
            adds = []
            for h in range(per):
                lanes = slice(h * LANES, (h + 1) * LANES)
                adds.append((dot(ps[h], gs[h, i], NN), dot(dss[h], qs[h, i, :, :LANES], NN), dot(stacked(dss[h]), by_head(k_ref[keys, lanes]), TN)))
            for h in range(per):
                lanes = slice(h * LANES, (h + 1) * LANES)
                dv_acc[h] += adds[h][0]
                dk_acc[h] += adds[h][1]
                dq_acc[rows, lanes] += adds[h][2]
            return 0

        if causal:
            step(j, 0, True)
            lax.fori_loop(j + 1, hi_ref[j], step, 0)
        else:
            lax.fori_loop(lo_ref[j], hi_ref[j], step, 0)
        for h in range(per):
            dk_ref[keys, h * LANES : (h + 1) * LANES] = dk_acc[h].astype(BF16)
            dv_ref[keys, h * LANES : (h + 1) * LANES] = dv_acc[h].astype(BF16)
    dq_ref[...] = (dq_acc[...] * HDIM ** -0.5).astype(BF16)


def block_range(own, other, block, other_block):
    own = own.reshape(-1, block)
    lo = jnp.sum((other[None, :] < own[:, :1]).astype(jnp.int32), axis=1) // other_block
    hi = jnp.sum((other[None, :] <= own[:, -1:]).astype(jnp.int32), axis=1)
    return lo, (hi + other_block - 1) // other_block


def seg_features(q_ids, k_ids):
    lanes = jnp.arange(LANES, dtype=jnp.int32)[None, :]
    fq = jnp.where((lanes < 5) & (q_ids[:, None] != lanes), MASKED, 0.0).astype(BF16)
    fk = (k_ids[:, None] == lanes).astype(BF16)
    return fq, fk


VMEM_LIMIT = 56 * 2**20
FWD_PER = 3
BWD_PER = 3


def attend(q, k, v, q_ids, k_ids, fq, fk, causal, block=256, per=FWD_PER):
    n, width = q.shape
    m = k.shape[0]
    lo, hi = block_range(q_ids, k_ids, block, block)
    wide = per * LANES
    pairs = width // LANES
    col = lambda rows: pl.BlockSpec((rows, wide), lambda i, *_: (0, i))
    whole = lambda rows: pl.BlockSpec((rows, LANES), lambda i, *_: (0, 0))
    vec = pl.BlockSpec((per, n // block, 1, 2 * block), lambda i, *_: (i, 0, 0, 0))
    return pl.pallas_call(
        functools.partial(attend_kernel, causal, block, per),
        out_shape=(
            jax.ShapeDtypeStruct((n, width), BF16),
            jax.ShapeDtypeStruct((pairs, n // block, 1, 2 * block), F32),
        ),
        grid_spec=pltpu.PrefetchScalarGridSpec(
            num_scalar_prefetch=2,
            grid=(pairs // per,),
            in_specs=[col(n), col(m), col(m), whole(n), whole(m)],
            out_specs=[col(n), vec],
            scratch_shapes=[pltpu.VMEM((per, m, 2 * block), F32), pltpu.VMEM((per, block, LANES), F32)],
        ),
        compiler_params=pltpu.CompilerParams(vmem_limit_bytes=VMEM_LIMIT),
        cost_estimate=pl.CostEstimate(flops=int(8e9), bytes_accessed=int(8e6), transcendentals=int(4e6)),
        name="attend",
    )(lo, hi, q, k, v, fq, fk)


def attend_back(q, k, v, g, out, lse, q_ids, k_ids, fq, fk, causal, block=256, per=BWD_PER):
    n, width = q.shape
    m = k.shape[0]
    lo, hi = block_range(k_ids, q_ids, block, block)
    wide = per * LANES
    pairs = width // LANES
    count = n // block
    col = lambda rows: pl.BlockSpec((rows, wide), lambda i, *_: (0, i))
    whole = lambda rows: pl.BlockSpec((rows, LANES), lambda i, *_: (0, 0))
    vec = pl.BlockSpec((per, count, 1, 2 * block), lambda i, *_: (i, 0, 0, 0))
    return pl.pallas_call(
        functools.partial(attend_back_kernel, causal, block, per),
        out_shape=(
            jax.ShapeDtypeStruct((n, width), BF16),
            jax.ShapeDtypeStruct((m, width), BF16),
            jax.ShapeDtypeStruct((m, width), BF16),
        ),
        grid_spec=pltpu.PrefetchScalarGridSpec(
            num_scalar_prefetch=2,
            grid=(pairs // per,),
            in_specs=[col(n), col(m), col(m), whole(n), whole(m), col(n), col(n), vec],
            out_specs=[col(n), col(m), col(m)],
            scratch_shapes=[
                pltpu.VMEM((n, wide), F32),
                pltpu.VMEM((per, block, LANES), F32),
                pltpu.VMEM((per, block, LANES), F32),
                pltpu.VMEM((per, count, 2 * block, 2 * LANES), BF16),
                pltpu.VMEM((per, count, 2 * block, LANES), BF16),
                pltpu.VMEM((per, count, 1, 2 * block), F32),
            ],
        ),
        compiler_params=pltpu.CompilerParams(vmem_limit_bytes=VMEM_LIMIT),
        cost_estimate=pl.CostEstimate(flops=int(20e9), bytes_accessed=int(12e6), transcendentals=int(4e6)),
        name="attend_back",
    )(lo, hi, q, k, v, fq, fk, g, out, lse)


def norm_forward(summed, gain, shift):
    centred = summed - jnp.mean(summed, axis=-1, keepdims=True)
    inverse = lax.rsqrt(jnp.mean(centred * centred, axis=-1, keepdims=True) + EPSILON)
    normed = centred * inverse
    return normed * gain + shift, normed, inverse


def norm_backward(upstream, normed, inverse, gain):
    scaled = upstream * gain
    first_mean = jnp.mean(scaled, axis=-1, keepdims=True)
    second_mean = jnp.mean(scaled * normed, axis=-1, keepdims=True)
    result = inverse * (scaled - first_mean - normed * second_mean)
    return result, jnp.sum(upstream * normed, axis=0, keepdims=True), jnp.sum(upstream, axis=0, keepdims=True)


CHUNK = 256


def ffn_kernel(
    r2_ref, ct_ref, gains_ref, shifts_ref, w_ref,
    acts_ref, slopes_ref, out_ref, dr3_ref, da3_ref, h2b_ref, gs_ref, h2, a3,
):
    step = pl.program_id(0)
    chunks = r2_ref.shape[0] // CHUNK
    rows_of = lambda c: pl.ds(pl.multiple_of(c * CHUNK, CHUNK), CHUNK)

    @pl.when(step == 0)
    def _():
        def first(c, _):
            rows = rows_of(c)
            h, _, _ = norm_forward(r2_ref[rows, :], gains_ref[1:2, :], shifts_ref[1:2, :])
            h2[rows, :] = h
            h2b_ref[rows, :] = h.astype(BF16)
            a3[rows, :] = jnp.zeros_like(h)
            return 0

        lax.fori_loop(0, chunks, first, 0)

    def main(c, _):
        rows = rows_of(c)
        u = dot(h2b_ref[rows, :], w_ref[0], NT)
        phi = 0.5 * (1.0 + lax.erf(u * (2 ** -0.5)))
        act = (u * phi).astype(BF16)
        acts_ref[rows, :] = act
        slopes_ref[rows, :] = (phi + u * jnp.exp(-0.5 * u * u) * ((2 * jnp.pi) ** -0.5)).astype(BF16)
        a3[rows, :] += dot(act, w_ref[1], NN)
        return 0

    lax.fori_loop(0, chunks, main, 0, unroll=True)

    @pl.when(step == pl.num_programs(0) - 1)
    def _():
        def final(c, carry):
            rows = rows_of(c)
            h, normed, inverse = norm_forward(h2[rows, :] + a3[rows, :], gains_ref[2:3, :], shifts_ref[2:3, :])
            out_ref[rows, :] = h.astype(BF16)
            dr, gg, gs = norm_backward(ct_ref[rows, :].astype(F32), normed, inverse, gains_ref[2:3, :])
            dr3_ref[rows, :] = dr
            da3_ref[rows, :] = dr.astype(BF16)
            return carry[0] + gg, carry[1] + gs

        zero = jnp.zeros((1, r2_ref.shape[1]), F32)
        gg, gs = lax.fori_loop(0, chunks, final, (zero, zero))
        gs_ref[...] = jnp.concatenate([gg, gs], axis=0)


def ffn_back_kernel(
    dr3_ref, da3_ref, h2b_ref, r2_ref, gains_ref, acts_ref, slopes_ref, w_ref,
    g_ref, dr2_ref, da2_ref, gs_ref, du, dh2,
):
    step = pl.program_id(0)
    chunks = dr3_ref.shape[0] // CHUNK
    rows_of = lambda c: pl.ds(pl.multiple_of(c * CHUNK, CHUNK), CHUNK)

    @pl.when(step == 0)
    def _():
        dh2[...] = dr3_ref[...]

    def main(c, _):
        rows = rows_of(c)
        dg = dot(da3_ref[rows, :], w_ref[1], NT)
        d = (slopes_ref[rows, :].astype(F32) * dg).astype(BF16)
        du[rows, :] = d
        dh2[rows, :] += dot(d, w_ref[0], NN)
        return 0

    lax.fori_loop(0, chunks, main, 0, unroll=True)
    g_ref[1] = dot(acts_ref[...], da3_ref[...], TN).astype(BF16)
    g_ref[0] = dot(du[...], h2b_ref[...], TN).astype(BF16)

    @pl.when(step == pl.num_programs(0) - 1)
    def _():
        def final(c, carry):
            rows = rows_of(c)
            r = r2_ref[rows, :]
            _, normed, inverse = norm_forward(r, gains_ref[1:2, :], 0.0)
            dr, gg, gs = norm_backward(dh2[rows, :], normed, inverse, gains_ref[1:2, :])
            dr2_ref[rows, :] = dr
            da2_ref[rows, :] = dr.astype(BF16)
            return carry[0] + gg, carry[1] + gs

        zero = jnp.zeros((1, r2_ref.shape[1]), F32)
        gg, gs = lax.fori_loop(0, chunks, final, (zero, zero))
        gs_ref[...] = jnp.concatenate([gg, gs], axis=0)


FFN_BLOCK = 768


def ffn(r2, ct, gains, shifts, w):
    n, width = r2.shape
    hidden = w.shape[1]
    whole = lambda *s: pl.BlockSpec(s, lambda i: (0,) * len(s))
    wblk = pl.BlockSpec((2, FFN_BLOCK, width), lambda i: (0, i, 0))
    ablk = pl.BlockSpec((n, FFN_BLOCK), lambda i: (0, i))
    return pl.pallas_call(
        ffn_kernel,
        grid=(hidden // FFN_BLOCK,),
        in_specs=[whole(n, width), whole(n, width), whole(3, width), whole(3, width), wblk],
        out_specs=[ablk, ablk, whole(n, width), whole(n, width), whole(n, width), whole(n, width), whole(2, width)],
        out_shape=[
            jax.ShapeDtypeStruct((n, hidden), BF16),
            jax.ShapeDtypeStruct((n, hidden), BF16),
            jax.ShapeDtypeStruct((n, width), BF16),
            jax.ShapeDtypeStruct((n, width), F32),
            jax.ShapeDtypeStruct((n, width), BF16),
            jax.ShapeDtypeStruct((n, width), BF16),
            jax.ShapeDtypeStruct((2, width), F32),
        ],
        scratch_shapes=[pltpu.VMEM((n, width), F32), pltpu.VMEM((n, width), F32)],
        compiler_params=pltpu.CompilerParams(vmem_limit_bytes=VMEM_LIMIT),
        cost_estimate=pl.CostEstimate(flops=4 * n * width * hidden, bytes_accessed=int(30e6), transcendentals=2 * n * hidden),
        name="ffn",
    )(r2, ct, gains, shifts, w)


def ffn_back(dr3, da3, h2b, r2, gains, acts, slopes, w):
    n, width = r2.shape
    hidden = w.shape[1]
    whole = lambda *s: pl.BlockSpec(s, lambda i: (0,) * len(s))
    wblk = pl.BlockSpec((2, FFN_BLOCK, width), lambda i: (0, i, 0))
    ablk = pl.BlockSpec((n, FFN_BLOCK), lambda i: (0, i))
    return pl.pallas_call(
        ffn_back_kernel,
        grid=(hidden // FFN_BLOCK,),
        in_specs=[whole(n, width), whole(n, width), whole(n, width), whole(n, width), whole(3, width), ablk, ablk, wblk],
        out_specs=[wblk, whole(n, width), whole(n, width), whole(2, width)],
        out_shape=[
            jax.ShapeDtypeStruct((2, hidden, width), BF16),
            jax.ShapeDtypeStruct((n, width), F32),
            jax.ShapeDtypeStruct((n, width), BF16),
            jax.ShapeDtypeStruct((2, width), F32),
        ],
        scratch_shapes=[pltpu.VMEM((n, FFN_BLOCK), BF16), pltpu.VMEM((n, width), F32)],
        compiler_params=pltpu.CompilerParams(vmem_limit_bytes=VMEM_LIMIT),
        cost_estimate=pl.CostEstimate(flops=8 * n * width * hidden, bytes_accessed=int(40e6), transcendentals=0),
        name="ffn_back",
    )(dr3, da3, h2b, r2, gains, acts, slopes, w)


def local_step(x, e, ct, t_ids, s_ids, w, gains, shifts, halvings):
    x32 = x.astype(F32)
    q, k, v = [dot(x, w["qkv"][c], NT).astype(BF16) for c in range(3)]
    k2, v2 = [dot(e, w["ckv"][c], NT).astype(BF16) for c in range(2)]
    fq, fk = seg_features(t_ids, t_ids)
    _, fs = seg_features(t_ids, s_ids)
    ctx1, lse1 = attend(q, k, v, t_ids, t_ids, fq, fk, True)
    h1, n1, i1 = norm_forward(x32 + dot(ctx1, w["out"], NN), gains[0], shifts[0])
    h1b = h1.astype(BF16)
    q2 = dot(h1b, w["cq"], NT).astype(BF16)
    ctx2, lse2 = attend(q2, k2, v2, t_ids, s_ids, fq, fs, False)
    r2 = h1 + dot(ctx2, w["cout"], NN)
    acts, slopes, layer_out, dr3, da3, h2b, small3 = ffn(r2, ct, gains, shifts, w["ffn"])
    g_ffn, dr2, da2, small2 = ffn_back(dr3, da3, h2b, r2, gains, acts, slopes, w["ffn"])
    g_ffn = halvings[0](g_ffn)
    g_cout = dot(ctx2, da2, TN).astype(BF16)
    dctx2 = dot(da2, w["cout"], NT).astype(BF16)
    dctx2, g_ffn = lax.optimization_barrier((dctx2, g_ffn))
    g_ffn = halvings[1](g_ffn)
    dq2, dk2, dv2 = attend_back(q2, k2, v2, dctx2, ctx2, lse2, t_ids, s_ids, fq, fs, False)
    dq2, dk2, dv2, g_ffn = lax.optimization_barrier((dq2, dk2, dv2, g_ffn))
    g_ffn = halvings[2](g_ffn)
    g_cq = dot(dq2, h1b, TN).astype(BF16)
    g_ckv = [dot(dk2, e, TN).astype(BF16), dot(dv2, e, TN).astype(BF16)]
    grad_e = (dot(dk2, w["ckv"][0], NN) + dot(dv2, w["ckv"][1], NN)).astype(BF16)
    dh1 = dr2 + dot(dq2, w["cq"], NN)
    dr1, gg1, gs1 = norm_backward(dh1, n1, i1, gains[0])
    da1 = dr1.astype(BF16)
    g_out = dot(ctx1, da1, TN).astype(BF16)
    dctx1 = dot(da1, w["out"], NT).astype(BF16)
    dq, dk, dv = attend_back(q, k, v, dctx1, ctx1, lse1, t_ids, t_ids, fq, fk, True)
    dq, dk, dv, g_ffn = lax.optimization_barrier((dq, dk, dv, g_ffn))
    g_qkv = [dot(d, x, TN).astype(BF16) for d in (dq, dk, dv)]
    grad_x = (dr1 + dot(dq, w["qkv"][0], NN) + dot(dk, w["qkv"][1], NN) + dot(dv, w["qkv"][2], NN)).astype(BF16)
    g_qkv, grad_x, grad_e = lax.optimization_barrier((g_qkv, grad_x, grad_e))
    grads = dict(qkv=g_qkv, out=g_out, cq=g_cq, ckv=g_ckv, cout=g_cout, ffn=g_ffn)
    grad_gains = jnp.concatenate([gg1, small2[0:1], small3[0:1]], axis=0)
    grad_shifts = jnp.concatenate([gs1, small2[1:2], small3[1:2]], axis=0)
    return layer_out, grad_x, grad_e, grads, grad_gains, grad_shifts

MESH = pl.DeviceIdType.MESH

def greet(devices):
    barrier = pltpu.get_barrier_semaphore()
    for device in devices:
        pl.semaphore_signal(barrier, inc=1, device_id=device, device_id_type=MESH)
    pl.semaphore_wait(barrier, len(devices))


def gather_kernel(groups, chunks, window, pack_ref, out_ref, local_sem, send_sem, recv_sem):
    p, t = lax.axis_index("dp"), lax.axis_index("tensor")
    rows = pack_ref.shape[1]
    n = rows // chunks
    zs = [jnp.bitwise_xor(t, j) for j in (1, 2, 3)]
    to_c, to_x, to_y = [(jnp.bitwise_xor(p, b), t) for b in (1, 2, 4)]
    far = jnp.bitwise_xor(p, 6)
    greet([to_c, to_x, to_y] + [(p, z) for z in zs])
    keep = pltpu.make_async_copy(pack_ref, out_ref.at[:, t], local_sem)
    keep.start()
    count = [0]
    copies = []

    def send(src, dst, device):
        i = count[0]
        count[0] += 1
        copy = pltpu.make_async_remote_copy(
            src, dst, send_sem.at[i], recv_sem.at[i], device_id=device, device_id_type=MESH
        )
        copy.start()
        copies.append(copy)
        return copy

    cut = lambda c: pl.ds(c * n, n)
    steps = [(g, c) for g in range(groups) for c in range(chunks)]
    z_in, x_in, y_in, xd_in, yd_in = {}, {}, {}, {}, {}
    last = []

    def start_z(i):
        g, c = steps[i]
        a = g * 8 + p
        for j in range(3):
            z_in[i, j] = send(pack_ref.at[a, cut(c)], out_ref.at[a, t, cut(c)], (p, zs[j]))

    def stage_z(i):
        g, c = steps[i]
        for j in range(3):
            z_in[i, j].wait_recv()
            ref = out_ref.at[g * 8 + p, zs[j], cut(c)]
            x_in[i, j] = send(ref, ref, to_x)
            y_in[i, j] = send(ref, ref, to_y)
            last.append(send(ref, ref, to_c))
        if i + window < len(steps):
            start_z(i + window)

    def stage_xy(i):
        g, c = steps[i]
        for j in range(3):
            x_in[i, j].wait_recv()
            ref = out_ref.at[g * 8 + to_x[0], zs[j]]
            part = ref.at[pl.ds(c * n, n // 2)]
            yd_in[i, j] = send(part, part, to_y)
            part = ref.at[cut(c)]
            last.append(send(part, part, to_c))
            y_in[i, j].wait_recv()
            ref = out_ref.at[g * 8 + to_y[0], zs[j]]
            part = ref.at[pl.ds(c * n + n // 2, n // 2)]
            xd_in[i, j] = send(part, part, to_x)
            part = ref.at[cut(c)]
            last.append(send(part, part, to_c))

    def stage_far(i):
        g, c = steps[i]
        for j in range(3):
            xd_in[i, j].wait_recv()
            yd_in[i, j].wait_recv()
            ref = out_ref.at[g * 8 + far, zs[j], cut(c)]
            last.append(send(ref, ref, to_c))

    for i in range(window):
        start_z(i)
    stages = (stage_z, stage_xy, stage_far)
    for step in range(len(steps) + 2):
        for k in (2, 1, 0):
            if 0 <= step - k < len(steps):
                stages[k](step - k)
    for copy in last:
        copy.wait_recv()
    for copy in copies:
        copy.wait_send()
    keep.wait()


def gather_pack(pack, collective_id, chunks=3, window=1):
    mats, rows, width = pack.shape
    groups = mats // 8
    count = groups * chunks * (3 + 9 + 3 * 2 + 3 * 2 + 3)
    return pl.pallas_call(
        functools.partial(gather_kernel, groups, chunks, window),
        out_shape=jax.ShapeDtypeStruct((mats, 4, rows, width), pack.dtype),
        in_specs=[pl.BlockSpec(memory_space=pltpu.VMEM)],
        out_specs=pl.BlockSpec(memory_space=pl.ANY),
        scratch_shapes=[
            pltpu.SemaphoreType.DMA,
            pltpu.SemaphoreType.DMA((count,)),
            pltpu.SemaphoreType.DMA((count,)),
        ],
        compiler_params=pltpu.CompilerParams(collective_id=collective_id, has_side_effects=True, vmem_limit_bytes=32 * 2**20),
        name="gather_pack",
    )(pack)


def reduce_kernel(chunks, mats, *refs):
    grads, small_ref, ffn_ref = refs[:mats], refs[mats], refs[mats + 1]
    (out_ref, small_out_ref, ffn_out_ref, ffn_z, ffn_piece, mine, from_c, from_x1, from_y1, from_x2, from_y2, from_z, piece,
     s_send, s_c, s_x, s_y, s_z, local_sem, send_sem, recv_sem, small_send, small_recv) = refs[mats + 2 :]
    p, t = lax.axis_index("dp"), lax.axis_index("tensor")
    half = grads[0].shape[1] // 2
    n = half // chunks
    per = mats // 4
    core, cx, cy = lax.rem(p, 2), lax.rem(p // 2, 2), p // 4
    chip = p // 2
    zs = [jnp.bitwise_xor(t, j) for j in (1, 2, 3)]
    to_c, to_x, to_y = [(jnp.bitwise_xor(p, b), t) for b in (1, 2, 4)]
    greet([to_c, to_x, to_y] + [(p, z) for z in zs])
    count = [0]
    copies = []

    def send(src, dst, device):
        i = count[0]
        count[0] += 1
        copy = pltpu.make_async_remote_copy(
            src, dst, send_sem.at[i], recv_sem.at[i], device_id=device, device_id_type=MESH
        )
        copy.start()
        copies.append(copy)
        return copy

    small_count = [0]

    def send_small(src, dst, device):
        i = small_count[0]
        small_count[0] += 1
        copy = pltpu.make_async_remote_copy(
            src, dst, small_send.at[i], small_recv.at[i], device_id=device, device_id_type=MESH
        )
        copy.start()
        return copy

    nx, ny = 1 - cx, 1 - cy
    c_in, x1, y1, x2, y2, z_in, gx, gy, gxd, gyd, last = {}, {}, {}, {}, {}, {}, {}, {}, {}, {}, []
    local = {}
    cut = lambda c: pl.ds(c * n, n)
    own_cut = lambda c: pl.ds(pl.multiple_of(core * half + c * n, 16), n)
    other_cut = lambda c: pl.ds(pl.multiple_of((1 - core) * half + c * n, 16), n)
    owned = lambda q: pl.ds(q * per, per)
    for c in range(chunks):
        c_in[c], local[c] = [], []
        for a in range(mats):
            c_in[c].append(send(grads[a].at[:, other_cut(c)], from_c.at[a, :, cut(c)], to_c))
            copy = pltpu.make_async_copy(
                grads[a].at[:, own_cut(c)], mine.at[a, :, cut(c)], local_sem.at[c * mats + a]
            )
            copy.start()
            local[c].append(copy)
    small = send_small(small_ref, s_c, to_c)
    f_in = [send(ffn_ref.at[:, zs[j]], ffn_z.at[j], (p, zs[j])) for j in range(3)]
    f_way = {}

    def ffn_total():
        for j in range(3):
            f_in[j].wait_recv()
        for i in range(2):
            total = ffn_ref[i, t].astype(F32)
            for j in range(3):
                total = total + ffn_z[j, i].astype(F32)
            ffn_piece[p, i] = total.astype(ffn_piece.dtype)
        ref = ffn_piece.at[p]
        f_way["x"] = send(ref, ref, to_x)
        f_way["y"] = send(ref, ref, to_y)
        last.append(send(ref, ref, to_c))

    def ffn_far():
        f_way["x"].wait_recv()
        ref = ffn_piece.at[to_x[0]]
        f_way["yd"] = send(ref.at[0], ref.at[0], to_y)
        last.append(send(ref, ref, to_c))
        f_way["y"].wait_recv()
        ref = ffn_piece.at[to_y[0]]
        f_way["xd"] = send(ref.at[1], ref.at[1], to_x)
        last.append(send(ref, ref, to_c))

    def ffn_end():
        f_way["xd"].wait_recv()
        f_way["yd"].wait_recv()
        ref = ffn_piece.at[jnp.bitwise_xor(p, 6)]
        last.append(send(ref, ref, to_c))

    def add(dst, src):
        dst[...] = (dst[...].astype(F32) + src[...].astype(F32)).astype(dst.dtype)

    def stage_c(c):
        for a in range(mats):
            c_in[c][a].wait_recv()
            local[c][a].wait()
            for b in range(4):
                add(mine.at[a, b, cut(c)], from_c.at[a, b, cut(c)])
        x1[c] = [send(mine.at[owned(q * 2 + nx), 0:2, cut(c)], from_x1.at[q, :, :, cut(c)], to_x) for q in range(2)]
        y1[c] = [send(mine.at[owned(ny * 2 + q), 2:4, cut(c)], from_y1.at[q, :, :, cut(c)], to_y) for q in range(2)]

    def stage_xy(c):
        for q in range(2):
            x1[c][q].wait_recv()
            for i in range(per):
                for b in range(2):
                    add(mine.at[(q * 2 + cx) * per + i, b, cut(c)], from_x1.at[q, i, b, cut(c)])
        x2[c] = send(mine.at[owned(ny * 2 + cx), 0:2, cut(c)], from_x2.at[:, :, cut(c)], to_y)
        for q in range(2):
            y1[c][q].wait_recv()
            for i in range(per):
                for b in range(2):
                    add(mine.at[(cy * 2 + q) * per + i, 2 + b, cut(c)], from_y1.at[q, i, b, cut(c)])
        y2[c] = send(mine.at[owned(cy * 2 + nx), 2:4, cut(c)], from_y2.at[:, :, cut(c)], to_x)

    def stage_z(c):
        x2[c].wait_recv()
        for i in range(per):
            for b in range(2):
                add(mine.at[chip * per + i, b, cut(c)], from_x2.at[i, b, cut(c)])
        y2[c].wait_recv()
        for i in range(per):
            for b in range(2):
                add(mine.at[chip * per + i, 2 + b, cut(c)], from_y2.at[i, b, cut(c)])
        z_in[c] = [
            send(mine.at[owned(chip), zs[j], cut(c)], from_z.at[j, :, cut(c)], (p, zs[j])) for j in range(3)
        ]

    def stage_out(c):
        for j in range(3):
            z_in[c][j].wait_recv()
        for i in range(per):
            total = mine[chip * per + i, t, cut(c), :].astype(F32)
            for j in range(3):
                total = total + from_z[j, i, cut(c), :].astype(F32)
            piece[chip * per + i, own_cut(c), :] = total.astype(piece.dtype)
        ref = piece.at[owned(chip), own_cut(c)]
        gx[c] = send(ref, ref, to_x)
        gy[c] = send(ref, ref, to_y)
        last.append(send(ref, ref, to_c))

    def stage_far(c):
        gx[c].wait_recv()
        ref = piece.at[owned(cy * 2 + nx), own_cut(c)]
        gyd[c] = send(ref.at[: per // 2], ref.at[: per // 2], to_y)
        last.append(send(ref, ref, to_c))
        gy[c].wait_recv()
        ref = piece.at[owned(ny * 2 + cx), own_cut(c)]
        gxd[c] = send(ref.at[per // 2 :], ref.at[per // 2 :], to_x)
        last.append(send(ref, ref, to_c))

    def stage_end(c):
        gxd[c].wait_recv()
        gyd[c].wait_recv()
        ref = piece.at[owned(ny * 2 + nx), own_cut(c)]
        last.append(send(ref, ref, to_c))

    stages = (stage_c, stage_xy, stage_z, stage_out, stage_far, stage_end)
    for step in range(chunks + len(stages) - 1):
        for k in reversed(range(len(stages))):
            if 0 <= step - k < chunks:
                stages[k](step - k)
        if step == 0:
            small.wait()
            s_send[0] = small_ref[...] + s_c[...]
            small = send_small(s_send.at[0], s_x, to_x)
        elif step == 1:
            small.wait()
            s_send[1] = s_send[0] + s_x[...]
            small = send_small(s_send.at[1], s_y, to_y)
        elif step == 2:
            small.wait()
            s_send[2] = s_send[1] + s_y[...]
            s_z[t] = s_send[2]
            small = [send_small(s_send.at[2], s_z.at[t], (p, z)) for z in zs]
            ffn_total()
        elif step == 4:
            ffn_far()
        elif step == 5:
            ffn_end()
    for copy in small:
        copy.wait()
    small_out_ref[...] = (s_z[0] + s_z[1]) + (s_z[2] + s_z[3])
    for copy in last:
        copy.wait_recv()
    for copy in copies:
        copy.wait_send()
    for a in range(mats):
        out_ref[a] = piece[a].astype(out_ref.dtype)
    part = ffn_piece.shape[2]
    for a in range(8):
        for i in range(2):
            ffn_out_ref[i, pl.ds(a * part, part), :] = ffn_piece[a, i].astype(ffn_out_ref.dtype)


def reduce_pack(grads, small, ffn, collective_id, chunks=3):
    mats = len(grads)
    tensor, rows, width = grads[0].shape
    half, per = rows // 2, mats // 4
    part = ffn.shape[2]
    count = chunks * (mats + 4 + 2 + 3 + 3 + 4 + 1) + 11
    vmem = pl.BlockSpec(memory_space=pltpu.VMEM)
    buf = lambda *s: pltpu.VMEM(s + (half, width), BF16)
    sb = lambda *s: pltpu.VMEM(s + small.shape, F32)
    return pl.pallas_call(
        functools.partial(reduce_kernel, chunks, mats),
        out_shape=(
            jax.ShapeDtypeStruct((mats, rows, width), F32),
            jax.ShapeDtypeStruct(small.shape, F32),
            jax.ShapeDtypeStruct((2, 8 * part, width), F32),
        ),
        in_specs=[pl.BlockSpec(memory_space=pl.ANY)] * mats + [vmem, vmem],
        out_specs=(vmem, vmem, vmem),
        scratch_shapes=[
            pltpu.VMEM((3, 2, part, width), BF16),
            pltpu.VMEM((8, 2, part, width), BF16),
            buf(mats, 4), buf(mats, 4), buf(2, per, 2), buf(2, per, 2), buf(per, 2), buf(per, 2), buf(3, per),
            pltpu.VMEM((mats, rows, width), BF16),
            sb(3), sb(), sb(), sb(), sb(4),
            pltpu.SemaphoreType.DMA((chunks * mats,)),
            pltpu.SemaphoreType.DMA((count,)),
            pltpu.SemaphoreType.DMA((count,)),
            pltpu.SemaphoreType.DMA((6,)),
            pltpu.SemaphoreType.DMA((6,)),
        ],
        compiler_params=pltpu.CompilerParams(
            collective_id=collective_id, has_side_effects=True, vmem_limit_bytes=48 * 2**20
        ),
        cost_estimate=pl.CostEstimate(flops=int(1e9), bytes_accessed=int(60e6), transcendentals=0),
        name="reduce_pack",
    )(*grads, small, ffn)


def flip(x, bit):
    return lax.ppermute(x, "dp", [(i, i ^ bit) for i in range(lax.axis_size("dp"))])


def take(x, i, axis):
    return lax.dynamic_index_in_dim(x, i, axis, keepdims=False)


def halve_core(grad):
    tensor = lax.axis_size("tensor")
    core = lax.axis_index("dp") % 2
    grad = grad.reshape(2, 2, 2, 2, tensor, grad.shape[1] // (8 * tensor), grad.shape[2])
    return take(grad, core, 3) + flip(take(grad, 1 - core, 3), 1)


def halve_plane(grad):
    p = lax.axis_index("dp")
    cx, cy = p // 2 % 2, p // 4
    cut = grad.shape[3] // 2
    left, right = grad[:, :, :, :cut], grad[:, :, :, cut:]
    left_in, right_in = flip(take(left, 1 - cx, 2), 2), flip(take(right, 1 - cy, 1), 4)
    return take(left, cx, 2) + left_in, take(right, cy, 1) + right_in


def halve_rest(halves):
    left, right = halves
    p = lax.axis_index("dp")
    cx, cy = p // 2 % 2, p // 4
    left_in, right_in = flip(take(left, 1 - cy, 1), 4), flip(take(right, 1 - cx, 1), 2)
    return jnp.concatenate([take(left, cy, 1) + left_in, take(right, cx, 1) + right_in], axis=1)


def gather_rows(shard):
    mats, rows, width = shard.shape
    dp, tensor = lax.axis_size("dp"), lax.axis_size("tensor")
    if own_kernels():
        return gather_pack(shard, 0).reshape(mats, tensor * rows, width)
    piece = mats * rows // dp
    mine = lax.dynamic_slice_in_dim(
        shard.reshape(mats * rows, width), lax.axis_index("dp") * piece, piece, 0
    )
    full = lax.all_gather(mine, ("dp", "tensor"), axis=0, tiled=True)
    full = full.reshape(mats, dp // mats, tensor, piece, width).transpose(0, 2, 1, 3, 4)
    return full.reshape(mats, tensor * rows, width)


def own_kernels():
    return (lax.axis_size("dp"), lax.axis_size("tensor")) == (8, 4)


def reduce_rows(grads, small, ffn):
    mats = len(grads)
    all_rows, width = grads[0].shape
    dp, tensor = lax.axis_size("dp"), lax.axis_size("tensor")
    rows = all_rows // tensor
    if own_kernels():
        return reduce_pack([g.reshape(tensor, rows, width) for g in grads], small, ffn, 1)
    piece = mats * rows // dp
    grad = jnp.stack(grads).reshape(mats, tensor, dp // mats, piece, width).transpose(0, 2, 1, 3, 4)
    mine = lax.psum_scatter(
        grad.reshape(dp * tensor * piece, width), ("dp", "tensor"), scatter_dimension=0, tiled=True
    )
    total = lax.all_gather(mine, "dp", axis=0, tiled=True).reshape(mats, rows, width).astype(F32)
    ffn = lax.psum_scatter(ffn, ("dp", "tensor"), scatter_dimension=1, tiled=True)
    ffn = lax.all_gather(ffn, "dp", axis=1, tiled=True).astype(F32)
    return total, lax.psum(small, ("dp", "tensor")), ffn


def per_device(
    inputs, encoded, cotangent, tgt_seg, src_seg, self_qkv, self_out, cross_q, cross_kv, cross_out, ffn_up, ffn_down, gains, shifts
):
    me = lax.axis_index("tensor")
    t_ids = lax.dynamic_index_in_dim(tgt_seg, me, 0, keepdims=False)
    s_ids = lax.dynamic_index_in_dim(src_seg, me, 0, keepdims=False)
    pack = jnp.concatenate(
        [
            self_qkv.transpose(0, 2, 1),
            self_out[None],
            cross_q.T[None],
            cross_kv.transpose(0, 2, 1),
            cross_out[None],
        ],
        axis=0,
    )
    pack = gather_rows(pack)
    hidden = ffn_down.shape[0]
    width = inputs.shape[1]
    dp, tensor = lax.axis_size("dp"), lax.axis_size("tensor")
    piece = hidden // dp
    start = lax.axis_index("dp") * piece
    ffn_w = jnp.stack([ffn_up.T, ffn_down], axis=0)
    ffn_w = lax.dynamic_slice_in_dim(ffn_w, start, piece, 1)
    ffn_w = lax.all_gather(ffn_w, ("dp", "tensor"), axis=1, tiled=True)
    w = dict(qkv=pack[0:3], out=pack[3], cq=pack[4], ckv=pack[5:7], cout=pack[7], ffn=ffn_w)
    halvings = (halve_core, halve_plane, halve_rest) if own_kernels() else (lambda g: g,) * 3
    layer_out, grad_x, grad_e, grads, grad_gains, grad_shifts = local_step(
        inputs, encoded, cotangent, t_ids, s_ids, w, gains, shifts, halvings
    )
    small = jnp.concatenate([grad_gains, grad_shifts, jnp.zeros((2, width), F32)], axis=0)
    total, small, g_ffn = reduce_rows(
        [*grads["qkv"], grads["out"], grads["cq"], *grads["ckv"], grads["cout"]], small, grads["ffn"]
    )
    return (
        layer_out,
        grad_x,
        grad_e,
        total[0:3].transpose(0, 2, 1),
        total[3],
        total[4].T,
        total[5:7].transpose(0, 2, 1),
        total[7],
        g_ffn[0].T,
        g_ffn[1],
        small[0:3],
        small[3:6],
    )


def solution(mesh):
    rows = P(("dp", "tensor"), None)
    in_specs = (
        rows, rows, rows, P("dp", None), P("dp", None),
        P(None, None, "tensor"), P("tensor", None), P(None, "tensor"), P(None, None, "tensor"), P("tensor", None),
        P(None, "tensor"), P("tensor", None), P(), P(),
    )
    out_specs = (
        rows, rows, rows,
        P(None, None, "tensor"), P("tensor", None), P(None, "tensor"), P(None, None, "tensor"), P("tensor", None),
        P(None, "tensor"), P("tensor", None), P(), P(),
    )
    return jax.shard_map(per_device, mesh=mesh, in_specs=in_specs, out_specs=out_specs, check_vma=False)
```

```python
import functools
import jax, jax.numpy as jnp
from jax import lax
from jax.sharding import PartitionSpec as P
from jax.experimental import pallas as pl
from jax.experimental.pallas import tpu as pltpu

HDIM = 64
LANES = 128
MASKED = -1e30
EPSILON = 1e-5
F32 = jnp.float32
BF16 = jnp.bfloat16
NT = (((1,), (1,)), ((), ()))
TN = (((0,), (0,)), ((), ()))
NN = (((1,), (0,)), ((), ()))


def dot(a, b, dims):
    return lax.dot_general(a, b, dims, preferred_element_type=F32)


def by_head(x):
    first = lax.broadcasted_iota(jnp.int32, x.shape, 1) < HDIM
    zero = jnp.zeros_like(x)
    return jnp.concatenate([jnp.where(first, x, zero), jnp.where(first, zero, x)], axis=0)


def later_keys(bk, bq, offset):
    row = lax.broadcasted_iota(jnp.int32, (bk, bq), 1)
    col = lax.broadcasted_iota(jnp.int32, (bk, bq), 0)
    late = col > row + offset
    return jnp.concatenate([late, late], axis=1)


def stacked(x):
    n = x.shape[1] // 2
    return jnp.concatenate([x[:, :n], x[:, n:]], axis=0)


def attend_kernel(causal, block, per, lo_ref, hi_ref, q_ref, k_ref, v_ref, fq_ref, fk_ref, o_ref, lse_ref, scores, acc):
    n = q_ref.shape[0]
    for i in range(n // block):
        rows = pl.ds(i * block, block)
        fq = fq_ref[rows, :]
        fq = jnp.concatenate([fq, fq], axis=0)
        qs = [
            jnp.concatenate(
                [by_head(q_ref[rows, h * LANES : (h + 1) * LANES] * jnp.asarray(HDIM ** -0.5, BF16)), fq], axis=1
            )
            for h in range(per)
        ]

        def score(j, tops, diagonal=False):
            keys = pl.ds(pl.multiple_of(j * block, block), block)
            fk = fk_ref[keys, :]
            out = []
            for h in range(per):
                k = k_ref[keys, h * LANES : (h + 1) * LANES]
                s = dot(jnp.concatenate([k, fk], axis=1), qs[h], NT)
                if diagonal:
                    s = jnp.where(later_keys(block, block, 0), MASKED, s)
                scores[h, keys, :] = s
                out.append(jnp.maximum(tops[h], jnp.max(s, axis=0, keepdims=True)))
            return tuple(out)

        def mix(j, totals, tops):
            keys = pl.ds(pl.multiple_of(j * block, block), block)
            out = []
            for h in range(per):
                p = jnp.exp(scores[h, keys, :] - tops[h])
                out.append(totals[h] + jnp.sum(p, axis=0, keepdims=True))
                v = by_head(v_ref[keys, h * LANES : (h + 1) * LANES])
                acc[h] += dot(stacked(p.astype(BF16)), v, TN)
            return tuple(out)

        tops = tuple(jnp.full((1, 2 * block), MASKED, F32) for _ in range(per))
        totals = tuple(jnp.zeros((1, 2 * block), F32) for _ in range(per))
        acc[...] = jnp.zeros_like(acc)
        if causal:
            tops = score(i, tops, True)
            tops = lax.fori_loop(lo_ref[i], i, score, tops)
            totals = lax.fori_loop(lo_ref[i], i + 1, functools.partial(mix, tops=tops), totals)
        else:
            tops = lax.fori_loop(lo_ref[i], hi_ref[i], score, tops)
            totals = lax.fori_loop(lo_ref[i], hi_ref[i], functools.partial(mix, tops=tops), totals)
        for h in range(per):
            inverse = 1.0 / totals[h]
            inverse = jnp.concatenate(
                [jnp.broadcast_to(inverse[:, side * block : (side + 1) * block], (HDIM, block)) for side in range(2)], axis=0
            )
            o_ref[rows, h * LANES : (h + 1) * LANES] = (acc[h] * inverse.T).astype(BF16)
            lse_ref[h, i] = tops[h] + jnp.log(totals[h])


def attend_back_kernel(
    causal, block, per, lo_ref, hi_ref, q_ref, k_ref, v_ref, fq_ref, fk_ref, g_ref, o_ref, lse_ref,
    dq_ref, dk_ref, dv_ref, dq_acc, dk_acc, dv_acc, qs, gs, delta,
):
    n = q_ref.shape[0]
    m = k_ref.shape[0]
    pick = lax.broadcasted_iota(jnp.int32, (8, LANES), 1) // HDIM == lax.broadcasted_iota(jnp.int32, (8, LANES), 0)
    pick = pick.astype(BF16)
    dq_acc[...] = jnp.zeros_like(dq_acc)
    for h in range(per):
        lanes = slice(h * LANES, (h + 1) * LANES)
        for i in range(n // block):
            rows = pl.ds(i * block, block)
            fq = fq_ref[rows, :]
            qs[h, i, :, :LANES] = by_head(q_ref[rows, lanes] * jnp.asarray(HDIM ** -0.5, BF16))
            qs[h, i, :, LANES:] = jnp.concatenate([fq, fq], axis=0)
            gs[h, i] = by_head(g_ref[rows, lanes])
            prod = g_ref[rows, lanes].astype(F32) * o_ref[rows, lanes].astype(F32)
            high = prod.astype(BF16)
            rest = (prod - high.astype(F32)).astype(BF16)
            sums = dot(pick, high, NT) + dot(pick, rest, NT)
            delta[h, i] = jnp.concatenate([sums[0:1], sums[1:2]], axis=1)
    for j in range(m // block):
        keys = pl.ds(j * block, block)
        fk = fk_ref[keys, :]
        dk_acc[...] = jnp.zeros_like(dk_acc)
        dv_acc[...] = jnp.zeros_like(dv_acc)

        def step(i, _, diagonal=False):
            rows = pl.ds(pl.multiple_of(i * block, block), block)
            ss, dps, ps, dss = [], [], [], []
            for h in range(per):
                lanes = slice(h * LANES, (h + 1) * LANES)
                ss.append(dot(jnp.concatenate([k_ref[keys, lanes], fk], axis=1), qs[h, i], NT))
                dps.append(dot(v_ref[keys, lanes], gs[h, i], NT))
            for h in range(per):
                s = ss[h]
                if diagonal:
                    s = jnp.where(later_keys(block, block, 0), MASKED, s)
                p = jnp.exp(s - lse_ref[h, i])
                ps.append(p.astype(BF16))
                dss.append((p * (dps[h] - delta[h, i])).astype(BF16))
            adds = []
            for h in range(per):
                lanes = slice(h * LANES, (h + 1) * LANES)
                adds.append((dot(ps[h], gs[h, i], NN), dot(dss[h], qs[h, i, :, :LANES], NN), dot(stacked(dss[h]), by_head(k_ref[keys, lanes]), TN)))
            for h in range(per):
                lanes = slice(h * LANES, (h + 1) * LANES)
                dv_acc[h] += adds[h][0]
                dk_acc[h] += adds[h][1]
                dq_acc[rows, lanes] += adds[h][2]
            return 0

        if causal:
            step(j, 0, True)
            lax.fori_loop(j + 1, hi_ref[j], step, 0)
        else:
            lax.fori_loop(lo_ref[j], hi_ref[j], step, 0)
        for h in range(per):
            dk_ref[keys, h * LANES : (h + 1) * LANES] = dk_acc[h].astype(BF16)
            dv_ref[keys, h * LANES : (h + 1) * LANES] = dv_acc[h].astype(BF16)
    dq_ref[...] = (dq_acc[...] * HDIM ** -0.5).astype(BF16)


def block_range(own, other, block, other_block):
    own = own.reshape(-1, block)
    lo = jnp.sum((other[None, :] < own[:, :1]).astype(jnp.int32), axis=1) // other_block
    hi = jnp.sum((other[None, :] <= own[:, -1:]).astype(jnp.int32), axis=1)
    return lo, (hi + other_block - 1) // other_block


def seg_features(q_ids, k_ids):
    lanes = jnp.arange(LANES, dtype=jnp.int32)[None, :]
    fq = jnp.where((lanes < 5) & (q_ids[:, None] != lanes), MASKED, 0.0).astype(BF16)
    fk = (k_ids[:, None] == lanes).astype(BF16)
    return fq, fk


VMEM_LIMIT = 56 * 2**20
FWD_PER = 3
BWD_PER = 3


def attend(q, k, v, q_ids, k_ids, fq, fk, causal, block=256, per=FWD_PER):
    n, width = q.shape
    m = k.shape[0]
    lo, hi = block_range(q_ids, k_ids, block, block)
    wide = per * LANES
    pairs = width // LANES
    col = lambda rows: pl.BlockSpec((rows, wide), lambda i, *_: (0, i))
    whole = lambda rows: pl.BlockSpec((rows, LANES), lambda i, *_: (0, 0))
    vec = pl.BlockSpec((per, n // block, 1, 2 * block), lambda i, *_: (i, 0, 0, 0))
    return pl.pallas_call(
        functools.partial(attend_kernel, causal, block, per),
        out_shape=(
            jax.ShapeDtypeStruct((n, width), BF16),
            jax.ShapeDtypeStruct((pairs, n // block, 1, 2 * block), F32),
        ),
        grid_spec=pltpu.PrefetchScalarGridSpec(
            num_scalar_prefetch=2,
            grid=(pairs // per,),
            in_specs=[col(n), col(m), col(m), whole(n), whole(m)],
            out_specs=[col(n), vec],
            scratch_shapes=[pltpu.VMEM((per, m, 2 * block), F32), pltpu.VMEM((per, block, LANES), F32)],
        ),
        compiler_params=pltpu.CompilerParams(vmem_limit_bytes=VMEM_LIMIT),
        cost_estimate=pl.CostEstimate(flops=int(8e9), bytes_accessed=int(8e6), transcendentals=int(4e6)),
        name="attend",
    )(lo, hi, q, k, v, fq, fk)


def attend_back(q, k, v, g, out, lse, q_ids, k_ids, fq, fk, causal, block=256, per=BWD_PER):
    n, width = q.shape
    m = k.shape[0]
    lo, hi = block_range(k_ids, q_ids, block, block)
    wide = per * LANES
    pairs = width // LANES
    count = n // block
    col = lambda rows: pl.BlockSpec((rows, wide), lambda i, *_: (0, i))
    whole = lambda rows: pl.BlockSpec((rows, LANES), lambda i, *_: (0, 0))
    vec = pl.BlockSpec((per, count, 1, 2 * block), lambda i, *_: (i, 0, 0, 0))
    return pl.pallas_call(
        functools.partial(attend_back_kernel, causal, block, per),
        out_shape=(
            jax.ShapeDtypeStruct((n, width), BF16),
            jax.ShapeDtypeStruct((m, width), BF16),
            jax.ShapeDtypeStruct((m, width), BF16),
        ),
        grid_spec=pltpu.PrefetchScalarGridSpec(
            num_scalar_prefetch=2,
            grid=(pairs // per,),
            in_specs=[col(n), col(m), col(m), whole(n), whole(m), col(n), col(n), vec],
            out_specs=[col(n), col(m), col(m)],
            scratch_shapes=[
                pltpu.VMEM((n, wide), F32),
                pltpu.VMEM((per, block, LANES), F32),
                pltpu.VMEM((per, block, LANES), F32),
                pltpu.VMEM((per, count, 2 * block, 2 * LANES), BF16),
                pltpu.VMEM((per, count, 2 * block, LANES), BF16),
                pltpu.VMEM((per, count, 1, 2 * block), F32),
            ],
        ),
        compiler_params=pltpu.CompilerParams(vmem_limit_bytes=VMEM_LIMIT),
        cost_estimate=pl.CostEstimate(flops=int(20e9), bytes_accessed=int(12e6), transcendentals=int(4e6)),
        name="attend_back",
    )(lo, hi, q, k, v, fq, fk, g, out, lse)


def norm_forward(summed, gain, shift):
    centred = summed - jnp.mean(summed, axis=-1, keepdims=True)
    inverse = lax.rsqrt(jnp.mean(centred * centred, axis=-1, keepdims=True) + EPSILON)
    normed = centred * inverse
    return normed * gain + shift, normed, inverse


def norm_backward(upstream, normed, inverse, gain):
    scaled = upstream * gain
    first_mean = jnp.mean(scaled, axis=-1, keepdims=True)
    second_mean = jnp.mean(scaled * normed, axis=-1, keepdims=True)
    result = inverse * (scaled - first_mean - normed * second_mean)
    return result, jnp.sum(upstream * normed, axis=0, keepdims=True), jnp.sum(upstream, axis=0, keepdims=True)


CHUNK = 256


def ffn_kernel(
    r2_ref, ct_ref, gains_ref, shifts_ref, w_ref,
    acts_ref, slopes_ref, out_ref, dr3_ref, da3_ref, h2b_ref, gs_ref, h2, a3,
):
    step = pl.program_id(0)
    chunks = r2_ref.shape[0] // CHUNK
    rows_of = lambda c: pl.ds(pl.multiple_of(c * CHUNK, CHUNK), CHUNK)

    @pl.when(step == 0)
    def _():
        def first(c, _):
            rows = rows_of(c)
            h, _, _ = norm_forward(r2_ref[rows, :], gains_ref[1:2, :], shifts_ref[1:2, :])
            h2[rows, :] = h
            h2b_ref[rows, :] = h.astype(BF16)
            a3[rows, :] = jnp.zeros_like(h)
            return 0

        lax.fori_loop(0, chunks, first, 0)

    def main(c, _):
        rows = rows_of(c)
        u = dot(h2b_ref[rows, :], w_ref[0], NT)
        phi = 0.5 * (1.0 + lax.erf(u * (2 ** -0.5)))
        act = (u * phi).astype(BF16)
        acts_ref[rows, :] = act
        slopes_ref[rows, :] = (phi + u * jnp.exp(-0.5 * u * u) * ((2 * jnp.pi) ** -0.5)).astype(BF16)
        a3[rows, :] += dot(act, w_ref[1], NN)
        return 0

    lax.fori_loop(0, chunks, main, 0, unroll=True)

    @pl.when(step == pl.num_programs(0) - 1)
    def _():
        def final(c, carry):
            rows = rows_of(c)
            h, normed, inverse = norm_forward(h2[rows, :] + a3[rows, :], gains_ref[2:3, :], shifts_ref[2:3, :])
            out_ref[rows, :] = h.astype(BF16)
            dr, gg, gs = norm_backward(ct_ref[rows, :].astype(F32), normed, inverse, gains_ref[2:3, :])
            dr3_ref[rows, :] = dr
            da3_ref[rows, :] = dr.astype(BF16)
            return carry[0] + gg, carry[1] + gs

        zero = jnp.zeros((1, r2_ref.shape[1]), F32)
        gg, gs = lax.fori_loop(0, chunks, final, (zero, zero))
        gs_ref[...] = jnp.concatenate([gg, gs], axis=0)


def ffn_back_kernel(
    dr3_ref, da3_ref, h2b_ref, r2_ref, gains_ref, acts_ref, slopes_ref, w_ref,
    g_ref, dr2_ref, da2_ref, gs_ref, du, dh2,
):
    step = pl.program_id(0)
    chunks = dr3_ref.shape[0] // CHUNK
    rows_of = lambda c: pl.ds(pl.multiple_of(c * CHUNK, CHUNK), CHUNK)

    @pl.when(step == 0)
    def _():
        dh2[...] = dr3_ref[...]

    def main(c, _):
        rows = rows_of(c)
        dg = dot(da3_ref[rows, :], w_ref[1], NT)
        d = (slopes_ref[rows, :].astype(F32) * dg).astype(BF16)
        du[rows, :] = d
        dh2[rows, :] += dot(d, w_ref[0], NN)
        return 0

    lax.fori_loop(0, chunks, main, 0, unroll=True)
    g_ref[1] = dot(acts_ref[...], da3_ref[...], TN).astype(BF16)
    g_ref[0] = dot(du[...], h2b_ref[...], TN).astype(BF16)

    @pl.when(step == pl.num_programs(0) - 1)
    def _():
        def final(c, carry):
            rows = rows_of(c)
            r = r2_ref[rows, :]
            _, normed, inverse = norm_forward(r, gains_ref[1:2, :], 0.0)
            dr, gg, gs = norm_backward(dh2[rows, :], normed, inverse, gains_ref[1:2, :])
            dr2_ref[rows, :] = dr
            da2_ref[rows, :] = dr.astype(BF16)
            return carry[0] + gg, carry[1] + gs

        zero = jnp.zeros((1, r2_ref.shape[1]), F32)
        gg, gs = lax.fori_loop(0, chunks, final, (zero, zero))
        gs_ref[...] = jnp.concatenate([gg, gs], axis=0)


FFN_BLOCK = 768


def ffn(r2, ct, gains, shifts, w):
    n, width = r2.shape
    hidden = w.shape[1]
    whole = lambda *s: pl.BlockSpec(s, lambda i: (0,) * len(s))
    wblk = pl.BlockSpec((2, FFN_BLOCK, width), lambda i: (0, i, 0))
    ablk = pl.BlockSpec((n, FFN_BLOCK), lambda i: (0, i))
    return pl.pallas_call(
        ffn_kernel,
        grid=(hidden // FFN_BLOCK,),
        in_specs=[whole(n, width), whole(n, width), whole(3, width), whole(3, width), wblk],
        out_specs=[ablk, ablk, whole(n, width), whole(n, width), whole(n, width), whole(n, width), whole(2, width)],
        out_shape=[
            jax.ShapeDtypeStruct((n, hidden), BF16),
            jax.ShapeDtypeStruct((n, hidden), BF16),
            jax.ShapeDtypeStruct((n, width), BF16),
            jax.ShapeDtypeStruct((n, width), F32),
            jax.ShapeDtypeStruct((n, width), BF16),
            jax.ShapeDtypeStruct((n, width), BF16),
            jax.ShapeDtypeStruct((2, width), F32),
        ],
        scratch_shapes=[pltpu.VMEM((n, width), F32), pltpu.VMEM((n, width), F32)],
        compiler_params=pltpu.CompilerParams(vmem_limit_bytes=VMEM_LIMIT),
        cost_estimate=pl.CostEstimate(flops=4 * n * width * hidden, bytes_accessed=int(30e6), transcendentals=2 * n * hidden),
        name="ffn",
    )(r2, ct, gains, shifts, w)


def ffn_back(dr3, da3, h2b, r2, gains, acts, slopes, w):
    n, width = r2.shape
    hidden = w.shape[1]
    whole = lambda *s: pl.BlockSpec(s, lambda i: (0,) * len(s))
    wblk = pl.BlockSpec((2, FFN_BLOCK, width), lambda i: (0, i, 0))
    ablk = pl.BlockSpec((n, FFN_BLOCK), lambda i: (0, i))
    return pl.pallas_call(
        ffn_back_kernel,
        grid=(hidden // FFN_BLOCK,),
        in_specs=[whole(n, width), whole(n, width), whole(n, width), whole(n, width), whole(3, width), ablk, ablk, wblk],
        out_specs=[wblk, whole(n, width), whole(n, width), whole(2, width)],
        out_shape=[
            jax.ShapeDtypeStruct((2, hidden, width), BF16),
            jax.ShapeDtypeStruct((n, width), F32),
            jax.ShapeDtypeStruct((n, width), BF16),
            jax.ShapeDtypeStruct((2, width), F32),
        ],
        scratch_shapes=[pltpu.VMEM((n, FFN_BLOCK), BF16), pltpu.VMEM((n, width), F32)],
        compiler_params=pltpu.CompilerParams(vmem_limit_bytes=VMEM_LIMIT),
        cost_estimate=pl.CostEstimate(flops=8 * n * width * hidden, bytes_accessed=int(40e6), transcendentals=0),
        name="ffn_back",
    )(dr3, da3, h2b, r2, gains, acts, slopes, w)


def local_step(x, e, ct, t_ids, s_ids, w, gains, shifts, halvings):
    x32 = x.astype(F32)
    q, k, v = [dot(x, w["qkv"][c], NT).astype(BF16) for c in range(3)]
    k2, v2 = [dot(e, w["ckv"][c], NT).astype(BF16) for c in range(2)]
    fq, fk = seg_features(t_ids, t_ids)
    _, fs = seg_features(t_ids, s_ids)
    ctx1, lse1 = attend(q, k, v, t_ids, t_ids, fq, fk, True)
    h1, n1, i1 = norm_forward(x32 + dot(ctx1, w["out"], NN), gains[0], shifts[0])
    h1b = h1.astype(BF16)
    q2 = dot(h1b, w["cq"], NT).astype(BF16)
    ctx2, lse2 = attend(q2, k2, v2, t_ids, s_ids, fq, fs, False)
    r2 = h1 + dot(ctx2, w["cout"], NN)
    acts, slopes, layer_out, dr3, da3, h2b, small3 = ffn(r2, ct, gains, shifts, w["ffn"])
    g_ffn, dr2, da2, small2 = ffn_back(dr3, da3, h2b, r2, gains, acts, slopes, w["ffn"])
    g_ffn = halvings[0](g_ffn)
    g_cout = dot(ctx2, da2, TN).astype(BF16)
    dctx2 = dot(da2, w["cout"], NT).astype(BF16)
    dctx2, g_ffn = lax.optimization_barrier((dctx2, g_ffn))
    g_ffn = halvings[1](g_ffn)
    dq2, dk2, dv2 = attend_back(q2, k2, v2, dctx2, ctx2, lse2, t_ids, s_ids, fq, fs, False)
    dq2, dk2, dv2, g_ffn = lax.optimization_barrier((dq2, dk2, dv2, g_ffn))
    g_ffn = halvings[2](g_ffn)
    g_cq = dot(dq2, h1b, TN).astype(BF16)
    g_ckv = [dot(dk2, e, TN).astype(BF16), dot(dv2, e, TN).astype(BF16)]
    grad_e = (dot(dk2, w["ckv"][0], NN) + dot(dv2, w["ckv"][1], NN)).astype(BF16)
    dh1 = dr2 + dot(dq2, w["cq"], NN)
    dr1, gg1, gs1 = norm_backward(dh1, n1, i1, gains[0])
    da1 = dr1.astype(BF16)
    g_out = dot(ctx1, da1, TN).astype(BF16)
    dctx1 = dot(da1, w["out"], NT).astype(BF16)
    dq, dk, dv = attend_back(q, k, v, dctx1, ctx1, lse1, t_ids, t_ids, fq, fk, True)
    dq, dk, dv, g_ffn = lax.optimization_barrier((dq, dk, dv, g_ffn))
    g_qkv = [dot(d, x, TN).astype(BF16) for d in (dq, dk, dv)]
    grad_x = (dr1 + dot(dq, w["qkv"][0], NN) + dot(dk, w["qkv"][1], NN) + dot(dv, w["qkv"][2], NN)).astype(BF16)
    g_qkv, grad_x, grad_e = lax.optimization_barrier((g_qkv, grad_x, grad_e))
    grads = dict(qkv=g_qkv, out=g_out, cq=g_cq, ckv=g_ckv, cout=g_cout, ffn=g_ffn)
    grad_gains = jnp.concatenate([gg1, small2[0:1], small3[0:1]], axis=0)
    grad_shifts = jnp.concatenate([gs1, small2[1:2], small3[1:2]], axis=0)
    return layer_out, grad_x, grad_e, grads, grad_gains, grad_shifts

MESH = pl.DeviceIdType.MESH

def greet(devices):
    barrier = pltpu.get_barrier_semaphore()
    for device in devices:
        pl.semaphore_signal(barrier, inc=1, device_id=device, device_id_type=MESH)
    pl.semaphore_wait(barrier, len(devices))


def gather_kernel(groups, chunks, window, pack_ref, out_ref, local_sem, send_sem, recv_sem):
    p, t = lax.axis_index("dp"), lax.axis_index("tensor")
    rows = pack_ref.shape[1]
    n = rows // chunks
    zs = [jnp.bitwise_xor(t, j) for j in (1, 2, 3)]
    to_c, to_x, to_y = [(jnp.bitwise_xor(p, b), t) for b in (1, 2, 4)]
    far = jnp.bitwise_xor(p, 6)
    greet([to_c, to_x, to_y] + [(p, z) for z in zs])
    keep = pltpu.make_async_copy(pack_ref, out_ref.at[:, t], local_sem)
    keep.start()
    count = [0]
    copies = []

    def send(src, dst, device):
        i = count[0]
        count[0] += 1
        copy = pltpu.make_async_remote_copy(
            src, dst, send_sem.at[i], recv_sem.at[i], device_id=device, device_id_type=MESH
        )
        copy.start()
        copies.append(copy)
        return copy

    cut = lambda c: pl.ds(c * n, n)
    steps = [(g, c) for g in range(groups) for c in range(chunks)]
    z_in, x_in, y_in, xd_in, yd_in = {}, {}, {}, {}, {}
    last = []

    def start_z(i):
        g, c = steps[i]
        a = g * 8 + p
        for j in range(3):
            z_in[i, j] = send(pack_ref.at[a, cut(c)], out_ref.at[a, t, cut(c)], (p, zs[j]))

    def stage_z(i):
        g, c = steps[i]
        for j in range(3):
            z_in[i, j].wait_recv()
            ref = out_ref.at[g * 8 + p, zs[j], cut(c)]
            x_in[i, j] = send(ref, ref, to_x)
            y_in[i, j] = send(ref, ref, to_y)
            last.append(send(ref, ref, to_c))
        if i + window < len(steps):
            start_z(i + window)

    def stage_xy(i):
        g, c = steps[i]
        for j in range(3):
            x_in[i, j].wait_recv()
            ref = out_ref.at[g * 8 + to_x[0], zs[j]]
            part = ref.at[pl.ds(c * n, n // 2)]
            yd_in[i, j] = send(part, part, to_y)
            part = ref.at[cut(c)]
            last.append(send(part, part, to_c))
            y_in[i, j].wait_recv()
            ref = out_ref.at[g * 8 + to_y[0], zs[j]]
            part = ref.at[pl.ds(c * n + n // 2, n // 2)]
            xd_in[i, j] = send(part, part, to_x)
            part = ref.at[cut(c)]
            last.append(send(part, part, to_c))

    def stage_far(i):
        g, c = steps[i]
        for j in range(3):
            xd_in[i, j].wait_recv()
            yd_in[i, j].wait_recv()
            ref = out_ref.at[g * 8 + far, zs[j], cut(c)]
            last.append(send(ref, ref, to_c))

    for i in range(window):
        start_z(i)
    stages = (stage_z, stage_xy, stage_far)
    for step in range(len(steps) + 2):
        for k in (2, 1, 0):
            if 0 <= step - k < len(steps):
                stages[k](step - k)
    for copy in last:
        copy.wait_recv()
    for copy in copies:
        copy.wait_send()
    keep.wait()


def gather_pack(pack, collective_id, chunks=3, window=1):
    mats, rows, width = pack.shape
    groups = mats // 8
    count = groups * chunks * (3 + 9 + 3 * 2 + 3 * 2 + 3)
    return pl.pallas_call(
        functools.partial(gather_kernel, groups, chunks, window),
        out_shape=jax.ShapeDtypeStruct((mats, 4, rows, width), pack.dtype),
        in_specs=[pl.BlockSpec(memory_space=pltpu.VMEM)],
        out_specs=pl.BlockSpec(memory_space=pl.ANY),
        scratch_shapes=[
            pltpu.SemaphoreType.DMA,
            pltpu.SemaphoreType.DMA((count,)),
            pltpu.SemaphoreType.DMA((count,)),
        ],
        compiler_params=pltpu.CompilerParams(collective_id=collective_id, has_side_effects=True, vmem_limit_bytes=32 * 2**20),
        name="gather_pack",
    )(pack)


def reduce_kernel(chunks, mats, *refs):
    grads, small_ref, ffn_ref = refs[:mats], refs[mats], refs[mats + 1]
    (out_ref, small_out_ref, ffn_out_ref, ffn_z, ffn_piece, mine, from_c, from_x1, from_y1, from_x2, from_y2, from_z, piece,
     s_send, s_c, s_x, s_y, s_z, local_sem, send_sem, recv_sem, small_send, small_recv) = refs[mats + 2 :]
    p, t = lax.axis_index("dp"), lax.axis_index("tensor")
    half = grads[0].shape[1] // 2
    n = half // chunks
    per = mats // 4
    core, cx, cy = lax.rem(p, 2), lax.rem(p // 2, 2), p // 4
    chip = p // 2
    zs = [jnp.bitwise_xor(t, j) for j in (1, 2, 3)]
    to_c, to_x, to_y = [(jnp.bitwise_xor(p, b), t) for b in (1, 2, 4)]
    greet([to_c, to_x, to_y] + [(p, z) for z in zs])
    count = [0]
    copies = []

    def send(src, dst, device):
        i = count[0]
        count[0] += 1
        copy = pltpu.make_async_remote_copy(
            src, dst, send_sem.at[i], recv_sem.at[i], device_id=device, device_id_type=MESH
        )
        copy.start()
        copies.append(copy)
        return copy

    small_count = [0]

    def send_small(src, dst, device):
        i = small_count[0]
        small_count[0] += 1
        copy = pltpu.make_async_remote_copy(
            src, dst, small_send.at[i], small_recv.at[i], device_id=device, device_id_type=MESH
        )
        copy.start()
        return copy

    nx, ny = 1 - cx, 1 - cy
    c_in, x1, y1, x2, y2, z_in, gx, gy, gxd, gyd, last = {}, {}, {}, {}, {}, {}, {}, {}, {}, {}, []
    local = {}
    cut = lambda c: pl.ds(c * n, n)
    own_cut = lambda c: pl.ds(pl.multiple_of(core * half + c * n, 16), n)
    other_cut = lambda c: pl.ds(pl.multiple_of((1 - core) * half + c * n, 16), n)
    owned = lambda q: pl.ds(q * per, per)
    for c in range(chunks):
        c_in[c], local[c] = [], []
        for a in range(mats):
            c_in[c].append(send(grads[a].at[:, other_cut(c)], from_c.at[a, :, cut(c)], to_c))
            copy = pltpu.make_async_copy(
                grads[a].at[:, own_cut(c)], mine.at[a, :, cut(c)], local_sem.at[c * mats + a]
            )
            copy.start()
            local[c].append(copy)
    small = send_small(small_ref, s_c, to_c)
    f_in = [send(ffn_ref.at[:, zs[j]], ffn_z.at[j], (p, zs[j])) for j in range(3)]
    f_way = {}

    def ffn_total():
        for j in range(3):
            f_in[j].wait_recv()
        for i in range(2):
            total = ffn_ref[i, t].astype(F32)
            for j in range(3):
                total = total + ffn_z[j, i].astype(F32)
            ffn_piece[p, i] = total.astype(ffn_piece.dtype)
        ref = ffn_piece.at[p]
        f_way["x"] = send(ref, ref, to_x)
        f_way["y"] = send(ref, ref, to_y)
        last.append(send(ref, ref, to_c))

    def ffn_far():
        f_way["x"].wait_recv()
        ref = ffn_piece.at[to_x[0]]
        f_way["yd"] = send(ref.at[0], ref.at[0], to_y)
        last.append(send(ref, ref, to_c))
        f_way["y"].wait_recv()
        ref = ffn_piece.at[to_y[0]]
        f_way["xd"] = send(ref.at[1], ref.at[1], to_x)
        last.append(send(ref, ref, to_c))

    def ffn_end():
        f_way["xd"].wait_recv()
        f_way["yd"].wait_recv()
        ref = ffn_piece.at[jnp.bitwise_xor(p, 6)]
        last.append(send(ref, ref, to_c))

    def add(dst, src):
        dst[...] = (dst[...].astype(F32) + src[...].astype(F32)).astype(dst.dtype)

    def stage_c(c):
        for a in range(mats):
            c_in[c][a].wait_recv()
            local[c][a].wait()
            for b in range(4):
                add(mine.at[a, b, cut(c)], from_c.at[a, b, cut(c)])
        x1[c] = [send(mine.at[owned(q * 2 + nx), 0:2, cut(c)], from_x1.at[q, :, :, cut(c)], to_x) for q in range(2)]
        y1[c] = [send(mine.at[owned(ny * 2 + q), 2:4, cut(c)], from_y1.at[q, :, :, cut(c)], to_y) for q in range(2)]

    def stage_xy(c):
        for q in range(2):
            x1[c][q].wait_recv()
            for i in range(per):
                for b in range(2):
                    add(mine.at[(q * 2 + cx) * per + i, b, cut(c)], from_x1.at[q, i, b, cut(c)])
        x2[c] = send(mine.at[owned(ny * 2 + cx), 0:2, cut(c)], from_x2.at[:, :, cut(c)], to_y)
        for q in range(2):
            y1[c][q].wait_recv()
            for i in range(per):
                for b in range(2):
                    add(mine.at[(cy * 2 + q) * per + i, 2 + b, cut(c)], from_y1.at[q, i, b, cut(c)])
        y2[c] = send(mine.at[owned(cy * 2 + nx), 2:4, cut(c)], from_y2.at[:, :, cut(c)], to_x)

    def stage_z(c):
        x2[c].wait_recv()
        for i in range(per):
            for b in range(2):
                add(mine.at[chip * per + i, b, cut(c)], from_x2.at[i, b, cut(c)])
        y2[c].wait_recv()
        for i in range(per):
            for b in range(2):
                add(mine.at[chip * per + i, 2 + b, cut(c)], from_y2.at[i, b, cut(c)])
        z_in[c] = [
            send(mine.at[owned(chip), zs[j], cut(c)], from_z.at[j, :, cut(c)], (p, zs[j])) for j in range(3)
        ]

    def stage_out(c):
        for j in range(3):
            z_in[c][j].wait_recv()
        for i in range(per):
            total = mine[chip * per + i, t, cut(c), :].astype(F32)
            for j in range(3):
                total = total + from_z[j, i, cut(c), :].astype(F32)
            piece[chip * per + i, own_cut(c), :] = total.astype(piece.dtype)
        ref = piece.at[owned(chip), own_cut(c)]
        gx[c] = send(ref, ref, to_x)
        gy[c] = send(ref, ref, to_y)
        last.append(send(ref, ref, to_c))

    def stage_far(c):
        gx[c].wait_recv()
        ref = piece.at[owned(cy * 2 + nx), own_cut(c)]
        gyd[c] = send(ref.at[: per // 2], ref.at[: per // 2], to_y)
        last.append(send(ref, ref, to_c))
        gy[c].wait_recv()
        ref = piece.at[owned(ny * 2 + cx), own_cut(c)]
        gxd[c] = send(ref.at[per // 2 :], ref.at[per // 2 :], to_x)
        last.append(send(ref, ref, to_c))

    def stage_end(c):
        gxd[c].wait_recv()
        gyd[c].wait_recv()
        ref = piece.at[owned(ny * 2 + nx), own_cut(c)]
        last.append(send(ref, ref, to_c))

    stages = (stage_c, stage_xy, stage_z, stage_out, stage_far, stage_end)
    for step in range(chunks + len(stages) - 1):
        for k in reversed(range(len(stages))):
            if 0 <= step - k < chunks:
                stages[k](step - k)
        if step == 0:
            small.wait()
            s_send[0] = small_ref[...] + s_c[...]
            small = send_small(s_send.at[0], s_x, to_x)
        elif step == 1:
            small.wait()
            s_send[1] = s_send[0] + s_x[...]
            small = send_small(s_send.at[1], s_y, to_y)
        elif step == 2:
            small.wait()
            s_send[2] = s_send[1] + s_y[...]
            s_z[t] = s_send[2]
            small = [send_small(s_send.at[2], s_z.at[t], (p, z)) for z in zs]
            ffn_total()
        elif step == 4:
            ffn_far()
        elif step == 5:
            ffn_end()
    for copy in small:
        copy.wait()
    small_out_ref[...] = (s_z[0] + s_z[1]) + (s_z[2] + s_z[3])
    for copy in last:
        copy.wait_recv()
    for copy in copies:
        copy.wait_send()
    for a in range(mats):
        out_ref[a] = piece[a].astype(out_ref.dtype)
    part = ffn_piece.shape[2]
    for a in range(8):
        for i in range(2):
            ffn_out_ref[i, pl.ds(a * part, part), :] = ffn_piece[a, i].astype(ffn_out_ref.dtype)


def reduce_pack(grads, small, ffn, collective_id, chunks=2):
    mats = len(grads)
    tensor, rows, width = grads[0].shape
    half, per = rows // 2, mats // 4
    part = ffn.shape[2]
    count = chunks * (mats + 4 + 2 + 3 + 3 + 4 + 1) + 11
    vmem = pl.BlockSpec(memory_space=pltpu.VMEM)
    buf = lambda *s: pltpu.VMEM(s + (half, width), BF16)
    sb = lambda *s: pltpu.VMEM(s + small.shape, F32)
    return pl.pallas_call(
        functools.partial(reduce_kernel, chunks, mats),
        out_shape=(
            jax.ShapeDtypeStruct((mats, rows, width), F32),
            jax.ShapeDtypeStruct(small.shape, F32),
            jax.ShapeDtypeStruct((2, 8 * part, width), F32),
        ),
        in_specs=[pl.BlockSpec(memory_space=pl.ANY)] * mats + [vmem, vmem],
        out_specs=(vmem, vmem, vmem),
        scratch_shapes=[
            pltpu.VMEM((3, 2, part, width), BF16),
            pltpu.VMEM((8, 2, part, width), BF16),
            buf(mats, 4), buf(mats, 4), buf(2, per, 2), buf(2, per, 2), buf(per, 2), buf(per, 2), buf(3, per),
            pltpu.VMEM((mats, rows, width), BF16),
            sb(3), sb(), sb(), sb(), sb(4),
            pltpu.SemaphoreType.DMA((chunks * mats,)),
            pltpu.SemaphoreType.DMA((count,)),
            pltpu.SemaphoreType.DMA((count,)),
            pltpu.SemaphoreType.DMA((6,)),
            pltpu.SemaphoreType.DMA((6,)),
        ],
        compiler_params=pltpu.CompilerParams(
            collective_id=collective_id, has_side_effects=True, vmem_limit_bytes=48 * 2**20
        ),
        cost_estimate=pl.CostEstimate(flops=int(1e9), bytes_accessed=int(60e6), transcendentals=0),
        name="reduce_pack",
    )(*grads, small, ffn)


def flip(x, bit):
    return lax.ppermute(x, "dp", [(i, i ^ bit) for i in range(lax.axis_size("dp"))])


def take(x, i, axis):
    return lax.dynamic_index_in_dim(x, i, axis, keepdims=False)


def halve_core(grad):
    tensor = lax.axis_size("tensor")
    core = lax.axis_index("dp") % 2
    grad = grad.reshape(2, 2, 2, 2, tensor, grad.shape[1] // (8 * tensor), grad.shape[2])
    return take(grad, core, 3) + flip(take(grad, 1 - core, 3), 1)


def halve_plane(grad):
    p = lax.axis_index("dp")
    cx, cy = p // 2 % 2, p // 4
    cut = grad.shape[3] // 2
    left, right = grad[:, :, :, :cut], grad[:, :, :, cut:]
    left_in, right_in = flip(take(left, 1 - cx, 2), 2), flip(take(right, 1 - cy, 1), 4)
    return take(left, cx, 2) + left_in, take(right, cy, 1) + right_in


def halve_rest(halves):
    left, right = halves
    p = lax.axis_index("dp")
    cx, cy = p // 2 % 2, p // 4
    left_in, right_in = flip(take(left, 1 - cy, 1), 4), flip(take(right, 1 - cx, 1), 2)
    return jnp.concatenate([take(left, cy, 1) + left_in, take(right, cx, 1) + right_in], axis=1)


def gather_rows(shard):
    mats, rows, width = shard.shape
    dp, tensor = lax.axis_size("dp"), lax.axis_size("tensor")
    if own_kernels():
        return gather_pack(shard, 0).reshape(mats, tensor * rows, width)
    piece = mats * rows // dp
    mine = lax.dynamic_slice_in_dim(
        shard.reshape(mats * rows, width), lax.axis_index("dp") * piece, piece, 0
    )
    full = lax.all_gather(mine, ("dp", "tensor"), axis=0, tiled=True)
    full = full.reshape(mats, dp // mats, tensor, piece, width).transpose(0, 2, 1, 3, 4)
    return full.reshape(mats, tensor * rows, width)


def own_kernels():
    return (lax.axis_size("dp"), lax.axis_size("tensor")) == (8, 4)


def reduce_rows(grads, small, ffn):
    mats = len(grads)
    all_rows, width = grads[0].shape
    dp, tensor = lax.axis_size("dp"), lax.axis_size("tensor")
    rows = all_rows // tensor
    if own_kernels():
        return reduce_pack([g.reshape(tensor, rows, width) for g in grads], small, ffn, 1)
    piece = mats * rows // dp
    grad = jnp.stack(grads).reshape(mats, tensor, dp // mats, piece, width).transpose(0, 2, 1, 3, 4)
    mine = lax.psum_scatter(
        grad.reshape(dp * tensor * piece, width), ("dp", "tensor"), scatter_dimension=0, tiled=True
    )
    total = lax.all_gather(mine, "dp", axis=0, tiled=True).reshape(mats, rows, width).astype(F32)
    ffn = lax.psum_scatter(ffn, ("dp", "tensor"), scatter_dimension=1, tiled=True)
    ffn = lax.all_gather(ffn, "dp", axis=1, tiled=True).astype(F32)
    return total, lax.psum(small, ("dp", "tensor")), ffn


def per_device(
    inputs, encoded, cotangent, tgt_seg, src_seg, self_qkv, self_out, cross_q, cross_kv, cross_out, ffn_up, ffn_down, gains, shifts
):
    me = lax.axis_index("tensor")
    t_ids = lax.dynamic_index_in_dim(tgt_seg, me, 0, keepdims=False)
    s_ids = lax.dynamic_index_in_dim(src_seg, me, 0, keepdims=False)
    pack = jnp.concatenate(
        [
            self_qkv.transpose(0, 2, 1),
            self_out[None],
            cross_q.T[None],
            cross_kv.transpose(0, 2, 1),
            cross_out[None],
        ],
        axis=0,
    )
    pack = gather_rows(pack)
    hidden = ffn_down.shape[0]
    width = inputs.shape[1]
    dp, tensor = lax.axis_size("dp"), lax.axis_size("tensor")
    piece = hidden // dp
    start = lax.axis_index("dp") * piece
    ffn_w = jnp.stack([ffn_up.T, ffn_down], axis=0)
    ffn_w = lax.dynamic_slice_in_dim(ffn_w, start, piece, 1)
    ffn_w = lax.all_gather(ffn_w, ("dp", "tensor"), axis=1, tiled=True)
    w = dict(qkv=pack[0:3], out=pack[3], cq=pack[4], ckv=pack[5:7], cout=pack[7], ffn=ffn_w)
    halvings = (halve_core, halve_plane, halve_rest) if own_kernels() else (lambda g: g,) * 3
    layer_out, grad_x, grad_e, grads, grad_gains, grad_shifts = local_step(
        inputs, encoded, cotangent, t_ids, s_ids, w, gains, shifts, halvings
    )
    small = jnp.concatenate([grad_gains, grad_shifts, jnp.zeros((2, width), F32)], axis=0)
    total, small, g_ffn = reduce_rows(
        [*grads["qkv"], grads["out"], grads["cq"], *grads["ckv"], grads["cout"]], small, grads["ffn"]
    )
    return (
        layer_out,
        grad_x,
        grad_e,
        total[0:3].transpose(0, 2, 1),
        total[3],
        total[4].T,
        total[5:7].transpose(0, 2, 1),
        total[7],
        g_ffn[0].T,
        g_ffn[1],
        small[0:3],
        small[3:6],
    )


def solution(mesh):
    rows = P(("dp", "tensor"), None)
    in_specs = (
        rows, rows, rows, P("dp", None), P("dp", None),
        P(None, None, "tensor"), P("tensor", None), P(None, "tensor"), P(None, None, "tensor"), P("tensor", None),
        P(None, "tensor"), P("tensor", None), P(), P(),
    )
    out_specs = (
        rows, rows, rows,
        P(None, None, "tensor"), P("tensor", None), P(None, "tensor"), P(None, None, "tensor"), P("tensor", None),
        P(None, "tensor"), P("tensor", None), P(), P(),
    )
    return jax.shard_map(per_device, mesh=mesh, in_specs=in_specs, out_specs=out_specs, check_vma=False)
```
